256 devices in a mesh: az: 32 (over z_lo, x, core), rad: 8 (over z_hi, y).
Axes of the slice: x: 4, y: 4, z: 8 (z_hi: 2, z_lo: 4; z = z_hi * 4 + z_lo), core: 2. Of those that a mesh axis runs over, the one named last changes fastest.
Arguments:
- conserved: float32 [8, 16, 64, 4096], P(None, None, 'rad', 'az'), as said below
- shear_shift: int32 [2], replicated, may hold values from 0 to 4095
Outputs:
- tendency: float32 [8, 16, 64, 4096], P(None, None, 'rad', 'az')
The draws below stay inside these ranges and needn't reach their ends.
Inputs may be any that keep to these rules, and one draw needn't show every extreme that they name: `conserved`: every cell has positive density and positive pressure.
All inputs are finite; a program needn't handle non-finite values.
Results may differ from the reference program's by a relative error of at most 0.0003.
Values sent between devices are 32-bit elements; how exact they have to be, the bound alone decides.
A program may use at most 64 MiB of HBM per device.

```python
import math
import jax
import jax.numpy as jnp
from jax import lax

CY = 128
NZ = 16
NX = 64
NY = 4096
N_AZ = 32


adiabatic = 5.0 / 3.0


def draw_conserved(key, part):
    key = jax.random.fold_in(key, 11)
    keys = jax.random.split(key, 4)
    grid = (NZ, NX, NY)
    density = jnp.exp(jax.random.uniform(keys[0], grid, jnp.float32, math.log(0.5), math.log(2.0)))
    velocity = 0.3 * jnp.clip(jax.random.normal(keys[1], (3,) + grid, jnp.float32), -2.5, 2.5)
    pressure = jnp.exp(jax.random.uniform(keys[2], grid, jnp.float32, math.log(0.5), math.log(2.0)))
    magnetic = 0.3 * jnp.clip(jax.random.normal(keys[3], (3,) + grid, jnp.float32), -2.5, 2.5)
    energy = pressure / (adiabatic - 1.0) + 0.5 * density * jnp.sum(velocity * velocity, axis=0) + 0.5 * jnp.sum(magnetic * magnetic, axis=0)
    return jnp.concatenate([density[None], density * velocity, energy[None], magnetic], axis=0).astype(jnp.float32)


def setup_inputs(seed: int = 0) -> dict:
    streams_of = jax.random.split(jax.random.key(seed), 3)
    return {
        "conserved": draw_conserved(jax.random.fold_in(streams_of[2], 71), 0),
        "shear_shift": jax.random.randint(streams_of[1], (2,), 0, NY).astype(jnp.int32),
    }


adiabatic = 5.0 / 3.0
time_step = 0.02
shear_jump = 0.5

def primitive_of(conserved):
    density = conserved[0]
    velocity = conserved[1:4] / density
    magnetic = conserved[5:8]
    pressure = (adiabatic - 1.0) * (conserved[4] - 0.5 * density * lax.optimization_barrier(jnp.sum(velocity * velocity, axis=0)) - 0.5 * lax.optimization_barrier(jnp.sum(magnetic * magnetic, axis=0)))
    return jnp.concatenate([density[None], velocity, pressure[None], magnetic], axis=0)

def flux_of(primitive, normal):
    density = primitive[0]
    velocity = primitive[1:4]
    pressure = primitive[4]
    magnetic = primitive[5:8]
    normal_vel = velocity[normal]
    normal_mag = magnetic[normal]
    mag_square = lax.optimization_barrier(jnp.sum(magnetic * magnetic, axis=0))
    total_pres = pressure + 0.5 * mag_square
    energy = pressure / (adiabatic - 1.0) + 0.5 * density * lax.optimization_barrier(jnp.sum(velocity * velocity, axis=0)) + 0.5 * mag_square
    conserved = jnp.concatenate([density[None], density * velocity, energy[None], magnetic], axis=0)
    selector = (jnp.arange(3) == normal).astype(primitive.dtype).reshape((3,) + (1,) * (primitive.ndim - 1))
    momentum = density * velocity * normal_vel - magnetic * normal_mag + selector * total_pres
    induction = magnetic * normal_vel - velocity * normal_mag
    power = (energy + total_pres) * normal_vel - normal_mag * lax.optimization_barrier(jnp.sum(velocity * magnetic, axis=0))
    face_flux = jnp.concatenate([(density * normal_vel)[None], momentum, power[None], induction], axis=0)
    signal_speed = jnp.abs(normal_vel) + jnp.sqrt((adiabatic * pressure + mag_square) / density)
    return (conserved, face_flux, signal_speed)

def face_difference(padded, along, normal):
    length = padded.shape[along]
    cells = length - 4
    centre = lax.slice_in_dim(padded, 1, length - 1, axis=along)
    back_diff = centre - lax.slice_in_dim(padded, 0, length - 2, axis=along)
    fore_diff = lax.slice_in_dim(padded, 2, length, axis=along) - centre
    slopes = 0.5 * (jnp.sign(back_diff) + jnp.sign(fore_diff)) * jnp.minimum(jnp.abs(back_diff), jnp.abs(fore_diff))
    left_state = lax.slice_in_dim(centre + 0.5 * slopes, 0, cells + 1, axis=along)
    right_state = lax.slice_in_dim(centre - 0.5 * slopes, 1, cells + 2, axis=along)
    left_cons, left_flux, left_speed = flux_of(left_state, normal)
    right_cons, right_flux, right_speed = flux_of(right_state, normal)
    face_flux = 0.5 * (left_flux + right_flux) - 0.5 * jnp.maximum(left_speed, right_speed) * (right_cons - left_cons)
    return lax.slice_in_dim(face_flux, 1, cells + 1, axis=along) - lax.slice_in_dim(face_flux, 0, cells, axis=along)

def tendency_of(x_padded, y_padded):
    core = x_padded[:, :, 2:-2, :]
    z_padded = jnp.concatenate([core[:, -2:], core, core[:, :2]], axis=1)
    return -(face_difference(x_padded, 2, 0) + face_difference(y_padded, 3, 1) + face_difference(z_padded, 1, 2))

def reference(conserved, shear_shift):

    def section(primitive, offset):
        kick = shear_jump * (jnp.arange(8) == 2).astype(primitive.dtype)[:, None, None, None]
        inner_rows = jnp.roll(primitive[:, :, NX - 2:, :], -offset, axis=3) + kick
        outer_rows = jnp.roll(primitive[:, :, :2, :], offset, axis=3) - kick
        x_padded = jnp.concatenate([inner_rows, primitive, outer_rows], axis=2)
        y_padded = jnp.concatenate([primitive[..., -2:], primitive, primitive[..., :2]], axis=3)

        def block(block_index):
            begin_col = block_index * CY
            return tendency_of(lax.dynamic_slice_in_dim(x_padded, begin_col, CY, axis=3), lax.dynamic_slice_in_dim(y_padded, begin_col, CY + 4, axis=3))
        blocks = lax.map(block, jnp.arange(N_AZ, dtype=jnp.int32))
        return jnp.moveaxis(blocks, 0, 3).reshape(8, NZ, NX, N_AZ * CY)
    first = section(primitive_of(conserved), shear_shift[0])
    midpoint = conserved + time_step * first
    second = section(primitive_of(midpoint), shear_shift[1])
    return 0.5 * (first + second)
```

```python
import functools

import jax
import jax.numpy as jnp
from jax import lax
from jax.experimental import pallas as pl
from jax.experimental.pallas import tpu as pltpu
from jax.sharding import PartitionSpec as P

MESH = pl.DeviceIdType.MESH
time_step = 0.02
shear_jump = 0.5
AZ, RAD = 32, 8
NF, NX, NZ, NY = 8, 8, 16, 128
COLS = AZ * NY


def primitive_of(u):
    inv = 1.0 / u[0]
    v = [u[i] * inv for i in (1, 2, 3)]
    vv = v[0] * v[0] + v[1] * v[1] + v[2] * v[2]
    bb = u[5] * u[5] + u[6] * u[6] + u[7] * u[7]
    p = (2.0 / 3.0) * (u[4] - 0.5 * u[0] * vv - 0.5 * bb)
    return [u[0], v[0], v[1], v[2], p, u[5], u[6], u[7]]


def half_slope(a, b):
    return 0.5 * jnp.maximum(jnp.minimum(a, b), jnp.minimum(jnp.maximum(a, b), 0.0))


def state_of(w, n):
    rho, v, p, b = w[0], w[1:4], w[4], w[5:8]
    vn, bn = v[n], b[n]
    bb = b[0] * b[0] + b[1] * b[1] + b[2] * b[2]
    hb = 0.5 * bb
    vv = v[0] * v[0] + v[1] * v[1] + v[2] * v[2]
    vb = v[0] * b[0] + v[1] * b[1] + v[2] * b[2]
    pt = p + hb
    mom = [rho * c for c in v]
    en = 1.5 * p + 0.5 * rho * vv + hb
    fm = [mom[i] * vn - b[i] * bn for i in range(3)]
    fm[n] = fm[n] + pt
    fe = (en + pt) * vn - bn * vb
    fb = [None if i == n else b[i] * vn - v[i] * bn for i in range(3)]
    a = (5.0 / 3.0) * p + bb
    speed = jnp.abs(vn) + (a * lax.rsqrt(a)) * lax.rsqrt(rho)
    return [rho] + mom + [en] + list(b), [mom[n]] + fm + [fe] + fb, speed


def twice_flux(left, right, n):
    ul, fl, cl = state_of(left, n)
    ur, fr, cr = state_of(right, n)
    c = jnp.maximum(cl, cr)
    out = []
    for i in range(NF):
        diff = c * (ur[i] - ul[i])
        out.append(-diff if fl[i] is None else fl[i] + fr[i] - diff)
    return out


def rolled_faces(w, axis, n):
    size = w[0].shape[axis]
    left, right = [], []
    for f in range(NF):
        d = w[f] - pltpu.roll(w[f], 1, axis)
        h = half_slope(d, pltpu.roll(d, size - 1, axis))
        left.append(pltpu.roll(w[f] + h, 1, axis))
        right.append(w[f] - h)
    return twice_flux(left, right, n)


def kernel(shift_ref, u_hbm, out_ref, raw, w1, w2, acc, fx, tend, corr, strips, y_lo, y_hi, ghost, relay_in, relay_roll,
           relay_out, in_sem, x_send, x_recv, y_send, y_recv, a_send, a_recv, b_send):
    az = lax.axis_index("az")
    rad = lax.axis_index("rad")
    right, left = (az + 1) % AZ, (az + AZ - 1) % AZ
    edge = (rad == 0) | (rad == RAD - 1)
    relay_lo = rad == 4 + az % 3
    relay_hi = rad == 3 - az % 3
    relay = relay_lo | relay_hi
    kick = [jnp.where(rad == 0, shear_jump, 0.0), jnp.where(rad == RAD - 1, -shear_jump, 0.0)]

    load = pltpu.make_async_copy(u_hbm, raw, in_sem)
    load.start()

    barrier = pltpu.get_barrier_semaphore()

    def signal(*device):
        pl.semaphore_signal(barrier, 1, device_id=device, device_id_type=MESH)

    signal(right, rad)
    signal(left, rad)

    @pl.when(edge)
    def _():
        def step(k, carry):
            p = (k + az) % AZ
            signal(p, 4 + p % 3)
            signal(p, 3 - p % 3)
            return carry
        lax.fori_loop(0, AZ, step, 0)

    @pl.when(relay)
    def _():
        def step(k, carry):
            p = (k + az) % AZ
            signal(p, 0)
            signal(p, RAD - 1)
            return carry
        lax.fori_loop(0, AZ, step, 0)

    @pl.when(rad > 0)
    def _():
        signal(az, rad - 1)

    @pl.when(rad < RAD - 1)
    def _():
        signal(az, rad + 1)

    lane = lax.broadcasted_iota(jnp.int32, (NZ, NY), 1)
    slot = lane % 16
    block = lane // 16
    inner = (lane > 1) & (lane < NY - 1)
    seam = (lane < 2) | (lane >= NY - 2)

    load.wait()
    u_rows = raw.reshape(NF * NZ * NX, NY)

    def conserved_row(x):
        return [u_rows[pl.ds(f * NZ * NX + x, NZ, NX), :] for f in range(NF)]

    def first_rows(x, carry):
        w = primitive_of(conserved_row(x))
        for f in range(NF):
            w1[f, x + 2] = w[f]
        return carry

    lax.fori_loop(0, NX, first_rows, 0)

    pl.semaphore_wait(barrier, jnp.where(edge, 2 * AZ + 3, jnp.where(relay, 2 * AZ + 4, 4)))

    def x_copy(sec, w, up):
        rows = w.at[:, pl.ds(8 if up else 2, 2)]
        side = 0 if up else 1
        return pltpu.make_async_remote_copy(
            rows, ghost.at[sec, side], x_send.at[sec, side], x_recv.at[sec, side],
            device_id=(az, rad + 1 if up else rad - 1), device_id_type=MESH)

    def y_copy(sec, up):
        return pltpu.make_async_remote_copy(
            strips.at[sec], (y_lo if up else y_hi).at[sec], y_send.at[sec, 0 if up else 1],
            y_recv.at[sec, 0 if up else 1],
            device_id=(right if up else left, rad), device_id_type=MESH)

    def start_x(sec, w):
        @pl.when(edge)
        def _():
            base = jnp.where(rad == 0, 2, 8)

            def step(k, carry):
                p = (k + az) % AZ
                f, j, half = p // 4, (p // 2) % 2, p % 2
                pltpu.make_async_remote_copy(
                    w.at[f, base + j, pl.ds(pl.multiple_of(half * 8, 8), 8)], relay_in.at[sec, az],
                    a_send.at[sec], a_recv.at[sec],
                    device_id=(p, jnp.where(rad == 0, 3 - p % 3, 4 + p % 3)), device_id_type=MESH).start()
                return carry

            lax.fori_loop(0, AZ, step, 0)

        @pl.when(rad < RAD - 1)
        def _():
            x_copy(sec, w, True).start()

        @pl.when(rad > 0)
        def _():
            x_copy(sec, w, False).start()

    def start_y(sec, w):
        for f in range(NF):
            q = w[f, 2]
            q = pltpu.roll(q, 8, 1)
            for x in range(1, NX):
                q = jnp.where(block == x, pltpu.roll(w[f, x + 2], (16 * x + 8) % NY, 1), q)
            strips[sec, f] = q
        y_copy(sec, True).start()
        y_copy(sec, False).start()

    def serve(sec):
        @pl.when(relay)
        def _():
            offset = shift_ref[sec]
            amount = jnp.where(relay_lo, offset, (COLS - offset) % COLS)
            whole, part = amount // NY, amount % NY
            pltpu.make_async_copy(relay_in.at[sec], relay_in.at[sec], a_recv.at[sec]).wait()

            def turn(k, carry):
                relay_roll[k] = pltpu.roll(relay_in[sec, k], (NY - part) % NY, 1)
                return carry

            lax.fori_loop(0, AZ, turn, 0, unroll=4)
            keep = lax.broadcasted_iota(jnp.int32, (8, NY), 1) < NY - part
            f, j, half = az // 4, (az // 2) % 2, az % 2
            side = jnp.where(relay_lo, 0, 1)
            target = jnp.where(relay_lo, 0, RAD - 1)

            def step(k, carry):
                d = (k + az) % AZ
                relay_out[sec, d] = jnp.where(
                    keep, relay_roll[(d + whole) % AZ], relay_roll[(d + whole + 1) % AZ])
                pltpu.make_async_remote_copy(
                    relay_out.at[sec, d],
                    ghost.at[sec, side, f, j, pl.ds(pl.multiple_of(half * 8, 8), 8)],
                    b_send.at[sec], x_recv.at[sec, side],
                    device_id=(d, target), device_id_type=MESH).start()
                return carry

            lax.fori_loop(0, AZ, step, 0)

    def inside(w):
        def row(x, carry):
            cells = [w[f, x + 2] for f in range(NF)]
            flux = rolled_faces(cells, 0, 2)
            for f in range(NF):
                acc[f, x] = pltpu.roll(flux[f], NZ - 1, 0) - flux[f]
            flux = rolled_faces(cells, 1, 1)
            for f in range(NF):
                masked = jnp.where(inner, flux[f], 0.0)
                acc[f, x] += pltpu.roll(masked, NY - 1, 1) - masked
            return carry

        lax.fori_loop(0, NX, row, 0)

    def x_faces(w, begin, end):
        def face(i, carry):
            lefts, rights = [], []
            for f in range(NF):
                c = [w[f, i + k] for k in range(4)]
                d = [c[k + 1] - c[k] for k in range(3)]
                lefts.append(c[1] + half_slope(d[0], d[1]))
                rights.append(c[2] - half_slope(d[1], d[2]))
            flux = twice_flux(lefts, rights, 0)
            for f in range(NF):
                fx[f, i] = flux[f]
            return carry

        lax.fori_loop(begin, end, face, 0)

    def finish_y(sec):
        y_copy(sec, True).wait_recv()
        y_copy(sec, False).wait_recv()
        cells = []
        for f in range(NF):
            own = strips[sec, f]
            lower = jnp.where((slot >= 4) & (slot < 8), y_lo[sec, f], own)
            upper = jnp.where((slot >= 8) & (slot < 12), y_hi[sec, f], own)
            cells.append(jnp.where(slot < 8, pltpu.roll(lower, NY - 4, 1), pltpu.roll(upper, 4, 1)))
        flux = rolled_faces(cells, 1, 1)
        for f in range(NF):
            masked = jnp.where((slot == 4) | (slot == 5) | (slot == 11) | (slot == 12), flux[f], 0.0)
            d = pltpu.roll(masked, NY - 1, 1) - masked
            far = pltpu.roll(d, NY - 8, 1)
            corr[f] = jnp.where((slot == 4) | (slot == 5), d, jnp.where((slot == 2) | (slot == 3), far, 0.0))
        for f in range(NF):
            value = corr[f]
            for x in range(NX):
                acc[f, x] += jnp.where(seam, pltpu.roll(value, (124 - 16 * x) % NY, 1), 0.0)

    def receive_x(sec, w):
        for side in range(2):
            pltpu.make_async_copy(ghost.at[sec, side], ghost.at[sec, side], x_recv.at[sec, side]).wait()
            for f in range(NF):
                for j in range(2):
                    value = ghost[sec, side, f, j]
                    if f == 2:
                        value = value + kick[side]
                    w[f, j + (10 if side else 0)] = value

    def row_total(x):
        return [-0.5 * (acc[f, x] + (fx[f, x + 1] - fx[f, x])) for f in range(NF)]

    def middle(x, carry):
        total = row_total(x)
        u = conserved_row(x)
        w = primitive_of([u[f] + time_step * total[f] for f in range(NF)])
        for f in range(NF):
            tend[f, x] = total[f]
            w2[f, x + 2] = w[f]
        return carry

    out_rows = out_ref.reshape(NF * NZ * NX, NY)

    def last(x, carry):
        total = row_total(x)
        for f in range(NF):
            out_rows[pl.ds(f * NZ * NX + x, NZ, NX), :] = 0.5 * (tend[f, x] + total[f])
        return carry

    for sec, w, end in ((0, w1, middle), (1, w2, last)):
        start_x(sec, w)
        start_y(sec, w)
        inside(w)
        x_faces(w, 2, 7)
        serve(sec)
        finish_y(sec)
        lax.fori_loop(2, 6, end, 0)
        receive_x(sec, w)
        x_faces(w, 0, 2)
        x_faces(w, 7, 9)
        lax.fori_loop(0, 2, end, 0)
        lax.fori_loop(6, 8, end, 0)

    for sec, w in ((0, w1), (1, w2)):
        y_copy(sec, True).wait_send()
        y_copy(sec, False).wait_send()

        @pl.when(rad < RAD - 1)
        def _():
            x_copy(sec, w, True).wait_send()

        @pl.when(rad > 0)
        def _():
            x_copy(sec, w, False).wait_send()

        @pl.when(edge)
        def _():
            pltpu.make_async_copy(relay_in.at[sec], relay_in.at[sec], a_send.at[sec]).wait()

        @pl.when(relay)
        def _():
            pltpu.make_async_copy(relay_out.at[sec], relay_out.at[sec], b_send.at[sec]).wait()


def shards(conserved, shear_shift):
    f32 = jnp.float32
    return pl.pallas_call(
        kernel,
        out_shape=jax.ShapeDtypeStruct((NF, NZ, NX, NY), f32),
        in_specs=[pl.BlockSpec(memory_space=pltpu.SMEM), pl.BlockSpec(memory_space=pl.ANY)],
        out_specs=pl.BlockSpec(memory_space=pltpu.VMEM),
        scratch_shapes=[
            pltpu.VMEM((NF, NZ, NX, NY), f32),
            pltpu.VMEM((NF, NX + 4, NZ, NY), f32),
            pltpu.VMEM((NF, NX + 4, NZ, NY), f32),
            pltpu.VMEM((NF, NX, NZ, NY), f32),
            pltpu.VMEM((NF, NX + 1, NZ, NY), f32),
            pltpu.VMEM((NF, NX, NZ, NY), f32),
            pltpu.VMEM((NF, NZ, NY), f32),
            pltpu.VMEM((2, NF, NZ, NY), f32),
            pltpu.VMEM((2, NF, NZ, NY), f32),
            pltpu.VMEM((2, NF, NZ, NY), f32),
            pltpu.VMEM((2, 2, NF, 2, NZ, NY), f32),
            pltpu.VMEM((2, AZ, 8, NY), f32),
            pltpu.VMEM((AZ, 8, NY), f32),
            pltpu.VMEM((2, AZ, 8, NY), f32),
            pltpu.SemaphoreType.DMA,
            pltpu.SemaphoreType.DMA((2, 2)),
            pltpu.SemaphoreType.DMA((2, 2)),
            pltpu.SemaphoreType.DMA((2, 2)),
            pltpu.SemaphoreType.DMA((2, 2)),
            pltpu.SemaphoreType.DMA((2,)),
            pltpu.SemaphoreType.DMA((2,)),
            pltpu.SemaphoreType.DMA((2,)),
        ],
        name="mhd_step",
        compiler_params=pltpu.CompilerParams(
            collective_id=0, has_side_effects=True, vmem_limit_bytes=32 * 1024 * 1024),
    )(shear_shift, conserved)


def solution(mesh):
    return jax.shard_map(
        shards,
        mesh=mesh,
        in_specs=(P(None, None, "rad", "az"), P()),
        out_specs=P(None, None, "rad", "az"),
        check_vma=False,
    )
```

```python
import functools

import jax
import jax.numpy as jnp
from jax import lax
from jax.experimental import pallas as pl
from jax.experimental.pallas import tpu as pltpu
from jax.sharding import PartitionSpec as P

MESH = pl.DeviceIdType.MESH
time_step = 0.02
shear_jump = 0.5
AZ, RAD = 32, 8
NF, NX, NZ, NY = 8, 8, 16, 128
COLS = AZ * NY


def primitive_of(u):
    inv = 1.0 / u[0]
    v = [u[i] * inv for i in (1, 2, 3)]
    vv = v[0] * v[0] + v[1] * v[1] + v[2] * v[2]
    bb = u[5] * u[5] + u[6] * u[6] + u[7] * u[7]
    p = (2.0 / 3.0) * (u[4] - 0.5 * u[0] * vv - 0.5 * bb)
    return [u[0], v[0], v[1], v[2], p, u[5], u[6], u[7]]


def conserved_of(w):
    rho, v, p, b = w[0], w[1:4], w[4], w[5:8]
    vv = v[0] * v[0] + v[1] * v[1] + v[2] * v[2]
    bb = b[0] * b[0] + b[1] * b[1] + b[2] * b[2]
    return [rho] + [rho * c for c in v] + [1.5 * p + 0.5 * rho * vv + 0.5 * bb] + list(b)


def half_slope(a, b):
    return 0.5 * jnp.maximum(jnp.minimum(a, b), jnp.minimum(jnp.maximum(a, b), 0.0))


def state_of(w, n):
    rho, v, p, b = w[0], w[1:4], w[4], w[5:8]
    vn, bn = v[n], b[n]
    bb = b[0] * b[0] + b[1] * b[1] + b[2] * b[2]
    hb = 0.5 * bb
    vv = v[0] * v[0] + v[1] * v[1] + v[2] * v[2]
    vb = v[0] * b[0] + v[1] * b[1] + v[2] * b[2]
    pt = p + hb
    mom = [rho * c for c in v]
    en = 1.5 * p + 0.5 * rho * vv + hb
    fm = [mom[i] * vn - b[i] * bn for i in range(3)]
    fm[n] = fm[n] + pt
    fe = (en + pt) * vn - bn * vb
    fb = [None if i == n else b[i] * vn - v[i] * bn for i in range(3)]
    a = (5.0 / 3.0) * p + bb
    speed = jnp.abs(vn) + (a * lax.rsqrt(a)) * lax.rsqrt(rho)
    return [rho] + mom + [en] + list(b), [mom[n]] + fm + [fe] + fb, speed


def twice_flux(left, right, n):
    ul, fl, cl = state_of(left, n)
    ur, fr, cr = state_of(right, n)
    c = jnp.maximum(cl, cr)
    out = []
    for i in range(NF):
        diff = c * (ur[i] - ul[i])
        out.append(-diff if fl[i] is None else fl[i] + fr[i] - diff)
    return out


def rolled_faces(w, axis, n):
    size = w[0].shape[axis]
    left, right = [], []
    for f in range(NF):
        d = w[f] - pltpu.roll(w[f], 1, axis)
        h = half_slope(d, pltpu.roll(d, size - 1, axis))
        left.append(pltpu.roll(w[f] + h, 1, axis))
        right.append(w[f] - h)
    return twice_flux(left, right, n)


def ghosted_divergence(w, g, lane, n):
    size = w[0].shape[1]
    first, final = lane == 0, lane == size - 1
    left, right, left_g, right_g = [], [], [], []
    for f in range(NF):
        w_up, g_up = pltpu.roll(w[f], 1, 1), pltpu.roll(g[f], 1, 1)
        d = w[f] - jnp.where(first, g_up, w_up)
        d_g = g[f] - jnp.where(first, w_up, g_up)
        d_down, d_g_down = pltpu.roll(d, size - 1, 1), pltpu.roll(d_g, size - 1, 1)
        h = half_slope(d, jnp.where(final, d_g_down, d_down))
        h_g = half_slope(d_g, jnp.where(final, d_down, d_g_down))
        l_up = pltpu.roll(w[f] + h, 1, 1)
        left.append(jnp.where(first, pltpu.roll(g[f] + h_g, 1, 1), l_up))
        right.append(w[f] - h)
        left_g.append(l_up)
        right_g.append(g[f] - h_g)
    flux = twice_flux(left, right, n)
    flux_g = twice_flux(left_g, right_g, n)
    return [jnp.where(final, pltpu.roll(flux_g[f], size - 1, 1), pltpu.roll(flux[f], size - 1, 1)) - flux[f]
            for f in range(NF)]


def kernel(shift_hbm, u_hbm, out_ref, raw, w1, w2, acc, fx, tend, corr, strips, y_lo, y_hi, ghost, stage, relay_in,
           relay_roll, near_out, far_out, plane_out, far_in, plane_in, ext_rows, ext_flux, shift_ref, in_sem, shift_sem,
           x_send, x_recv, y_send, y_recv, a_send, a_recv, b_send, far_send, far_recv, plane_send, plane_recv):
    az = lax.axis_index("az")
    rad = lax.axis_index("rad")
    right, left = (az + 1) % AZ, (az + AZ - 1) % AZ
    edge = (rad == 0) | (rad == RAD - 1)
    relay_lo = rad == 4 + az % 3
    relay_hi = rad == 3 - az % 3
    relay = relay_lo | relay_hi
    kick = [jnp.where(rad == 0, shear_jump, 0.0), jnp.where(rad == RAD - 1, -shear_jump, 0.0)]

    barrier = pltpu.get_barrier_semaphore()

    def signal(*device):
        pl.semaphore_signal(barrier, 1, device_id=device, device_id_type=MESH)

    load = pltpu.make_async_copy(u_hbm, raw, in_sem)
    load.start()
    load_shift = pltpu.make_async_copy(shift_hbm, shift_ref, shift_sem)
    load_shift.start()

    @pl.when(relay)
    def _():
        source = jnp.where(relay_lo, RAD - 1, 0)

        def step(k, carry):
            signal((k + az) % AZ, source)
            return carry
        lax.fori_loop(0, AZ, step, 0)

    signal(right, rad)
    signal(left, rad)

    @pl.when(rad > 0)
    def _():
        signal(az, rad - 1)

    @pl.when(rad < RAD - 1)
    def _():
        signal(az, rad + 1)

    @pl.when(edge)
    def _():
        def step(k, carry):
            p = (k + az) % AZ
            signal(p, 4 + p % 3)
            signal(p, 3 - p % 3)
            return carry
        lax.fori_loop(0, AZ, step, 0)

    lane = lax.broadcasted_iota(jnp.int32, (NZ, NY), 1)
    slot = lane % 16
    block = lane // 16
    inner = (lane > 1) & (lane < NY - 1)
    seam = (lane < 2) | (lane >= NY - 2)

    load.wait()
    u_rows = raw.reshape(NF * NZ * NX, NY)

    def conserved_row(x):
        return [u_rows[pl.ds(f * NZ * NX + x, NZ, NX), :] for f in range(NF)]

    def first_rows(x, carry):
        w = primitive_of(conserved_row(x))
        for f in range(NF):
            w1[f, x + 2] = w[f]
        return carry

    lax.fori_loop(0, NX, first_rows, 0)

    @pl.when(edge)
    def _():
        near, far = jnp.where(rad == 0, 2, 8), jnp.where(rad == 0, 4, 6)
        for f in range(NF):
            for j in range(2):
                for t, base in ((0, near), (1, far)):
                    row = w1[f, base + j]
                    for half in range(2):
                        stage[f * 4 + j * 2 + half, t] = row[half * 8:half * 8 + 8]

    pl.semaphore_wait(barrier, jnp.where(edge, AZ + 3, jnp.where(relay, 2 * AZ + 4, 4)))

    def x_copy(sec, w, up):
        rows = w.at[:, pl.ds(8 if up else 2, 2)]
        side = 0 if up else 1
        return pltpu.make_async_remote_copy(
            rows, ghost.at[sec, side], x_send.at[sec, side], x_recv.at[sec, side],
            device_id=(az, rad + 1 if up else rad - 1), device_id_type=MESH)

    def y_copy(sec, up):
        return pltpu.make_async_remote_copy(
            strips.at[sec], (y_lo if up else y_hi).at[sec], y_send.at[sec, 0 if up else 1],
            y_recv.at[sec, 0 if up else 1],
            device_id=(right if up else left, rad), device_id_type=MESH)

    def scatter():
        @pl.when(edge)
        def _():
            def step(k, carry):
                p = (k + az) % AZ
                pltpu.make_async_remote_copy(
                    stage.at[p], relay_in.at[az], a_send, a_recv,
                    device_id=(p, jnp.where(rad == 0, 3 - p % 3, 4 + p % 3)), device_id_type=MESH).start()
                return carry

            lax.fori_loop(0, AZ, step, 0)

    def start_x(sec, w):
        @pl.when(rad < RAD - 1)
        def _():
            x_copy(sec, w, True).start()

        @pl.when(rad > 0)
        def _():
            x_copy(sec, w, False).start()

    def start_y(sec, w):
        for f in range(NF):
            q = w[f, 2]
            q = pltpu.roll(q, 8, 1)
            for x in range(1, NX):
                q = jnp.where(block == x, pltpu.roll(w[f, x + 2], (16 * x + 8) % NY, 1), q)
            strips[sec, f] = q
        y_copy(sec, True).start()
        y_copy(sec, False).start()

    def serve():
        @pl.when(relay)
        def _():
            def signed(s):
                return jnp.where(relay_lo, s, COLS - s) % COLS

            shift_0, shift_1 = signed(shift_ref[0]), signed(shift_ref[1])
            f, j, half = az // 4, (az // 2) % 2, az % 2
            rows = pl.ds(pl.multiple_of(half * 8, 8), 8)
            side = jnp.where(relay_lo, 0, 1)
            across = jnp.where(relay_lo, 0, RAD - 1)
            small = lax.broadcasted_iota(jnp.int32, (8, NY), 1)
            pltpu.make_async_copy(relay_in, relay_in, a_recv).wait()

            def turn(slots, tiles, amount):
                part = amount % NY

                def step(k, carry):
                    for c, t in zip(slots, tiles):
                        relay_roll[c, k] = pltpu.roll(relay_in[k, t], (NY - part) % NY, 1)
                    return carry

                lax.fori_loop(0, AZ, step, 0, unroll=4)

            def pick(c, d, amount):
                whole, part = amount // NY, amount % NY
                return jnp.where(
                    small < NY - part, relay_roll[c, (d + whole) % AZ], relay_roll[c, (d + whole + 1) % AZ])

            turn((0,), (0,), shift_0)

            def near_step(k, carry):
                d = (k + az) % AZ
                near_out[d] = pick(0, d, shift_0)
                pltpu.make_async_remote_copy(
                    near_out.at[d], ghost.at[0, side, f, j, rows], b_send, x_recv.at[0, side],
                    device_id=(d, across), device_id_type=MESH).start()
                return carry

            lax.fori_loop(0, AZ, near_step, 0)
            turn((0, 1), (0, 1), shift_1)

            def pick_step(d, carry):
                for t in range(2):
                    far_out[d, t] = pick(t, d, shift_1)
                return carry

            lax.fori_loop(0, AZ, pick_step, 0)

            def far_step(k, carry):
                d = (k + az) % AZ
                far_out[d, 2] = jnp.where(small < NY // 2, far_out[(d + 1) % AZ, 0], far_out[(d + AZ - 1) % AZ, 0])
                pltpu.make_async_remote_copy(
                    far_out.at[d], far_in.at[:, f, j, rows], far_send, far_recv,
                    device_id=(d, across), device_id_type=MESH).start()
                return carry

            lax.fori_loop(0, AZ, far_step, 0)
            shift_2 = (shift_0 - shift_1 + COLS) % COLS
            turn((0,), (0,), shift_2)

            def plane_step(k, carry):
                d = (k + az) % AZ
                plane_out[d] = pick(0, d, shift_2)
                pltpu.make_async_remote_copy(
                    plane_out.at[d], plane_in.at[f, j, rows], plane_send, plane_recv,
                    device_id=(d, RAD - 1 - across), device_id_type=MESH).start()
                return carry

            lax.fori_loop(0, AZ, plane_step, 0)

    def inside(w):
        def row(x, carry):
            cells = [w[f, x + 2] for f in range(NF)]
            flux = rolled_faces(cells, 0, 2)
            for f in range(NF):
                acc[f, x] = pltpu.roll(flux[f], NZ - 1, 0) - flux[f]
            flux = rolled_faces(cells, 1, 1)
            for f in range(NF):
                masked = jnp.where(inner, flux[f], 0.0)
                acc[f, x] += pltpu.roll(masked, NY - 1, 1) - masked
            return carry

        lax.fori_loop(0, NX, row, 0)

    def x_faces(w, flux_ref, begin, end):
        def face(i, carry):
            lefts, rights = [], []
            for f in range(NF):
                c = [w[f, i + k] for k in range(4)]
                d = [c[k + 1] - c[k] for k in range(3)]
                lefts.append(c[1] + half_slope(d[0], d[1]))
                rights.append(c[2] - half_slope(d[1], d[2]))
            flux = twice_flux(lefts, rights, 0)
            for f in range(NF):
                flux_ref[f, i] = flux[f]
            return carry

        lax.fori_loop(begin, end, face, 0)

    def finish_y(sec):
        y_copy(sec, True).wait_recv()
        y_copy(sec, False).wait_recv()
        cells = []
        for f in range(NF):
            own = strips[sec, f]
            lower = jnp.where((slot >= 4) & (slot < 8), y_lo[sec, f], own)
            upper = jnp.where((slot >= 8) & (slot < 12), y_hi[sec, f], own)
            cells.append(jnp.where(slot < 8, pltpu.roll(lower, NY - 4, 1), pltpu.roll(upper, 4, 1)))
        flux = rolled_faces(cells, 1, 1)
        for f in range(NF):
            masked = jnp.where((slot == 4) | (slot == 5) | (slot == 11) | (slot == 12), flux[f], 0.0)
            d = pltpu.roll(masked, NY - 1, 1) - masked
            far = pltpu.roll(d, NY - 8, 1)
            corr[f] = jnp.where((slot == 4) | (slot == 5), d, jnp.where((slot == 2) | (slot == 3), far, 0.0))
        for f in range(NF):
            value = corr[f]
            for x in range(NX):
                acc[f, x] += jnp.where(seam, pltpu.roll(value, (124 - 16 * x) % NY, 1), 0.0)

    def receive_side(sec, w, side):
        pltpu.make_async_copy(ghost.at[sec, side], ghost.at[sec, side], x_recv.at[sec, side]).wait()
        for f in range(NF):
            for j in range(2):
                value = ghost[sec, side, f, j]
                if f == 2:
                    value = value + kick[side]
                w[f, j + (10 if side else 0)] = value

    def sheared_rows(w):
        pltpu.make_async_copy(plane_in, plane_in, plane_recv).wait()
        pltpu.make_async_copy(far_in, far_in, far_recv).wait()
        far_at = jnp.where(rad == 0, 0, 4)
        plane_kick = jnp.where(rad == 0, -shear_jump, shear_jump)
        for f in range(NF):
            for j in range(2):
                ext_rows[f, 2 + j] = far_in[0, f, j]
                ext_rows[f, far_at + j] = far_in[1, f, j]
                value = plane_in[f, j]
                if f == 2:
                    value = value + plane_kick
                ext_rows[f, 4 - far_at + j] = value
        x_faces(ext_rows, ext_flux, 0, 3)

        def row(j, carry):
            cells = [ext_rows[f, 2 + j] for f in range(NF)]
            flux = rolled_faces(cells, 0, 2)
            part = ghosted_divergence(cells, [far_in[2, f, j] for f in range(NF)], lane, 1)
            u = conserved_of(cells)
            for f in range(NF):
                total = pltpu.roll(flux[f], NZ - 1, 0) - flux[f] + part[f] + (ext_flux[f, j + 1] - ext_flux[f, j])
                u[f] = u[f] - (0.5 * time_step) * total
            mid = primitive_of(u)
            mid[2] = mid[2] - plane_kick
            at = jnp.where(rad == 0, 0, 10)
            for f in range(NF):
                w[f, at + j] = mid[f]
            return carry

        lax.fori_loop(0, 2, row, 0)

    def receive_x(sec, w):
        if sec == 0:
            receive_side(0, w, 0)
            receive_side(0, w, 1)
            return

        @pl.when(rad > 0)
        def _():
            receive_side(1, w, 0)

        @pl.when(rad < RAD - 1)
        def _():
            receive_side(1, w, 1)

        @pl.when(edge)
        def _():
            sheared_rows(w)

    def row_total(x):
        return [-0.5 * (acc[f, x] + (fx[f, x + 1] - fx[f, x])) for f in range(NF)]

    def middle(x, carry):
        total = row_total(x)
        u = conserved_row(x)
        w = primitive_of([u[f] + time_step * total[f] for f in range(NF)])
        for f in range(NF):
            tend[f, x] = total[f]
            w2[f, x + 2] = w[f]
        return carry

    out_rows = out_ref.reshape(NF * NZ * NX, NY)

    def last(x, carry):
        total = row_total(x)
        for f in range(NF):
            out_rows[pl.ds(f * NZ * NX + x, NZ, NX), :] = 0.5 * (tend[f, x] + total[f])
        return carry

    scatter()
    for sec, w, end in ((0, w1, middle), (1, w2, last)):
        start_x(sec, w)
        start_y(sec, w)
        inside(w)
        x_faces(w, fx, 2, 7)
        finish_y(sec)
        lax.fori_loop(2, 6, end, 0)
        if sec == 0:
            load_shift.wait()
            serve()
        receive_x(sec, w)
        x_faces(w, fx, 0, 2)
        x_faces(w, fx, 7, 9)
        lax.fori_loop(0, 2, end, 0)
        lax.fori_loop(6, 8, end, 0)

    for sec, w in ((0, w1), (1, w2)):
        y_copy(sec, True).wait_send()
        y_copy(sec, False).wait_send()

        @pl.when(rad < RAD - 1)
        def _():
            x_copy(sec, w, True).wait_send()

        @pl.when(rad > 0)
        def _():
            x_copy(sec, w, False).wait_send()

    @pl.when(edge)
    def _():
        pltpu.make_async_copy(stage, stage, a_send).wait()

    @pl.when(relay)
    def _():
        pltpu.make_async_copy(near_out, near_out, b_send).wait()
        pltpu.make_async_copy(far_out, far_out, far_send).wait()
        pltpu.make_async_copy(plane_out, plane_out, plane_send).wait()


def shards(conserved, shear_shift):
    f32 = jnp.float32
    return pl.pallas_call(
        kernel,
        out_shape=jax.ShapeDtypeStruct((NF, NZ, NX, NY), f32),
        in_specs=[pl.BlockSpec(memory_space=pltpu.HBM), pl.BlockSpec(memory_space=pltpu.HBM)],
        out_specs=pl.BlockSpec(memory_space=pltpu.VMEM),
        scratch_shapes=[
            pltpu.VMEM((NF, NZ, NX, NY), f32),
            pltpu.VMEM((NF, NX + 4, NZ, NY), f32),
            pltpu.VMEM((NF, NX + 4, NZ, NY), f32),
            pltpu.VMEM((NF, NX, NZ, NY), f32),
            pltpu.VMEM((NF, NX + 1, NZ, NY), f32),
            pltpu.VMEM((NF, NX, NZ, NY), f32),
            pltpu.VMEM((NF, NZ, NY), f32),
            pltpu.VMEM((2, NF, NZ, NY), f32),
            pltpu.VMEM((2, NF, NZ, NY), f32),
            pltpu.VMEM((2, NF, NZ, NY), f32),
            pltpu.VMEM((2, 2, NF, 2, NZ, NY), f32),
            pltpu.VMEM((AZ, 2, 8, NY), f32),
            pltpu.VMEM((AZ, 2, 8, NY), f32),
            pltpu.VMEM((2, AZ, 8, NY), f32),
            pltpu.VMEM((AZ, 8, NY), f32),
            pltpu.VMEM((AZ, 3, 8, NY), f32),
            pltpu.VMEM((AZ, 8, NY), f32),
            pltpu.VMEM((3, NF, 2, NZ, NY), f32),
            pltpu.VMEM((NF, 2, NZ, NY), f32),
            pltpu.VMEM((NF, 6, NZ, NY), f32),
            pltpu.VMEM((NF, 3, NZ, NY), f32),
            pltpu.SMEM((2,), jnp.int32),
            pltpu.SemaphoreType.DMA,
            pltpu.SemaphoreType.DMA,
            pltpu.SemaphoreType.DMA((2, 2)),
            pltpu.SemaphoreType.DMA((2, 2)),
            pltpu.SemaphoreType.DMA((2, 2)),
            pltpu.SemaphoreType.DMA((2, 2)),
            pltpu.SemaphoreType.DMA,
            pltpu.SemaphoreType.DMA,
            pltpu.SemaphoreType.DMA,
            pltpu.SemaphoreType.DMA,
            pltpu.SemaphoreType.DMA,
            pltpu.SemaphoreType.DMA,
            pltpu.SemaphoreType.DMA,
        ],
        name="mhd_step",
        compiler_params=pltpu.CompilerParams(
            collective_id=0, has_side_effects=True, vmem_limit_bytes=32 * 1024 * 1024),
    )(shear_shift, conserved)


def solution(mesh):
    return jax.shard_map(
        shards,
        mesh=mesh,
        in_specs=(P(None, None, "rad", "az"), P()),
        out_specs=P(None, None, "rad", "az"),
        check_vma=False,
    )
```

```python
import functools

import jax
import jax.numpy as jnp
from jax import lax
from jax.experimental import pallas as pl
from jax.experimental.pallas import tpu as pltpu
from jax.sharding import PartitionSpec as P

MESH = pl.DeviceIdType.MESH
time_step = 0.02
shear_jump = 0.5
AZ, RAD = 32, 8
NF, NX, NZ, NY = 8, 8, 16, 128
COLS = AZ * NY


def primitive_of(u):
    inv = 1.0 / u[0]
    v = [u[i] * inv for i in (1, 2, 3)]
    vv = v[0] * v[0] + v[1] * v[1] + v[2] * v[2]
    bb = u[5] * u[5] + u[6] * u[6] + u[7] * u[7]
    p = (2.0 / 3.0) * (u[4] - 0.5 * u[0] * vv - 0.5 * bb)
    return [u[0], v[0], v[1], v[2], p, u[5], u[6], u[7]]


def conserved_of(w):
    rho, v, p, b = w[0], w[1:4], w[4], w[5:8]
    vv = v[0] * v[0] + v[1] * v[1] + v[2] * v[2]
    bb = b[0] * b[0] + b[1] * b[1] + b[2] * b[2]
    return [rho] + [rho * c for c in v] + [1.5 * p + 0.5 * rho * vv + 0.5 * bb] + list(b)


def half_slope(a, b):
    return 0.5 * jnp.maximum(jnp.minimum(a, b), jnp.minimum(jnp.maximum(a, b), 0.0))


def state_of(w, n):
    rho, v, p, b = w[0], w[1:4], w[4], w[5:8]
    vn, bn = v[n], b[n]
    bb = b[0] * b[0] + b[1] * b[1] + b[2] * b[2]
    hb = 0.5 * bb
    vv = v[0] * v[0] + v[1] * v[1] + v[2] * v[2]
    vb = v[0] * b[0] + v[1] * b[1] + v[2] * b[2]
    pt = p + hb
    mom = [rho * c for c in v]
    en = 1.5 * p + 0.5 * rho * vv + hb
    fm = [mom[i] * vn - b[i] * bn for i in range(3)]
    fm[n] = fm[n] + pt
    fe = (en + pt) * vn - bn * vb
    fb = [None if i == n else b[i] * vn - v[i] * bn for i in range(3)]
    a = (5.0 / 3.0) * p + bb
    speed = jnp.abs(vn) + (a * lax.rsqrt(a)) * lax.rsqrt(rho)
    return [rho] + mom + [en] + list(b), [mom[n]] + fm + [fe] + fb, speed


def twice_flux(left, right, n):
    ul, fl, cl = state_of(left, n)
    ur, fr, cr = state_of(right, n)
    c = jnp.maximum(cl, cr)
    out = []
    for i in range(NF):
        diff = c * (ur[i] - ul[i])
        out.append(-diff if fl[i] is None else fl[i] + fr[i] - diff)
    return out


def rolled_faces(w, axis, n):
    size = w[0].shape[axis]
    left, right = [], []
    for f in range(NF):
        d = w[f] - pltpu.roll(w[f], 1, axis)
        h = half_slope(d, pltpu.roll(d, size - 1, axis))
        left.append(pltpu.roll(w[f] + h, 1, axis))
        right.append(w[f] - h)
    return twice_flux(left, right, n)


def ghosted_divergence(w, g, lane, n):
    size = w[0].shape[1]
    first, final = lane == 0, lane == size - 1
    left, right, left_g, right_g = [], [], [], []
    for f in range(NF):
        w_up, g_up = pltpu.roll(w[f], 1, 1), pltpu.roll(g[f], 1, 1)
        d = w[f] - jnp.where(first, g_up, w_up)
        d_g = g[f] - jnp.where(first, w_up, g_up)
        d_down, d_g_down = pltpu.roll(d, size - 1, 1), pltpu.roll(d_g, size - 1, 1)
        h = half_slope(d, jnp.where(final, d_g_down, d_down))
        h_g = half_slope(d_g, jnp.where(final, d_down, d_g_down))
        l_up = pltpu.roll(w[f] + h, 1, 1)
        left.append(jnp.where(first, pltpu.roll(g[f] + h_g, 1, 1), l_up))
        right.append(w[f] - h)
        left_g.append(l_up)
        right_g.append(g[f] - h_g)
    flux = twice_flux(left, right, n)
    flux_g = twice_flux(left_g, right_g, n)
    return [jnp.where(final, pltpu.roll(flux_g[f], size - 1, 1), pltpu.roll(flux[f], size - 1, 1)) - flux[f]
            for f in range(NF)]


def plane_of(p):
    return ((p // 2) % 4 + p // 8 + 2 * (p % 2)) % 4


def kernel(shift_hbm, u_hbm, out_ref, raw, w1, w2, acc, fx, tend, wt, ft, y_out, y_in, ghost, stage, relay_in,
           relay_roll, near_out, far_out, plane_out, far_in, plane_in, ext_rows, ext_flux, shift_ref, in_sem, shift_sem,
           x_send, x_recv, y_send, y_recv, a_send, a_recv, b_send, far_send, far_recv, plane_send, plane_recv):
    az = lax.axis_index("az")
    rad = lax.axis_index("rad")
    right, left = (az + 1) % AZ, (az + AZ - 1) % AZ
    edge = (rad == 0) | (rad == RAD - 1)
    relay_lo = rad == 4 + plane_of(az)
    relay_hi = rad == 3 - plane_of(az)
    relay = relay_lo | relay_hi
    both = edge & relay

    barrier = pltpu.get_barrier_semaphore()

    def signal(*device):
        pl.semaphore_signal(barrier, 1, device_id=device, device_id_type=MESH)

    load = pltpu.make_async_copy(u_hbm, raw, in_sem)
    load.start()
    load_shift = pltpu.make_async_copy(shift_hbm, shift_ref, shift_sem)
    load_shift.start()

    def others(body):
        @pl.when(jnp.logical_not(both))
        def _():
            body(az)

        def step(k, carry):
            body((k + az) % AZ)
            return carry

        lax.fori_loop(1, AZ, step, 0)

    @pl.when(relay)
    def _():
        others(lambda p: signal(p, jnp.where(relay_lo, RAD - 1, 0)))

    signal(right, rad)
    signal(left, rad)

    @pl.when(rad > 0)
    def _():
        signal(az, rad - 1)

    @pl.when(rad < RAD - 1)
    def _():
        signal(az, rad + 1)

    @pl.when(edge)
    def _():
        others(lambda p: signal(p, jnp.where(rad == 0, 3 - plane_of(p), 4 + plane_of(p))))

        def step(k, carry):
            p = (k + az) % AZ
            signal(p, jnp.where(rad == 0, 4 + plane_of(p), 3 - plane_of(p)))
            return carry

        lax.fori_loop(0, AZ, step, 0)

    lane = lax.broadcasted_iota(jnp.int32, (NZ, NY), 1)
    load.wait()
    u_rows = raw.reshape(NF * NZ * NX, NY)

    def conserved_row(x):
        return [u_rows[pl.ds(f * NZ * NX + x, NZ, NX), :] for f in range(NF)]

    def first_rows(x, carry):
        w = primitive_of(conserved_row(x))
        for f in range(NF):
            w1[f, x + 2] = w[f]
        return carry

    lax.fori_loop(0, NX, first_rows, 0)

    def turn_y(sec, w):
        for f in range(NF):
            wt[f, 8:8 + NY] = w[f, 2:2 + NX].reshape(NX * NZ, NY).T
        for f in range(NF):
            y_out[sec, 0, 2 * f:2 * f + 2] = wt[f, 8 + NY - 2:8 + NY]
            y_out[sec, 1, 2 * f:2 * f + 2] = wt[f, 8:10]

    @pl.when(edge)
    def _():
        near, far = jnp.where(rad == 0, 2, 8), jnp.where(rad == 0, 4, 6)
        for f in range(NF):
            for j in range(2):
                for t, base in ((0, near), (1, far)):
                    row = w1[f, base + j]
                    for half in range(2):
                        stage[f * 4 + j * 2 + half, t] = row[half * 8:half * 8 + 8]

    turn_y(0, w1)
    pl.semaphore_wait(barrier, jnp.where(edge, AZ + 3, 4) + jnp.where(relay, 2 * AZ, 0) - jnp.where(both, 2, 0))

    def x_copy(sec, w, up):
        rows = w.at[:, pl.ds(8 if up else 2, 2)]
        side = 0 if up else 1
        return pltpu.make_async_remote_copy(
            rows, ghost.at[sec, side], x_send.at[sec, side], x_recv.at[sec, side],
            device_id=(az, rad + 1 if up else rad - 1), device_id_type=MESH)

    def y_copy(sec, up):
        side = 0 if up else 1
        return pltpu.make_async_remote_copy(
            y_out.at[sec, side], y_in.at[sec, side], y_send.at[sec, side], y_recv.at[sec, side],
            device_id=(right if up else left, rad), device_id_type=MESH)

    def scatter():
        @pl.when(edge)
        def _():
            def send(p):
                pltpu.make_async_remote_copy(
                    stage.at[p], relay_in.at[az], a_send, a_recv,
                    device_id=(p, jnp.where(rad == 0, 3 - plane_of(p), 4 + plane_of(p))), device_id_type=MESH).start()

            others(send)

            @pl.when(both)
            def _():
                pltpu.make_async_copy(stage.at[az], relay_in.at[az], a_recv).start()

    def start_x(sec, w):
        @pl.when(rad < RAD - 1)
        def _():
            x_copy(sec, w, True).start()

        @pl.when(rad > 0)
        def _():
            x_copy(sec, w, False).start()

    def start_y(sec):
        y_copy(sec, True).start()
        y_copy(sec, False).start()

    def serve():
        @pl.when(relay)
        def _():
            def signed(s):
                return jnp.where(relay_lo, s, COLS - s) % COLS

            shift_0, shift_1 = signed(shift_ref[0]), signed(shift_ref[1])
            f, j, half = az // 4, (az // 2) % 2, az % 2
            rows = pl.ds(pl.multiple_of(half * 8, 8), 8)
            side = jnp.where(relay_lo, 0, 1)
            across = jnp.where(relay_lo, 0, RAD - 1)
            small = lax.broadcasted_iota(jnp.int32, (8, NY), 1)
            pltpu.make_async_copy(relay_in, relay_in, a_recv).wait()

            def turn(slots, tiles, amount):
                part = amount % NY

                for k in range(AZ):
                    for c, t in zip(slots, tiles):
                        relay_roll[c, k] = pltpu.roll(relay_in[k, t], (NY - part) % NY, 1)

            def pick(c, d, amount):
                whole, part = amount // NY, amount % NY
                return jnp.where(
                    small < NY - part, relay_roll[c, (d + whole) % AZ], relay_roll[c, (d + whole + 1) % AZ])

            turn((0,), (0,), shift_0)

            def near_step(k, carry):
                d = (k + az) % AZ
                near_out[d] = pick(0, d, shift_0)
                pltpu.make_async_remote_copy(
                    near_out.at[d], ghost.at[0, side, f, j, rows], b_send, x_recv.at[0, side],
                    device_id=(d, across), device_id_type=MESH).start()
                return carry

            lax.fori_loop(0, AZ, near_step, 0, unroll=4)
            turn((0, 1), (0, 1), shift_1)

            def pick_step(d, carry):
                for t in range(2):
                    far_out[d, t] = pick(t, d, shift_1)
                return carry

            lax.fori_loop(0, AZ, pick_step, 0, unroll=8)

            def far_step(k, carry):
                d = (k + az) % AZ
                far_out[d, 2] = jnp.where(small < NY // 2, far_out[(d + 1) % AZ, 0], far_out[(d + AZ - 1) % AZ, 0])
                pltpu.make_async_remote_copy(
                    far_out.at[d], far_in.at[:, f, j, rows], far_send, far_recv,
                    device_id=(d, across), device_id_type=MESH).start()
                return carry

            lax.fori_loop(0, AZ, far_step, 0, unroll=4)
            shift_2 = (shift_0 - shift_1 + COLS) % COLS
            turn((0,), (0,), shift_2)

            def plane_step(d, carry):
                plane_out[d] = pick(0, d, shift_2)
                return carry

            lax.fori_loop(0, AZ, plane_step, 0, unroll=8)

            def send(d):
                pltpu.make_async_remote_copy(
                    plane_out.at[d], plane_in.at[f, j, rows], plane_send, plane_recv,
                    device_id=(d, RAD - 1 - across), device_id_type=MESH).start()

            others(send)

            @pl.when(both)
            def _():
                pltpu.make_async_copy(plane_out.at[az], plane_in.at[f, j, rows], plane_recv).start()

    def z_part(w):
        def row(x, carry):
            flux = rolled_faces([w[f, x + 2] for f in range(NF)], 0, 2)
            for f in range(NF):
                acc[f, x] = pltpu.roll(flux[f], NZ - 1, 0) - flux[f]
            return carry

        lax.fori_loop(0, NX, row, 0)

    def y_faces(k):
        lefts, rights = [], []
        for f in range(NF):
            c = [wt[f, pl.ds(8 * k + 6 + o, 8)] for o in range(4)]
            d = [c[o + 1] - c[o] for o in range(3)]
            lefts.append(c[1] + half_slope(d[0], d[1]))
            rights.append(c[2] - half_slope(d[1], d[2]))
        flux = twice_flux(lefts, rights, 1)
        for f in range(NF):
            ft[f, pl.ds(pl.multiple_of(8 * k, 8), 8)] = flux[f]

    def y_part():
        def pair(k, carry):
            y_faces(2 * k + 1)
            y_faces(2 * k + 2)
            return carry

        lax.fori_loop(0, 7, pair, 0)

    def x_faces(w, flux_ref, begin, end):
        def face(i, carry):
            lefts, rights = [], []
            for f in range(NF):
                c = [w[f, i + k] for k in range(4)]
                d = [c[k + 1] - c[k] for k in range(3)]
                lefts.append(c[1] + half_slope(d[0], d[1]))
                rights.append(c[2] - half_slope(d[1], d[2]))
            flux = twice_flux(lefts, rights, 0)
            for f in range(NF):
                flux_ref[f, i] = flux[f]
            return carry

        lax.fori_loop(begin, end, face, 0)

    def finish_y(sec):
        y_copy(sec, True).wait_recv()
        y_copy(sec, False).wait_recv()
        for f in range(NF):
            wt[f, 6:8] = y_in[sec, 0, 2 * f:2 * f + 2]
            wt[f, 8 + NY:10 + NY] = y_in[sec, 1, 2 * f:2 * f + 2]
        for k in (0, 15, 16):
            y_faces(k)
        for f in range(NF):
            part = (ft[f, 1:NY + 1] - ft[f, 0:NY]).T
            acc[f] += part.reshape(NX, NZ, NY)

    def receive_side(sec, w, side):
        pltpu.make_async_copy(ghost.at[sec, side], ghost.at[sec, side], x_recv.at[sec, side]).wait()
        kick = jnp.where((rad == 0) & (side == 0), shear_jump, 0.0) - jnp.where(
            (rad == RAD - 1) & (side == 1), shear_jump, 0.0)
        for f in range(NF):
            for j in range(2):
                value = ghost[sec, side, f, j]
                w[f, 10 * side + j] = value + kick if f == 2 else value

    def sheared_rows(w):
        pltpu.make_async_copy(plane_in, plane_in, plane_recv).wait()
        pltpu.make_async_copy(far_in, far_in, far_recv).wait()
        far_at = jnp.where(rad == 0, 0, 4)
        plane_kick = jnp.where(rad == 0, -shear_jump, shear_jump)
        for f in range(NF):
            for j in range(2):
                ext_rows[f, 2 + j] = far_in[0, f, j]
                ext_rows[f, far_at + j] = far_in[1, f, j]
                value = plane_in[f, j]
                if f == 2:
                    value = value + plane_kick
                ext_rows[f, 4 - far_at + j] = value
        x_faces(ext_rows, ext_flux, 0, 3)

        def row(j, carry):
            cells = [ext_rows[f, 2 + j] for f in range(NF)]
            flux = rolled_faces(cells, 0, 2)
            part = ghosted_divergence(cells, [far_in[2, f, j] for f in range(NF)], lane, 1)
            u = conserved_of(cells)
            for f in range(NF):
                total = pltpu.roll(flux[f], NZ - 1, 0) - flux[f] + part[f] + (ext_flux[f, j + 1] - ext_flux[f, j])
                u[f] = u[f] - (0.5 * time_step) * total
            mid = primitive_of(u)
            mid[2] = mid[2] - plane_kick
            at = jnp.where(rad == 0, 0, 10)
            for f in range(NF):
                w[f, at + j] = mid[f]
            return carry

        lax.fori_loop(0, 2, row, 0)

    def sides(sec, w, end):
        def step(k, carry):
            side = (k + jnp.where(rad == 0, 1, 0)) % 2
            if sec == 0:
                receive_side(sec, w, side)
            else:
                sheared = edge & (k == 1)

                @pl.when(sheared)
                def _():
                    sheared_rows(w)

                @pl.when(jnp.logical_not(sheared))
                def _():
                    receive_side(sec, w, side)

            x_faces(w, fx, 7 * side, 7 * side + 2)
            lax.fori_loop(6 * side, 6 * side + 2, end, 0)
            return carry

        lax.fori_loop(0, 2, step, 0)

    def row_total(x):
        return [-0.5 * (acc[f, x] + (fx[f, x + 1] - fx[f, x])) for f in range(NF)]

    def middle(x, carry):
        total = row_total(x)
        u = conserved_row(x)
        w = primitive_of([u[f] + time_step * total[f] for f in range(NF)])
        for f in range(NF):
            tend[f, x] = total[f]
            w2[f, x + 2] = w[f]
        return carry

    out_rows = out_ref.reshape(NF * NZ * NX, NY)

    def last(x, carry):
        total = row_total(x)
        for f in range(NF):
            out_rows[pl.ds(f * NZ * NX + x, NZ, NX), :] = 0.5 * (tend[f, x] + total[f])
        return carry

    scatter()
    for sec, w, end in ((0, w1, middle), (1, w2, last)):
        start_x(sec, w)
        if sec == 1:
            turn_y(sec, w)
        start_y(sec)
        z_part(w)
        y_part()
        x_faces(w, fx, 2, 7)
        finish_y(sec)
        lax.fori_loop(2, 6, end, 0)
        if sec == 0:
            load_shift.wait()
            serve()
        sides(sec, w, end)

    for sec, w in ((0, w1), (1, w2)):
        y_copy(sec, True).wait_send()
        y_copy(sec, False).wait_send()

        @pl.when(rad < RAD - 1)
        def _():
            x_copy(sec, w, True).wait_send()

        @pl.when(rad > 0)
        def _():
            x_copy(sec, w, False).wait_send()

    @pl.when(edge)
    def _():
        most = stage.at[pl.ds(0, AZ - 1)]
        pltpu.make_async_copy(most, most, a_send).wait()

        @pl.when(jnp.logical_not(relay))
        def _():
            pltpu.make_async_copy(stage.at[0], stage.at[0], a_send).wait()

    @pl.when(relay)
    def _():
        pltpu.make_async_copy(near_out, near_out, b_send).wait()
        pltpu.make_async_copy(far_out, far_out, far_send).wait()
        most = plane_out.at[pl.ds(0, AZ - 1)]
        pltpu.make_async_copy(most, most, plane_send).wait()

        @pl.when(jnp.logical_not(edge))
        def _():
            pltpu.make_async_copy(plane_out.at[0], plane_out.at[0], plane_send).wait()


def shards(conserved, shear_shift):
    f32 = jnp.float32
    return pl.pallas_call(
        kernel,
        out_shape=jax.ShapeDtypeStruct((NF, NZ, NX, NY), f32),
        in_specs=[pl.BlockSpec(memory_space=pltpu.HBM), pl.BlockSpec(memory_space=pltpu.HBM)],
        out_specs=pl.BlockSpec(memory_space=pltpu.VMEM),
        scratch_shapes=[
            pltpu.VMEM((NF, NZ, NX, NY), f32),
            pltpu.VMEM((NF, NX + 4, NZ, NY), f32),
            pltpu.VMEM((NF, NX + 4, NZ, NY), f32),
            pltpu.VMEM((NF, NX, NZ, NY), f32),
            pltpu.VMEM((NF, NX + 1, NZ, NY), f32),
            pltpu.VMEM((NF, NX, NZ, NY), f32),
            pltpu.VMEM((NF, NY + 24, NX * NZ), f32),
            pltpu.VMEM((NF, NY + 8, NX * NZ), f32),
            pltpu.VMEM((2, 2, 2 * NF, NX * NZ), f32),
            pltpu.VMEM((2, 2, 2 * NF, NX * NZ), f32),
            pltpu.VMEM((2, 2, NF, 2, NZ, NY), f32),
            pltpu.VMEM((AZ, 2, 8, NY), f32),
            pltpu.VMEM((AZ, 2, 8, NY), f32),
            pltpu.VMEM((2, AZ, 8, NY), f32),
            pltpu.VMEM((AZ, 8, NY), f32),
            pltpu.VMEM((AZ, 3, 8, NY), f32),
            pltpu.VMEM((AZ, 8, NY), f32),
            pltpu.VMEM((3, NF, 2, NZ, NY), f32),
            pltpu.VMEM((NF, 2, NZ, NY), f32),
            pltpu.VMEM((NF, 6, NZ, NY), f32),
            pltpu.VMEM((NF, 3, NZ, NY), f32),
            pltpu.SMEM((2,), jnp.int32),
            pltpu.SemaphoreType.DMA,
            pltpu.SemaphoreType.DMA,
            pltpu.SemaphoreType.DMA((2, 2)),
            pltpu.SemaphoreType.DMA((2, 2)),
            pltpu.SemaphoreType.DMA((2, 2)),
            pltpu.SemaphoreType.DMA((2, 2)),
            pltpu.SemaphoreType.DMA,
            pltpu.SemaphoreType.DMA,
            pltpu.SemaphoreType.DMA,
            pltpu.SemaphoreType.DMA,
            pltpu.SemaphoreType.DMA,
            pltpu.SemaphoreType.DMA,
            pltpu.SemaphoreType.DMA,
        ],
        name="mhd_step",
        compiler_params=pltpu.CompilerParams(
            collective_id=0, has_side_effects=True, vmem_limit_bytes=53 * 1024 * 1024),
    )(shear_shift, conserved)


def solution(mesh):
    return jax.shard_map(
        shards,
        mesh=mesh,
        in_specs=(P(None, None, "rad", "az"), P()),
        out_specs=P(None, None, "rad", "az"),
        check_vma=False,
    )
```

```python
import functools

import jax
import jax.numpy as jnp
from jax import lax
from jax.experimental import pallas as pl
from jax.experimental.pallas import tpu as pltpu
from jax.sharding import PartitionSpec as P

MESH = pl.DeviceIdType.MESH
time_step = 0.02
shear_jump = 0.5
AZ, RAD = 32, 8
NF, NX, NZ, NY = 8, 8, 16, 128
COLS = AZ * NY


def primitive_of(u):
    inv = 1.0 / u[0]
    v = [u[i] * inv for i in (1, 2, 3)]
    vv = v[0] * v[0] + v[1] * v[1] + v[2] * v[2]
    bb = u[5] * u[5] + u[6] * u[6] + u[7] * u[7]
    p = (2.0 / 3.0) * (u[4] - 0.5 * u[0] * vv - 0.5 * bb)
    return [u[0], v[0], v[1], v[2], p, u[5], u[6], u[7]]


def conserved_of(w):
    rho, v, p, b = w[0], w[1:4], w[4], w[5:8]
    vv = v[0] * v[0] + v[1] * v[1] + v[2] * v[2]
    bb = b[0] * b[0] + b[1] * b[1] + b[2] * b[2]
    return [rho] + [rho * c for c in v] + [1.5 * p + 0.5 * rho * vv + 0.5 * bb] + list(b)


def half_slope(a, b):
    return 0.5 * jnp.maximum(jnp.minimum(a, b), jnp.minimum(jnp.maximum(a, b), 0.0))


def state_of(w, n):
    rho, v, p, b = w[0], w[1:4], w[4], w[5:8]
    vn, bn = v[n], b[n]
    bb = b[0] * b[0] + b[1] * b[1] + b[2] * b[2]
    hb = 0.5 * bb
    vv = v[0] * v[0] + v[1] * v[1] + v[2] * v[2]
    vb = v[0] * b[0] + v[1] * b[1] + v[2] * b[2]
    pt = p + hb
    mom = [rho * c for c in v]
    en = 1.5 * p + 0.5 * rho * vv + hb
    fm = [mom[i] * vn - b[i] * bn for i in range(3)]
    fm[n] = fm[n] + pt
    fe = (en + pt) * vn - bn * vb
    fb = [None if i == n else b[i] * vn - v[i] * bn for i in range(3)]
    a = (5.0 / 3.0) * p + bb
    speed = jnp.abs(vn) + (a * lax.rsqrt(a)) * lax.rsqrt(rho)
    return [rho] + mom + [en] + list(b), [mom[n]] + fm + [fe] + fb, speed


def twice_flux(left, right, n):
    ul, fl, cl = state_of(left, n)
    ur, fr, cr = state_of(right, n)
    c = jnp.maximum(cl, cr)
    out = []
    for i in range(NF):
        diff = c * (ur[i] - ul[i])
        out.append(-diff if fl[i] is None else fl[i] + fr[i] - diff)
    return out


def rolled_faces(w, axis, n):
    size = w[0].shape[axis]
    left, right = [], []
    for f in range(NF):
        d = w[f] - pltpu.roll(w[f], 1, axis)
        h = half_slope(d, pltpu.roll(d, size - 1, axis))
        left.append(pltpu.roll(w[f] + h, 1, axis))
        right.append(w[f] - h)
    return twice_flux(left, right, n)


def ghosted_divergence(w, g, lane, n):
    size = w[0].shape[1]
    first, final = lane == 0, lane == size - 1
    left, right, left_g, right_g = [], [], [], []
    for f in range(NF):
        w_up, g_up = pltpu.roll(w[f], 1, 1), pltpu.roll(g[f], 1, 1)
        d = w[f] - jnp.where(first, g_up, w_up)
        d_g = g[f] - jnp.where(first, w_up, g_up)
        d_down, d_g_down = pltpu.roll(d, size - 1, 1), pltpu.roll(d_g, size - 1, 1)
        h = half_slope(d, jnp.where(final, d_g_down, d_down))
        h_g = half_slope(d_g, jnp.where(final, d_down, d_g_down))
        l_up = pltpu.roll(w[f] + h, 1, 1)
        left.append(jnp.where(first, pltpu.roll(g[f] + h_g, 1, 1), l_up))
        right.append(w[f] - h)
        left_g.append(l_up)
        right_g.append(g[f] - h_g)
    flux = twice_flux(left, right, n)
    flux_g = twice_flux(left_g, right_g, n)
    return [jnp.where(final, pltpu.roll(flux_g[f], size - 1, 1), pltpu.roll(flux[f], size - 1, 1)) - flux[f]
            for f in range(NF)]


def plane_of(p):
    return 3 - ((p // 2) % 4 + p // 8 + p % 2) % 3


def kernel(shift_hbm, u_hbm, out_ref, raw, w1, w2, acc, fx, tend, wt, ft, y_out, y_in, ghost, stage, relay_in,
           relay_roll, near_out, far_out, plane_out, far_in, plane_in, ext_rows, ext_flux, shift_ref, in_sem, shift_sem,
           x_send, x_recv, y_send, y_recv, a_send, a_recv, b_send, far_send, far_recv, plane_send, plane_recv):
    az = lax.axis_index("az")
    rad = lax.axis_index("rad")
    right, left = (az + 1) % AZ, (az + AZ - 1) % AZ
    edge = (rad == 0) | (rad == RAD - 1)
    relay_lo = rad == 4 + plane_of(az)
    relay_hi = rad == 3 - plane_of(az)
    relay = relay_lo | relay_hi
    both = edge & relay

    barrier = pltpu.get_barrier_semaphore()

    def signal(*device):
        pl.semaphore_signal(barrier, 1, device_id=device, device_id_type=MESH)

    load = pltpu.make_async_copy(u_hbm, raw, in_sem)
    load.start()
    load_shift = pltpu.make_async_copy(shift_hbm, shift_ref, shift_sem)
    load_shift.start()

    def peer(k, across):
        z, x, core = az // 8, (az // 2) % 4, az % 2
        zi, xi = k // 8, (k // 2) % 4
        if across:
            zi = 3 - zi
        z = jnp.where(zi == 0, 3 - z, jnp.where(zi == 1, (z + 2) % 4, jnp.where(zi == 2, z + 1 - 2 * (z % 2), z)))
        x = (x + jnp.where(xi == 0, 2, jnp.where(xi == 3, 0, 2 * xi - 1))) % 4
        core = jnp.where(k % 2 == 0, 1 - core, core)
        return (z * 4 + x) * 2 + core

    def others(body):
        def step(k, carry):
            body(peer(k, False))
            return carry

        lax.fori_loop(0, AZ - 1, step, 0)

        @pl.when(jnp.logical_not(both))
        def _():
            body(az)

    @pl.when(relay)
    def _():
        others(lambda p: signal(p, jnp.where(relay_lo, RAD - 1, 0)))

    signal(right, rad)
    signal(left, rad)

    @pl.when(rad > 0)
    def _():
        signal(az, rad - 1)

    @pl.when(rad < RAD - 1)
    def _():
        signal(az, rad + 1)

    @pl.when(edge)
    def _():
        signal(az, RAD - 1 - rad)

    lane = lax.broadcasted_iota(jnp.int32, (NZ, NY), 1)
    load.wait()
    u_rows = raw.reshape(NF * NZ * NX, NY)

    def conserved_row(x):
        return [u_rows[pl.ds(f * NZ * NX + x, NZ, NX), :] for f in range(NF)]

    def first_rows(x, carry):
        w = primitive_of(conserved_row(x))
        for f in range(NF):
            w1[f, x + 2] = w[f]
        return carry

    lax.fori_loop(0, NX, first_rows, 0)

    def turn_y(sec, w):
        for f in range(NF):
            wt[f, 8:8 + NY] = w[f, 2:2 + NX].reshape(NX * NZ, NY).T
        for f in range(NF):
            y_out[sec, 0, 2 * f:2 * f + 2] = wt[f, 8 + NY - 2:8 + NY]
            y_out[sec, 1, 2 * f:2 * f + 2] = wt[f, 8:10]

    @pl.when(edge)
    def _():
        near, far = jnp.where(rad == 0, 2, 8), jnp.where(rad == 0, 4, 6)
        for f in range(NF):
            for j in range(2):
                for t, base in ((0, near), (1, far)):
                    row = w1[f, base + j]
                    for half in range(2):
                        stage[t, f * 4 + j * 2 + half] = row[half * 8:half * 8 + 8]

    turn_y(0, w1)
    pl.semaphore_wait(barrier, jnp.where(edge, AZ + 4, 4) - jnp.where(both, 1, 0))

    def x_copy(sec, w, up):
        rows = w.at[:, pl.ds(8 if up else 2, 2)]
        side = 0 if up else 1
        return pltpu.make_async_remote_copy(
            rows, ghost.at[sec, side], x_send.at[sec, side], x_recv.at[sec, side],
            device_id=(az, rad + 1 if up else rad - 1), device_id_type=MESH)

    def y_copy(sec, up):
        side = 0 if up else 1
        return pltpu.make_async_remote_copy(
            y_out.at[sec, side], y_in.at[sec, side], y_send.at[sec, side], y_recv.at[sec, side],
            device_id=(right if up else left, rad), device_id_type=MESH)

    def scatter():
        @pl.when(edge)
        def _():
            for t in range(2):
                def send(p):
                    pltpu.make_async_remote_copy(
                        stage.at[t, p], relay_in.at[t, az], a_send.at[t], a_recv.at[t],
                        device_id=(p, jnp.where(rad == 0, 3 - plane_of(p), 4 + plane_of(p))), device_id_type=MESH).start()

                others(send)

                @pl.when(both)
                def _():
                    pltpu.make_async_copy(stage.at[t, az], relay_in.at[t, az], a_recv.at[t]).start()

    def start_x(sec, w, side):
        @pl.when((side == 1) & (rad < RAD - 1))
        def _():
            x_copy(sec, w, True).start()

        @pl.when((side == 0) & (rad > 0))
        def _():
            x_copy(sec, w, False).start()

    def start_y(sec):
        y_copy(sec, True).start()
        y_copy(sec, False).start()

    def serve():
        @pl.when(relay)
        def _():
            def signed(s):
                return jnp.where(relay_lo, s, COLS - s) % COLS

            shift_0, shift_1 = signed(shift_ref[0]), signed(shift_ref[1])
            f, j, half = az // 4, (az // 2) % 2, az % 2
            rows = pl.ds(pl.multiple_of(half * 8, 8), 8)
            side = jnp.where(relay_lo, 0, 1)
            across = jnp.where(relay_lo, 0, RAD - 1)
            small = lax.broadcasted_iota(jnp.int32, (8, NY), 1)

            def arrived(t):
                pltpu.make_async_copy(relay_in.at[t], relay_in.at[t], a_recv.at[t]).wait()

            def turn(slots, tiles, amount):
                part = amount % NY

                for k in range(AZ):
                    for c, t in zip(slots, tiles):
                        relay_roll[c, k] = pltpu.roll(relay_in[t, k], (NY - part) % NY, 1)

            def pick(c, d, amount):
                whole, part = amount // NY, amount % NY
                return jnp.where(
                    small < NY - part, relay_roll[c, (d + whole) % AZ], relay_roll[c, (d + whole + 1) % AZ])

            arrived(0)
            turn((0,), (0,), shift_0)

            def near_step(k, carry):
                d = peer(k, True)
                near_out[d] = pick(0, d, shift_0)
                pltpu.make_async_remote_copy(
                    near_out.at[d], ghost.at[0, side, f, j, rows], b_send, x_recv.at[0, side],
                    device_id=(d, across), device_id_type=MESH).start()
                return carry

            lax.fori_loop(0, AZ, near_step, 0, unroll=4)
            turn((0,), (0,), shift_1)
            arrived(1)
            turn((1,), (1,), shift_1)

            def pick_step(d, carry):
                for t in range(2):
                    far_out[d, t] = pick(t, d, shift_1)
                return carry

            lax.fori_loop(0, AZ, pick_step, 0, unroll=8)

            def far_step(k, carry):
                d = peer(k, True)
                far_out[d, 2] = jnp.where(small < NY // 2, far_out[(d + 1) % AZ, 0], far_out[(d + AZ - 1) % AZ, 0])
                pltpu.make_async_remote_copy(
                    far_out.at[d], far_in.at[:, f, j, rows], far_send, far_recv,
                    device_id=(d, across), device_id_type=MESH).start()
                return carry

            lax.fori_loop(0, AZ, far_step, 0, unroll=4)
            shift_2 = (shift_0 - shift_1 + COLS) % COLS
            turn((0,), (0,), shift_2)

            def plane_step(d, carry):
                plane_out[d] = pick(0, d, shift_2)
                return carry

            lax.fori_loop(0, AZ, plane_step, 0, unroll=8)

            def send(d):
                pltpu.make_async_remote_copy(
                    plane_out.at[d], plane_in.at[f, j, rows], plane_send, plane_recv,
                    device_id=(d, RAD - 1 - across), device_id_type=MESH).start()

            others(send)

            @pl.when(both)
            def _():
                pltpu.make_async_copy(plane_out.at[az], plane_in.at[f, j, rows], plane_recv).start()

    def z_part(w):
        def row(x, carry):
            flux = rolled_faces([w[f, x + 2] for f in range(NF)], 0, 2)
            for f in range(NF):
                acc[f, x] = pltpu.roll(flux[f], NZ - 1, 0) - flux[f]
            return carry

        lax.fori_loop(0, NX, row, 0)

    def y_faces(k):
        lefts, rights = [], []
        for f in range(NF):
            c = [wt[f, pl.ds(8 * k + 6 + o, 8)] for o in range(4)]
            d = [c[o + 1] - c[o] for o in range(3)]
            lefts.append(c[1] + half_slope(d[0], d[1]))
            rights.append(c[2] - half_slope(d[1], d[2]))
        flux = twice_flux(lefts, rights, 1)
        for f in range(NF):
            ft[f, pl.ds(pl.multiple_of(8 * k, 8), 8)] = flux[f]

    def y_part():
        def pair(k, carry):
            y_faces(2 * k + 1)
            y_faces(2 * k + 2)
            return carry

        lax.fori_loop(0, 7, pair, 0)

    def x_faces(w, flux_ref, begin, end):
        def face(i, carry):
            lefts, rights = [], []
            for f in range(NF):
                c = [w[f, i + k] for k in range(4)]
                d = [c[k + 1] - c[k] for k in range(3)]
                lefts.append(c[1] + half_slope(d[0], d[1]))
                rights.append(c[2] - half_slope(d[1], d[2]))
            flux = twice_flux(lefts, rights, 0)
            for f in range(NF):
                flux_ref[f, i] = flux[f]
            return carry

        lax.fori_loop(begin, end, face, 0)

    def finish_y(sec):
        y_copy(sec, True).wait_recv()
        y_copy(sec, False).wait_recv()
        for f in range(NF):
            wt[f, 6:8] = y_in[sec, 0, 2 * f:2 * f + 2]
            wt[f, 8 + NY:10 + NY] = y_in[sec, 1, 2 * f:2 * f + 2]
        for k in (0, 15, 16):
            y_faces(k)
        for f in range(NF):
            part = (ft[f, 1:NY + 1] - ft[f, 0:NY]).T
            acc[f] += part.reshape(NX, NZ, NY)

    def receive_side(sec, w, side):
        pltpu.make_async_copy(ghost.at[sec, side], ghost.at[sec, side], x_recv.at[sec, side]).wait()
        kick = jnp.where((rad == 0) & (side == 0), shear_jump, 0.0) - jnp.where(
            (rad == RAD - 1) & (side == 1), shear_jump, 0.0)
        for f in range(NF):
            for j in range(2):
                value = ghost[sec, side, f, j]
                w[f, 10 * side + j] = value + kick if f == 2 else value

    def sheared_rows(w):
        pltpu.make_async_copy(plane_in, plane_in, plane_recv).wait()
        pltpu.make_async_copy(far_in, far_in, far_recv).wait()
        far_at = jnp.where(rad == 0, 0, 4)
        plane_kick = jnp.where(rad == 0, -shear_jump, shear_jump)
        for f in range(NF):
            for j in range(2):
                ext_rows[f, 2 + j] = far_in[0, f, j]
                ext_rows[f, far_at + j] = far_in[1, f, j]
                value = plane_in[f, j]
                if f == 2:
                    value = value + plane_kick
                ext_rows[f, 4 - far_at + j] = value
        x_faces(ext_rows, ext_flux, 0, 3)

        at = jnp.where(rad == 0, 0, 10)
        for j in range(2):
            cells = [ext_rows[f, 2 + j] for f in range(NF)]
            flux = rolled_faces(cells, 0, 2)
            part = ghosted_divergence(cells, [far_in[2, f, j] for f in range(NF)], lane, 1)
            u = conserved_of(cells)
            for f in range(NF):
                total = pltpu.roll(flux[f], NZ - 1, 0) - flux[f] + part[f] + (ext_flux[f, j + 1] - ext_flux[f, j])
                u[f] = u[f] - (0.5 * time_step) * total
            mid = primitive_of(u)
            mid[2] = mid[2] - plane_kick
            for f in range(NF):
                w[f, at + j] = mid[f]

    def side_at(k):
        return (k + jnp.where(rad == 0, 1, 0)) % 2

    def side_faces(w, side):
        x_faces(w, fx, 7 * side, 7 * side + 2)

    def row_total(x):
        return [-0.5 * (acc[f, x] + (fx[f, x + 1] - fx[f, x])) for f in range(NF)]

    def middle(x, carry):
        total = row_total(x)
        u = conserved_row(x)
        w = primitive_of([u[f] + time_step * total[f] for f in range(NF)])
        for f in range(NF):
            tend[f, x] = total[f]
            w2[f, x + 2] = w[f]
        return carry

    out_rows = out_ref.reshape(NF * NZ * NX, NY)

    def last(x, carry):
        total = row_total(x)
        for f in range(NF):
            out_rows[pl.ds(f * NZ * NX + x, NZ, NX), :] = 0.5 * (tend[f, x] + total[f])
        return carry

    def bulk(w):
        z_part(w)
        y_part()
        x_faces(w, fx, 2, 7)

    scatter()
    start_y(0)
    bulk(w1)
    finish_y(0)
    lax.fori_loop(2, 6, middle, 0)
    start_x(0, w1, 0)
    start_x(0, w1, 1)
    load_shift.wait()
    serve()

    def first_side(k, carry):
        side = side_at(k)
        receive_side(0, w1, side)
        side_faces(w1, side)
        lax.fori_loop(6 * side, 6 * side + 2, middle, 0)
        start_x(1, w2, side)
        return carry

    lax.fori_loop(0, 2, first_side, 0)
    turn_y(1, w2)
    start_y(1)
    bulk(w2)

    def second_side(k, carry):
        side = side_at(k)
        sheared = edge & (k == 1)

        @pl.when(sheared)
        def _():
            sheared_rows(w2)

        @pl.when(jnp.logical_not(sheared))
        def _():
            receive_side(1, w2, side)

        side_faces(w2, side)
        return carry

    lax.fori_loop(0, 2, second_side, 0)
    finish_y(1)
    lax.fori_loop(0, NX, last, 0)

    for sec, w in ((0, w1), (1, w2)):
        y_copy(sec, True).wait_send()
        y_copy(sec, False).wait_send()

        @pl.when(rad < RAD - 1)
        def _():
            x_copy(sec, w, True).wait_send()

        @pl.when(rad > 0)
        def _():
            x_copy(sec, w, False).wait_send()

    @pl.when(edge)
    def _():
        for t in range(2):
            most = stage.at[t, pl.ds(0, AZ - 1)]
            pltpu.make_async_copy(most, most, a_send.at[t]).wait()

            @pl.when(jnp.logical_not(relay))
            def _():
                pltpu.make_async_copy(stage.at[t, 0], stage.at[t, 0], a_send.at[t]).wait()

    @pl.when(relay)
    def _():
        pltpu.make_async_copy(near_out, near_out, b_send).wait()
        pltpu.make_async_copy(far_out, far_out, far_send).wait()
        most = plane_out.at[pl.ds(0, AZ - 1)]
        pltpu.make_async_copy(most, most, plane_send).wait()

        @pl.when(jnp.logical_not(edge))
        def _():
            pltpu.make_async_copy(plane_out.at[0], plane_out.at[0], plane_send).wait()


def shards(conserved, shear_shift):
    f32 = jnp.float32
    return pl.pallas_call(
        kernel,
        out_shape=jax.ShapeDtypeStruct((NF, NZ, NX, NY), f32),
        in_specs=[pl.BlockSpec(memory_space=pltpu.HBM), pl.BlockSpec(memory_space=pltpu.HBM)],
        out_specs=pl.BlockSpec(memory_space=pltpu.VMEM),
        scratch_shapes=[
            pltpu.VMEM((NF, NZ, NX, NY), f32),
            pltpu.VMEM((NF, NX + 4, NZ, NY), f32),
            pltpu.VMEM((NF, NX + 4, NZ, NY), f32),
            pltpu.VMEM((NF, NX, NZ, NY), f32),
            pltpu.VMEM((NF, NX + 1, NZ, NY), f32),
            pltpu.VMEM((NF, NX, NZ, NY), f32),
            pltpu.VMEM((NF, NY + 24, NX * NZ), f32),
            pltpu.VMEM((NF, NY + 8, NX * NZ), f32),
            pltpu.VMEM((2, 2, 2 * NF, NX * NZ), f32),
            pltpu.VMEM((2, 2, 2 * NF, NX * NZ), f32),
            pltpu.VMEM((2, 2, NF, 2, NZ, NY), f32),
            pltpu.VMEM((2, AZ, 8, NY), f32),
            pltpu.VMEM((2, AZ, 8, NY), f32),
            pltpu.VMEM((2, AZ, 8, NY), f32),
            pltpu.VMEM((AZ, 8, NY), f32),
            pltpu.VMEM((AZ, 3, 8, NY), f32),
            pltpu.VMEM((AZ, 8, NY), f32),
            pltpu.VMEM((3, NF, 2, NZ, NY), f32),
            pltpu.VMEM((NF, 2, NZ, NY), f32),
            pltpu.VMEM((NF, 6, NZ, NY), f32),
            pltpu.VMEM((NF, 3, NZ, NY), f32),
            pltpu.SMEM((2,), jnp.int32),
            pltpu.SemaphoreType.DMA,
            pltpu.SemaphoreType.DMA,
            pltpu.SemaphoreType.DMA((2, 2)),
            pltpu.SemaphoreType.DMA((2, 2)),
            pltpu.SemaphoreType.DMA((2, 2)),
            pltpu.SemaphoreType.DMA((2, 2)),
            pltpu.SemaphoreType.DMA((2,)),
            pltpu.SemaphoreType.DMA((2,)),
            pltpu.SemaphoreType.DMA,
            pltpu.SemaphoreType.DMA,
            pltpu.SemaphoreType.DMA,
            pltpu.SemaphoreType.DMA,
            pltpu.SemaphoreType.DMA,
        ],
        name="mhd_step",
        compiler_params=pltpu.CompilerParams(
            collective_id=0, has_side_effects=True, vmem_limit_bytes=53 * 1024 * 1024),
    )(shear_shift, conserved)


def solution(mesh):
    return jax.shard_map(
        shards,
        mesh=mesh,
        in_specs=(P(None, None, "rad", "az"), P()),
        out_specs=P(None, None, "rad", "az"),
        check_vma=False,
    )
```

```python
import functools

import jax
import jax.numpy as jnp
from jax import lax
from jax.experimental import pallas as pl
from jax.experimental.pallas import tpu as pltpu
from jax.sharding import PartitionSpec as P

MESH = pl.DeviceIdType.MESH
time_step = 0.02
shear_jump = 0.5
AZ, RAD = 32, 8
NF, NX, NZ, NY = 8, 8, 16, 128
COLS = AZ * NY


def primitive_of(u):
    inv = 1.0 / u[0]
    v = [u[i] * inv for i in (1, 2, 3)]
    vv = v[0] * v[0] + v[1] * v[1] + v[2] * v[2]
    bb = u[5] * u[5] + u[6] * u[6] + u[7] * u[7]
    p = (2.0 / 3.0) * (u[4] - 0.5 * u[0] * vv - 0.5 * bb)
    return [u[0], v[0], v[1], v[2], p, u[5], u[6], u[7]]


def conserved_of(w):
    rho, v, p, b = w[0], w[1:4], w[4], w[5:8]
    vv = v[0] * v[0] + v[1] * v[1] + v[2] * v[2]
    bb = b[0] * b[0] + b[1] * b[1] + b[2] * b[2]
    return [rho] + [rho * c for c in v] + [1.5 * p + 0.5 * rho * vv + 0.5 * bb] + list(b)


def half_slope(a, b):
    return 0.5 * jnp.maximum(jnp.minimum(a, b), jnp.minimum(jnp.maximum(a, b), 0.0))


def state_of(w, n):
    rho, v, p, b = w[0], w[1:4], w[4], w[5:8]
    vn, bn = v[n], b[n]
    bb = b[0] * b[0] + b[1] * b[1] + b[2] * b[2]
    hb = 0.5 * bb
    vv = v[0] * v[0] + v[1] * v[1] + v[2] * v[2]
    vb = v[0] * b[0] + v[1] * b[1] + v[2] * b[2]
    pt = p + hb
    mom = [rho * c for c in v]
    en = 1.5 * p + 0.5 * rho * vv + hb
    fm = [mom[i] * vn - b[i] * bn for i in range(3)]
    fm[n] = fm[n] + pt
    fe = (en + pt) * vn - bn * vb
    fb = [None if i == n else b[i] * vn - v[i] * bn for i in range(3)]
    a = (5.0 / 3.0) * p + bb
    speed = jnp.abs(vn) + (a * lax.rsqrt(a)) * lax.rsqrt(rho)
    return [rho] + mom + [en] + list(b), [mom[n]] + fm + [fe] + fb, speed


def twice_flux(left, right, n):
    ul, fl, cl = state_of(left, n)
    ur, fr, cr = state_of(right, n)
    c = jnp.maximum(cl, cr)
    out = []
    for i in range(NF):
        diff = c * (ur[i] - ul[i])
        out.append(-diff if fl[i] is None else fl[i] + fr[i] - diff)
    return out


def rolled_faces(w, axis, n):
    size = w[0].shape[axis]
    left, right = [], []
    for f in range(NF):
        d = w[f] - pltpu.roll(w[f], 1, axis)
        h = half_slope(d, pltpu.roll(d, size - 1, axis))
        left.append(pltpu.roll(w[f] + h, 1, axis))
        right.append(w[f] - h)
    return twice_flux(left, right, n)


def ghosted_divergence(w, g, lane, n):
    size = w[0].shape[1]
    first, final = lane == 0, lane == size - 1
    left, right, left_g, right_g = [], [], [], []
    for f in range(NF):
        w_up, g_up = pltpu.roll(w[f], 1, 1), pltpu.roll(g[f], 1, 1)
        d = w[f] - jnp.where(first, g_up, w_up)
        d_g = g[f] - jnp.where(first, w_up, g_up)
        d_down, d_g_down = pltpu.roll(d, size - 1, 1), pltpu.roll(d_g, size - 1, 1)
        h = half_slope(d, jnp.where(final, d_g_down, d_down))
        h_g = half_slope(d_g, jnp.where(final, d_down, d_g_down))
        l_up = pltpu.roll(w[f] + h, 1, 1)
        left.append(jnp.where(first, pltpu.roll(g[f] + h_g, 1, 1), l_up))
        right.append(w[f] - h)
        left_g.append(l_up)
        right_g.append(g[f] - h_g)
    flux = twice_flux(left, right, n)
    flux_g = twice_flux(left_g, right_g, n)
    return [jnp.where(final, pltpu.roll(flux_g[f], size - 1, 1), pltpu.roll(flux[f], size - 1, 1)) - flux[f]
            for f in range(NF)]


def plane_of(z, x, core):
    s = z + x + core
    return 3 - (s - 3 * ((s * 11) >> 5))


def kernel(shift_hbm, u_hbm, out_ref, raw, w1, w2, acc, fx, tend, wt, ft, y_out, y_in, ghost, stage, relay_in,
           relay_roll, near_out, far_out, plane_out, far_in, plane_in, ext_rows, ext_flux, shift_ref, in_sem, shift_sem,
           x_send, x_recv, y_send, y_recv, a_send, a_recv, b_send, far_send, far_recv, plane_send, plane_recv):
    az = lax.axis_index("az")
    rad = lax.axis_index("rad")
    right, left = (az + 1) % AZ, (az + AZ - 1) % AZ
    edge = (rad == 0) | (rad == RAD - 1)
    my_z, my_x, my_core = az >> 3, (az >> 1) & 3, az & 1
    my_plane = plane_of(my_z, my_x, my_core)
    relay_lo = rad == 4 + my_plane
    relay_hi = rad == 3 - my_plane
    relay = relay_lo | relay_hi
    both = edge & relay

    barrier = pltpu.get_barrier_semaphore()

    def signal(*device):
        pl.semaphore_signal(barrier, 1, device_id=device, device_id_type=MESH)

    load = pltpu.make_async_copy(u_hbm, raw, in_sem)
    load.start()
    load_shift = pltpu.make_async_copy(shift_hbm, shift_ref, shift_sem)
    load_shift.start()

    z_list = [3 - my_z, (my_z + 2) & 3, my_z + 1 - 2 * (my_z & 1), my_z]
    x_list = [(my_x + 2) & 3, (my_x + 1) & 3, (my_x + 3) & 3, my_x]
    core_list = [1 - my_core, my_core]

    def peers(across):
        out = []
        for z in reversed(z_list) if across else z_list:
            for x in x_list:
                for core in core_list:
                    out.append((z * 8 + x * 2 + core, plane_of(z, x, core)))
        return out

    def others(body):
        everyone = peers(False)
        for p, plane in everyone[:-1]:
            body(p, plane)

        @pl.when(jnp.logical_not(both))
        def _():
            body(*everyone[-1])

    @pl.when(relay)
    def _():
        source = jnp.where(relay_lo, RAD - 1, 0)
        others(lambda p, plane: signal(p, source))

    signal(right, rad)
    signal(left, rad)

    @pl.when(rad > 0)
    def _():
        signal(az, rad - 1)

    @pl.when(rad < RAD - 1)
    def _():
        signal(az, rad + 1)

    @pl.when(edge)
    def _():
        signal(az, RAD - 1 - rad)

    lane = lax.broadcasted_iota(jnp.int32, (NZ, NY), 1)
    load.wait()
    u_rows = raw.reshape(NF * NZ * NX, NY)

    def conserved_row(x):
        return [u_rows[pl.ds(f * NZ * NX + x, NZ, NX), :] for f in range(NF)]

    def first_rows(x, carry):
        w = primitive_of(conserved_row(x))
        for f in range(NF):
            w1[f, x + 2] = w[f]
        return carry

    lax.fori_loop(0, NX, first_rows, 0)

    def turn_y(sec, w):
        for f in range(NF):
            wt[f, 8:8 + NY] = w[f, 2:2 + NX].reshape(NX * NZ, NY).T
        for f in range(NF):
            y_out[sec, 0, 2 * f:2 * f + 2] = wt[f, 8 + NY - 2:8 + NY]
            y_out[sec, 1, 2 * f:2 * f + 2] = wt[f, 8:10]

    @pl.when(edge)
    def _():
        near, far = jnp.where(rad == 0, 2, 8), jnp.where(rad == 0, 4, 6)
        for f in range(NF):
            for j in range(2):
                for t, base in ((0, near), (1, far)):
                    row = w1[f, base + j]
                    for half in range(2):
                        stage[t, f * 4 + j * 2 + half] = row[half * 8:half * 8 + 8]

    turn_y(0, w1)
    pl.semaphore_wait(barrier, jnp.where(edge, AZ + 4, 4) - jnp.where(both, 1, 0))

    def x_copy(sec, w, up):
        rows = w.at[:, pl.ds(8 if up else 2, 2)]
        side = 0 if up else 1
        return pltpu.make_async_remote_copy(
            rows, ghost.at[sec, side], x_send.at[sec, side], x_recv.at[sec, side],
            device_id=(az, rad + 1 if up else rad - 1), device_id_type=MESH)

    def y_copy(sec, up):
        side = 0 if up else 1
        return pltpu.make_async_remote_copy(
            y_out.at[sec, side], y_in.at[sec, side], y_send.at[sec, side], y_recv.at[sec, side],
            device_id=(right if up else left, rad), device_id_type=MESH)

    def scatter():
        @pl.when(edge)
        def _():
            base, sign = jnp.where(rad == 0, 3, 4), jnp.where(rad == 0, -1, 1)
            for t in range(2):
                def send(p, plane):
                    pltpu.make_async_remote_copy(
                        stage.at[t, p], relay_in.at[t, az], a_send.at[t], a_recv.at[t],
                        device_id=(p, base + sign * plane), device_id_type=MESH).start()

                others(send)

                @pl.when(both)
                def _():
                    pltpu.make_async_copy(stage.at[t, az], relay_in.at[t, az], a_recv.at[t]).start()

    def start_x(sec, w, side):
        @pl.when((side == 1) & (rad < RAD - 1))
        def _():
            x_copy(sec, w, True).start()

        @pl.when((side == 0) & (rad > 0))
        def _():
            x_copy(sec, w, False).start()

    def start_y(sec):
        y_copy(sec, True).start()
        y_copy(sec, False).start()

    def serve():
        @pl.when(relay)
        def _():
            def signed(s):
                return jnp.where(relay_lo, s, COLS - s) % COLS

            shift_0, shift_1 = signed(shift_ref[0]), signed(shift_ref[1])
            f, j, half = az >> 2, (az >> 1) & 1, az & 1
            rows = pl.ds(pl.multiple_of(half * 8, 8), 8)
            side = jnp.where(relay_lo, 0, 1)
            across = jnp.where(relay_lo, 0, RAD - 1)
            small = lax.broadcasted_iota(jnp.int32, (8, NY), 1)

            def arrived(t):
                pltpu.make_async_copy(relay_in.at[t], relay_in.at[t], a_recv.at[t]).wait()

            def turn(slots, tiles, amount):
                part = amount % NY

                for k in range(AZ):
                    for c, t in zip(slots, tiles):
                        relay_roll[c, k] = pltpu.roll(relay_in[t, k], (NY - part) % NY, 1)

            def pick(c, d, amount):
                whole, part = amount >> 7, amount & (NY - 1)
                return jnp.where(
                    small < NY - part, relay_roll[c, (d + whole) & (AZ - 1)], relay_roll[c, (d + whole + 1) & (AZ - 1)])

            arrived(0)
            turn((0,), (0,), shift_0)
            for d in range(AZ):
                near_out[d] = pick(0, d, shift_0)
            for d, _ in peers(True):
                pltpu.make_async_remote_copy(
                    near_out.at[d], ghost.at[0, side, f, j, rows], b_send, x_recv.at[0, side],
                    device_id=(d, across), device_id_type=MESH).start()

            turn((0,), (0,), shift_1)
            for d in range(AZ):
                far_out[d, 0:8] = pick(0, d, shift_1)
            sub = lax.broadcasted_iota(jnp.int32, (8, NY), 0)
            for d in range(AZ):
                ends = jnp.where(small < NY // 2, far_out[(d + 1) % AZ, 0:8], far_out[(d + AZ - 1) % AZ, 0:8])
                ends = jnp.where(small < 4, pltpu.roll(ends, 2, 1), 0.0)
                for width in (4, 8, 16):
                    ends = ends + pltpu.roll(ends, width, 1)
                ends = jnp.where(small >> 2 == 7 - sub, ends, 0.0)
                far_out[d, 16:17] = jnp.sum(ends, axis=0, keepdims=True)
            arrived(1)
            turn((1,), (1,), shift_1)
            for d in range(AZ):
                far_out[d, 8:16] = pick(1, d, shift_1)
            piece = far_in.at[az, pl.ds(0, 17)]
            for d, _ in peers(True):
                pltpu.make_async_remote_copy(
                    far_out.at[d, pl.ds(0, 17)], piece, far_send, far_recv,
                    device_id=(d, across), device_id_type=MESH).start()

            shift_2 = (shift_0 - shift_1 + COLS) % COLS
            turn((0,), (0,), shift_2)

            for d in range(AZ):
                plane_out[d] = pick(0, d, shift_2)

            def send(d, plane):
                pltpu.make_async_remote_copy(
                    plane_out.at[d], plane_in.at[f, j, rows], plane_send, plane_recv,
                    device_id=(d, RAD - 1 - across), device_id_type=MESH).start()

            others(send)

            @pl.when(both)
            def _():
                pltpu.make_async_copy(plane_out.at[az], plane_in.at[f, j, rows], plane_recv).start()

    def z_part(w):
        def row(x, carry):
            flux = rolled_faces([w[f, x + 2] for f in range(NF)], 0, 2)
            for f in range(NF):
                acc[f, x] = pltpu.roll(flux[f], NZ - 1, 0) - flux[f]
            return carry

        lax.fori_loop(0, NX, row, 0)

    def y_faces(k):
        lefts, rights = [], []
        for f in range(NF):
            c = [wt[f, pl.ds(8 * k + 6 + o, 8)] for o in range(4)]
            d = [c[o + 1] - c[o] for o in range(3)]
            lefts.append(c[1] + half_slope(d[0], d[1]))
            rights.append(c[2] - half_slope(d[1], d[2]))
        flux = twice_flux(lefts, rights, 1)
        for f in range(NF):
            ft[f, pl.ds(pl.multiple_of(8 * k, 8), 8)] = flux[f]

    def y_part():
        def pair(k, carry):
            y_faces(2 * k + 1)
            y_faces(2 * k + 2)
            return carry

        lax.fori_loop(0, 7, pair, 0)

    def x_faces(w, flux_ref, begin, end):
        def face(i, carry):
            lefts, rights = [], []
            for f in range(NF):
                c = [w[f, i + k] for k in range(4)]
                d = [c[k + 1] - c[k] for k in range(3)]
                lefts.append(c[1] + half_slope(d[0], d[1]))
                rights.append(c[2] - half_slope(d[1], d[2]))
            flux = twice_flux(lefts, rights, 0)
            for f in range(NF):
                flux_ref[f, i] = flux[f]
            return carry

        lax.fori_loop(begin, end, face, 0)

    def finish_y(sec):
        y_copy(sec, True).wait_recv()
        y_copy(sec, False).wait_recv()
        for f in range(NF):
            wt[f, 6:8] = y_in[sec, 0, 2 * f:2 * f + 2]
            wt[f, 8 + NY:10 + NY] = y_in[sec, 1, 2 * f:2 * f + 2]
        for k in (0, 15, 16):
            y_faces(k)
        for f in range(NF):
            part = (ft[f, 1:NY + 1] - ft[f, 0:NY]).T
            acc[f] += part.reshape(NX, NZ, NY)

    def receive_side(sec, w, side):
        pltpu.make_async_copy(ghost.at[sec, side], ghost.at[sec, side], x_recv.at[sec, side]).wait()
        kick = jnp.where((rad == 0) & (side == 0), shear_jump, 0.0) - jnp.where(
            (rad == RAD - 1) & (side == 1), shear_jump, 0.0)
        for f in range(NF):
            for j in range(2):
                value = ghost[sec, side, f, j]
                w[f, 10 * side + j] = value + kick if f == 2 else value

    def sheared_rows(w):
        pltpu.make_async_copy(plane_in, plane_in, plane_recv).wait()
        whole = far_in.at[:, pl.ds(0, 17)]
        pltpu.make_async_copy(whole, whole, far_recv).wait()
        far_at = jnp.where(rad == 0, 0, 4)
        plane_kick = jnp.where(rad == 0, -shear_jump, shear_jump)
        for f in range(NF):
            for j in range(2):
                at = f * 4 + j * 2
                ext_rows[f, 2 + j] = far_in[at:at + 2, 0:8].reshape(NZ, NY)
                ext_rows[f, far_at + j] = far_in[at:at + 2, 8:16].reshape(NZ, NY)
                value = plane_in[f, j]
                if f == 2:
                    value = value + plane_kick
                ext_rows[f, 4 - far_at + j] = value
        x_faces(ext_rows, ext_flux, 0, 3)

        at = jnp.where(rad == 0, 0, 10)
        for j in range(2):
            cells = [ext_rows[f, 2 + j] for f in range(NF)]
            flux = rolled_faces(cells, 0, 2)
            columns = []
            for f in range(NF):
                pair = [pltpu.roll(jnp.broadcast_to(far_in[f * 4 + j * 2 + half, 16:17], (8, NY)), NY - 30, 1,
                                   stride=4, stride_axis=0) for half in range(2)]
                columns.append(jnp.concatenate(pair, axis=0))
            part = ghosted_divergence(cells, columns, lane, 1)
            u = conserved_of(cells)
            for f in range(NF):
                total = pltpu.roll(flux[f], NZ - 1, 0) - flux[f] + part[f] + (ext_flux[f, j + 1] - ext_flux[f, j])
                u[f] = u[f] - (0.5 * time_step) * total
            mid = primitive_of(u)
            mid[2] = mid[2] - plane_kick
            for f in range(NF):
                w[f, at + j] = mid[f]

    def side_at(k):
        return (k + jnp.where(rad == 0, 1, 0)) % 2

    def side_faces(w, side):
        x_faces(w, fx, 7 * side, 7 * side + 2)

    def row_total(x):
        return [-0.5 * (acc[f, x] + (fx[f, x + 1] - fx[f, x])) for f in range(NF)]

    def middle(x, carry):
        total = row_total(x)
        u = conserved_row(x)
        w = primitive_of([u[f] + time_step * total[f] for f in range(NF)])
        for f in range(NF):
            tend[f, x] = total[f]
            w2[f, x + 2] = w[f]
        return carry

    out_rows = out_ref.reshape(NF * NZ * NX, NY)

    def last(x, carry):
        total = row_total(x)
        for f in range(NF):
            out_rows[pl.ds(f * NZ * NX + x, NZ, NX), :] = 0.5 * (tend[f, x] + total[f])
        return carry

    def bulk(w):
        z_part(w)
        y_part()
        x_faces(w, fx, 2, 7)

    start_y(0)
    scatter()
    bulk(w1)
    finish_y(0)
    lax.fori_loop(2, 6, middle, 0)
    start_x(0, w1, 0)
    start_x(0, w1, 1)
    load_shift.wait()
    serve()

    def first_side(k, carry):
        side = side_at(k)
        receive_side(0, w1, side)
        side_faces(w1, side)
        lax.fori_loop(6 * side, 6 * side + 2, middle, 0)
        start_x(1, w2, side)
        return carry

    lax.fori_loop(0, 2, first_side, 0)
    turn_y(1, w2)
    start_y(1)
    bulk(w2)

    def second_side(k, carry):
        side = side_at(k)
        sheared = edge & (k == 1)

        @pl.when(sheared)
        def _():
            sheared_rows(w2)

        @pl.when(jnp.logical_not(sheared))
        def _():
            receive_side(1, w2, side)

        side_faces(w2, side)
        return carry

    lax.fori_loop(0, 2, second_side, 0)
    finish_y(1)
    lax.fori_loop(0, NX, last, 0)

    for sec, w in ((0, w1), (1, w2)):
        y_copy(sec, True).wait_send()
        y_copy(sec, False).wait_send()

        @pl.when(rad < RAD - 1)
        def _():
            x_copy(sec, w, True).wait_send()

        @pl.when(rad > 0)
        def _():
            x_copy(sec, w, False).wait_send()

    @pl.when(edge)
    def _():
        for t in range(2):
            most = stage.at[t, pl.ds(0, AZ - 1)]
            pltpu.make_async_copy(most, most, a_send.at[t]).wait()

            @pl.when(jnp.logical_not(relay))
            def _():
                pltpu.make_async_copy(stage.at[t, 0], stage.at[t, 0], a_send.at[t]).wait()

    @pl.when(relay)
    def _():
        pltpu.make_async_copy(near_out, near_out, b_send).wait()
        sent = far_out.at[:, pl.ds(0, 17)]
        pltpu.make_async_copy(sent, sent, far_send).wait()
        most = plane_out.at[pl.ds(0, AZ - 1)]
        pltpu.make_async_copy(most, most, plane_send).wait()

        @pl.when(jnp.logical_not(edge))
        def _():
            pltpu.make_async_copy(plane_out.at[0], plane_out.at[0], plane_send).wait()


def shards(conserved, shear_shift):
    f32 = jnp.float32
    return pl.pallas_call(
        kernel,
        out_shape=jax.ShapeDtypeStruct((NF, NZ, NX, NY), f32),
        in_specs=[pl.BlockSpec(memory_space=pltpu.HBM), pl.BlockSpec(memory_space=pltpu.HBM)],
        out_specs=pl.BlockSpec(memory_space=pltpu.VMEM),
        scratch_shapes=[
            pltpu.VMEM((NF, NZ, NX, NY), f32),
            pltpu.VMEM((NF, NX + 4, NZ, NY), f32),
            pltpu.VMEM((NF, NX + 4, NZ, NY), f32),
            pltpu.VMEM((NF, NX, NZ, NY), f32),
            pltpu.VMEM((NF, NX + 1, NZ, NY), f32),
            pltpu.VMEM((NF, NX, NZ, NY), f32),
            pltpu.VMEM((NF, NY + 24, NX * NZ), f32),
            pltpu.VMEM((NF, NY + 8, NX * NZ), f32),
            pltpu.VMEM((2, 2, 2 * NF, NX * NZ), f32),
            pltpu.VMEM((2, 2, 2 * NF, NX * NZ), f32),
            pltpu.VMEM((2, 2, NF, 2, NZ, NY), f32),
            pltpu.VMEM((2, AZ, 8, NY), f32),
            pltpu.VMEM((2, AZ, 8, NY), f32),
            pltpu.VMEM((2, AZ, 8, NY), f32),
            pltpu.VMEM((AZ, 8, NY), f32),
            pltpu.VMEM((AZ, 24, NY), f32),
            pltpu.VMEM((AZ, 8, NY), f32),
            pltpu.VMEM((AZ, 24, NY), f32),
            pltpu.VMEM((NF, 2, NZ, NY), f32),
            pltpu.VMEM((NF, 6, NZ, NY), f32),
            pltpu.VMEM((NF, 3, NZ, NY), f32),
            pltpu.SMEM((2,), jnp.int32),
            pltpu.SemaphoreType.DMA,
            pltpu.SemaphoreType.DMA,
            pltpu.SemaphoreType.DMA((2, 2)),
            pltpu.SemaphoreType.DMA((2, 2)),
            pltpu.SemaphoreType.DMA((2, 2)),
            pltpu.SemaphoreType.DMA((2, 2)),
            pltpu.SemaphoreType.DMA((2,)),
            pltpu.SemaphoreType.DMA((2,)),
            pltpu.SemaphoreType.DMA,
            pltpu.SemaphoreType.DMA,
            pltpu.SemaphoreType.DMA,
            pltpu.SemaphoreType.DMA,
            pltpu.SemaphoreType.DMA,
        ],
        name="mhd_step",
        compiler_params=pltpu.CompilerParams(
            collective_id=0, has_side_effects=True, vmem_limit_bytes=53 * 1024 * 1024),
    )(shear_shift, conserved)


def solution(mesh):
    return jax.shard_map(
        shards,
        mesh=mesh,
        in_specs=(P(None, None, "rad", "az"), P()),
        out_specs=P(None, None, "rad", "az"),
        check_vma=False,
    )
```

```python
import functools

import jax
import jax.numpy as jnp
from jax import lax
from jax.experimental import pallas as pl
from jax.experimental.pallas import tpu as pltpu
from jax.sharding import PartitionSpec as P

MESH = pl.DeviceIdType.MESH
time_step = 0.02
shear_jump = 0.5
AZ, RAD = 32, 8
NF, NX, NZ, NY = 8, 8, 16, 128
COLS = AZ * NY


def primitive_of(u):
    inv = 1.0 / u[0]
    v = [u[i] * inv for i in (1, 2, 3)]
    vv = v[0] * v[0] + v[1] * v[1] + v[2] * v[2]
    bb = u[5] * u[5] + u[6] * u[6] + u[7] * u[7]
    p = (2.0 / 3.0) * (u[4] - 0.5 * u[0] * vv - 0.5 * bb)
    return [u[0], v[0], v[1], v[2], p, u[5], u[6], u[7]]


def conserved_of(w):
    rho, v, p, b = w[0], w[1:4], w[4], w[5:8]
    vv = v[0] * v[0] + v[1] * v[1] + v[2] * v[2]
    bb = b[0] * b[0] + b[1] * b[1] + b[2] * b[2]
    return [rho] + [rho * c for c in v] + [1.5 * p + 0.5 * rho * vv + 0.5 * bb] + list(b)


def half_slope(a, b):
    return 0.5 * jnp.maximum(jnp.minimum(a, b), jnp.minimum(jnp.maximum(a, b), 0.0))


def state_of(w, n):
    rho, v, p, b = w[0], w[1:4], w[4], w[5:8]
    vn, bn = v[n], b[n]
    bb = b[0] * b[0] + b[1] * b[1] + b[2] * b[2]
    hb = 0.5 * bb
    vv = v[0] * v[0] + v[1] * v[1] + v[2] * v[2]
    vb = v[0] * b[0] + v[1] * b[1] + v[2] * b[2]
    pt = p + hb
    mom = [rho * c for c in v]
    en = 1.5 * p + 0.5 * rho * vv + hb
    fm = [mom[i] * vn - b[i] * bn for i in range(3)]
    fm[n] = fm[n] + pt
    fe = (en + pt) * vn - bn * vb
    fb = [None if i == n else b[i] * vn - v[i] * bn for i in range(3)]
    a = (5.0 / 3.0) * p + bb
    speed = jnp.abs(vn) + (a * lax.rsqrt(a)) * lax.rsqrt(rho)
    return [rho] + mom + [en] + list(b), [mom[n]] + fm + [fe] + fb, speed


def twice_flux(left, right, n):
    ul, fl, cl = state_of(left, n)
    ur, fr, cr = state_of(right, n)
    c = jnp.maximum(cl, cr)
    out = []
    for i in range(NF):
        diff = c * (ur[i] - ul[i])
        out.append(-diff if fl[i] is None else fl[i] + fr[i] - diff)
    return out


def rolled_faces(w, axis, n):
    size = w[0].shape[axis]
    left, right = [], []
    for f in range(NF):
        d = w[f] - pltpu.roll(w[f], 1, axis)
        h = half_slope(d, pltpu.roll(d, size - 1, axis))
        left.append(pltpu.roll(w[f] + h, 1, axis))
        right.append(w[f] - h)
    return twice_flux(left, right, n)


def ghosted_divergence(w, g, lane, n):
    size = w[0].shape[1]
    first, final = lane == 0, lane == size - 1
    left, right, left_g, right_g = [], [], [], []
    for f in range(NF):
        w_up, g_up = pltpu.roll(w[f], 1, 1), pltpu.roll(g[f], 1, 1)
        d = w[f] - jnp.where(first, g_up, w_up)
        d_g = g[f] - jnp.where(first, w_up, g_up)
        d_down, d_g_down = pltpu.roll(d, size - 1, 1), pltpu.roll(d_g, size - 1, 1)
        h = half_slope(d, jnp.where(final, d_g_down, d_down))
        h_g = half_slope(d_g, jnp.where(final, d_down, d_g_down))
        l_up = pltpu.roll(w[f] + h, 1, 1)
        left.append(jnp.where(first, pltpu.roll(g[f] + h_g, 1, 1), l_up))
        right.append(w[f] - h)
        left_g.append(l_up)
        right_g.append(g[f] - h_g)
    flux = twice_flux(left, right, n)
    flux_g = twice_flux(left_g, right_g, n)
    return [jnp.where(final, pltpu.roll(flux_g[f], size - 1, 1), pltpu.roll(flux[f], size - 1, 1)) - flux[f]
            for f in range(NF)]


def plane_of(z, x, core):
    s = z + x + core
    return 3 - (s - 3 * ((s * 11) >> 5))


def kernel(shift_hbm, u_hbm, out_ref, raw, w1, w2, acc, fx, tend, wt, ft, y_out, y_in, ghost, stage, relay_in,
           relay_roll, near_out, far_out, plane_out, far_in, plane_in, ext_rows, ext_flux, shift_ref, in_sem, shift_sem,
           x_send, x_recv, y_send, y_recv, a_send, a_recv, b_send, far_send, far_recv, plane_send, plane_recv):
    az = lax.axis_index("az")
    rad = lax.axis_index("rad")
    right, left = (az + 1) % AZ, (az + AZ - 1) % AZ
    edge = (rad == 0) | (rad == RAD - 1)
    my_z, my_x, my_core = az >> 3, (az >> 1) & 3, az & 1
    my_plane = plane_of(my_z, my_x, my_core)
    relay_lo = rad == 4 + my_plane
    relay_hi = rad == 3 - my_plane
    relay = relay_lo | relay_hi
    both = edge & relay

    barrier = pltpu.get_barrier_semaphore()

    def signal(*device):
        pl.semaphore_signal(barrier, 1, device_id=device, device_id_type=MESH)

    load = pltpu.make_async_copy(u_hbm, raw, in_sem)
    load.start()
    load_shift = pltpu.make_async_copy(shift_hbm, shift_ref, shift_sem)
    load_shift.start()

    z_list = [3 - my_z, (my_z + 2) & 3, my_z + 1 - 2 * (my_z & 1), my_z]
    x_list = [(my_x + 2) & 3, (my_x + 1) & 3, (my_x + 3) & 3, my_x]
    core_list = [1 - my_core, my_core]

    def peers(across):
        out = []
        for z in range(4) if across else z_list:
            for x in x_list:
                for core in core_list:
                    out.append((z * 8 + x * 2 + core, plane_of(z, x, core)))
        return out

    def others(body):
        everyone = peers(False)
        for p, plane in everyone[:-1]:
            body(p, plane)

        @pl.when(jnp.logical_not(both))
        def _():
            body(*everyone[-1])

    @pl.when(relay)
    def _():
        source = jnp.where(relay_lo, RAD - 1, 0)
        others(lambda p, plane: signal(p, source))

    signal(right, rad)
    signal(left, rad)

    @pl.when(rad > 0)
    def _():
        signal(az, rad - 1)

    @pl.when(rad < RAD - 1)
    def _():
        signal(az, rad + 1)

    @pl.when(edge)
    def _():
        signal(az, RAD - 1 - rad)

    lane = lax.broadcasted_iota(jnp.int32, (NZ, NY), 1)
    load.wait()
    u_rows = raw.reshape(NF * NZ * NX, NY)

    def conserved_row(x):
        return [u_rows[pl.ds(f * NZ * NX + x, NZ, NX), :] for f in range(NF)]

    def first_rows(x, carry):
        w = primitive_of(conserved_row(x))
        for f in range(NF):
            w1[f, x + 2] = w[f]
        return carry

    lax.fori_loop(0, NX, first_rows, 0)

    def turn_y(sec, w):
        for f in range(NF):
            wt[f, 8:8 + NY] = w[f, 2:2 + NX].reshape(NX * NZ, NY).T
        for f in range(NF):
            y_out[sec, 0, 2 * f:2 * f + 2] = wt[f, 8 + NY - 2:8 + NY]
            y_out[sec, 1, 2 * f:2 * f + 2] = wt[f, 8:10]

    @pl.when(edge)
    def _():
        near, far = jnp.where(rad == 0, 2, 8), jnp.where(rad == 0, 4, 6)
        for f in range(NF):
            for j in range(2):
                for t, base in ((0, near), (1, far)):
                    row = w1[f, base + j]
                    for half in range(2):
                        stage[t, f * 4 + j * 2 + half] = row[half * 8:half * 8 + 8]

    turn_y(0, w1)
    pl.semaphore_wait(barrier, jnp.where(edge, AZ + 4, 4) - jnp.where(both, 1, 0))

    def x_copy(sec, w, up):
        rows = w.at[:, pl.ds(8 if up else 2, 2)]
        side = 0 if up else 1
        return pltpu.make_async_remote_copy(
            rows, ghost.at[sec, side], x_send.at[sec, side], x_recv.at[sec, side],
            device_id=(az, rad + 1 if up else rad - 1), device_id_type=MESH)

    def y_copy(sec, up):
        side = 0 if up else 1
        return pltpu.make_async_remote_copy(
            y_out.at[sec, side], y_in.at[sec, side], y_send.at[sec, side], y_recv.at[sec, side],
            device_id=(right if up else left, rad), device_id_type=MESH)

    def scatter():
        @pl.when(edge)
        def _():
            base, sign = jnp.where(rad == 0, 3, 4), jnp.where(rad == 0, -1, 1)
            for t in range(2):
                def send(p, plane):
                    pltpu.make_async_remote_copy(
                        stage.at[t, p], relay_in.at[t, az], a_send.at[t], a_recv.at[t],
                        device_id=(p, base + sign * plane), device_id_type=MESH).start()

                others(send)

                @pl.when(both)
                def _():
                    pltpu.make_async_copy(stage.at[t, az], relay_in.at[t, az], a_recv.at[t]).start()

    def start_x(sec, w, side):
        @pl.when((side == 1) & (rad < RAD - 1))
        def _():
            x_copy(sec, w, True).start()

        @pl.when((side == 0) & (rad > 0))
        def _():
            x_copy(sec, w, False).start()

    def start_y(sec):
        y_copy(sec, True).start()
        y_copy(sec, False).start()

    def serve():
        @pl.when(relay)
        def _():
            def signed(s):
                return jnp.where(relay_lo, s, COLS - s) % COLS

            shift_0, shift_1 = signed(shift_ref[0]), signed(shift_ref[1])
            f, j, half = az >> 2, (az >> 1) & 1, az & 1
            rows = pl.ds(pl.multiple_of(half * 8, 8), 8)
            side = jnp.where(relay_lo, 0, 1)
            across = jnp.where(relay_lo, 0, RAD - 1)
            small = lax.broadcasted_iota(jnp.int32, (8, NY), 1)

            def arrived(t):
                pltpu.make_async_copy(relay_in.at[t], relay_in.at[t], a_recv.at[t]).wait()

            def turn(slots, tiles, amount):
                part = amount % NY

                for k in range(AZ):
                    for c, t in zip(slots, tiles):
                        relay_roll[c, k] = pltpu.roll(relay_in[t, k], (NY - part) % NY, 1)

            def pick(c, d, amount):
                whole, part = amount >> 7, amount & (NY - 1)
                return jnp.where(
                    small < NY - part, relay_roll[c, (d + whole) & (AZ - 1)], relay_roll[c, (d + whole + 1) & (AZ - 1)])

            arrived(0)
            turn((0,), (0,), shift_0)
            for d in range(AZ):
                near_out[d] = pick(0, d, shift_0)
            for d, _ in peers(True):
                pltpu.make_async_remote_copy(
                    near_out.at[d], ghost.at[0, side, f, j, rows], b_send, x_recv.at[0, side],
                    device_id=(d, across), device_id_type=MESH).start()

            turn((0,), (0,), shift_1)
            for d in range(AZ):
                far_out[d, 0:8] = pick(0, d, shift_1)
            sub = lax.broadcasted_iota(jnp.int32, (8, NY), 0)
            for d in range(AZ):
                ends = jnp.where(small < NY // 2, far_out[(d + 1) % AZ, 0:8], far_out[(d + AZ - 1) % AZ, 0:8])
                ends = jnp.where(small < 4, pltpu.roll(ends, 2, 1), 0.0)
                for width in (4, 8, 16):
                    ends = ends + pltpu.roll(ends, width, 1)
                ends = jnp.where(small >> 2 == 7 - sub, ends, 0.0)
                far_out[d, 16:17] = jnp.sum(ends, axis=0, keepdims=True)
            arrived(1)
            turn((1,), (1,), shift_1)
            for d in range(AZ):
                far_out[d, 8:16] = pick(1, d, shift_1)
            piece = far_in.at[az, pl.ds(0, 17)]
            for d, _ in peers(True):
                pltpu.make_async_remote_copy(
                    far_out.at[d, pl.ds(0, 17)], piece, far_send, far_recv,
                    device_id=(d, across), device_id_type=MESH).start()

            shift_2 = (shift_0 - shift_1 + COLS) % COLS
            turn((0,), (0,), shift_2)

            for d in range(AZ):
                plane_out[d] = pick(0, d, shift_2)

            def send(d, plane):
                pltpu.make_async_remote_copy(
                    plane_out.at[d], plane_in.at[f, j, rows], plane_send, plane_recv,
                    device_id=(d, RAD - 1 - across), device_id_type=MESH).start()

            others(send)

            @pl.when(both)
            def _():
                pltpu.make_async_copy(plane_out.at[az], plane_in.at[f, j, rows], plane_recv).start()

    def z_part(w):
        def row(x, carry):
            flux = rolled_faces([w[f, x + 2] for f in range(NF)], 0, 2)
            for f in range(NF):
                acc[f, x] = pltpu.roll(flux[f], NZ - 1, 0) - flux[f]
            return carry

        lax.fori_loop(0, NX, row, 0)

    def y_faces(k):
        lefts, rights = [], []
        for f in range(NF):
            c = [wt[f, pl.ds(8 * k + 6 + o, 8)] for o in range(4)]
            d = [c[o + 1] - c[o] for o in range(3)]
            lefts.append(c[1] + half_slope(d[0], d[1]))
            rights.append(c[2] - half_slope(d[1], d[2]))
        flux = twice_flux(lefts, rights, 1)
        for f in range(NF):
            ft[f, pl.ds(pl.multiple_of(8 * k, 8), 8)] = flux[f]

    def y_part():
        def pair(k, carry):
            y_faces(2 * k + 1)
            y_faces(2 * k + 2)
            return carry

        lax.fori_loop(0, 7, pair, 0)

    def x_faces(w, flux_ref, begin, end):
        def face(i, carry):
            lefts, rights = [], []
            for f in range(NF):
                c = [w[f, i + k] for k in range(4)]
                d = [c[k + 1] - c[k] for k in range(3)]
                lefts.append(c[1] + half_slope(d[0], d[1]))
                rights.append(c[2] - half_slope(d[1], d[2]))
            flux = twice_flux(lefts, rights, 0)
            for f in range(NF):
                flux_ref[f, i] = flux[f]
            return carry

        lax.fori_loop(begin, end, face, 0)

    def finish_y(sec):
        y_copy(sec, True).wait_recv()
        y_copy(sec, False).wait_recv()
        for f in range(NF):
            wt[f, 6:8] = y_in[sec, 0, 2 * f:2 * f + 2]
            wt[f, 8 + NY:10 + NY] = y_in[sec, 1, 2 * f:2 * f + 2]
        for k in (0, 15, 16):
            y_faces(k)
        for f in range(NF):
            part = (ft[f, 1:NY + 1] - ft[f, 0:NY]).T
            acc[f] += part.reshape(NX, NZ, NY)

    def receive_side(sec, w, side):
        pltpu.make_async_copy(ghost.at[sec, side], ghost.at[sec, side], x_recv.at[sec, side]).wait()
        kick = jnp.where((rad == 0) & (side == 0), shear_jump, 0.0) - jnp.where(
            (rad == RAD - 1) & (side == 1), shear_jump, 0.0)
        for f in range(NF):
            for j in range(2):
                value = ghost[sec, side, f, j]
                w[f, 10 * side + j] = value + kick if f == 2 else value

    def sheared_rows(w):
        pltpu.make_async_copy(plane_in, plane_in, plane_recv).wait()
        whole = far_in.at[:, pl.ds(0, 17)]
        pltpu.make_async_copy(whole, whole, far_recv).wait()
        far_at = jnp.where(rad == 0, 0, 4)
        plane_kick = jnp.where(rad == 0, -shear_jump, shear_jump)
        for f in range(NF):
            for j in range(2):
                at = f * 4 + j * 2
                ext_rows[f, 2 + j] = far_in[at:at + 2, 0:8].reshape(NZ, NY)
                ext_rows[f, far_at + j] = far_in[at:at + 2, 8:16].reshape(NZ, NY)
                value = plane_in[f, j]
                if f == 2:
                    value = value + plane_kick
                ext_rows[f, 4 - far_at + j] = value
        x_faces(ext_rows, ext_flux, 0, 3)

        at = jnp.where(rad == 0, 0, 10)
        for j in range(2):
            cells = [ext_rows[f, 2 + j] for f in range(NF)]
            flux = rolled_faces(cells, 0, 2)
            columns = []
            for f in range(NF):
                pair = [pltpu.roll(jnp.broadcast_to(far_in[f * 4 + j * 2 + half, 16:17], (8, NY)), NY - 30, 1,
                                   stride=4, stride_axis=0) for half in range(2)]
                columns.append(jnp.concatenate(pair, axis=0))
            part = ghosted_divergence(cells, columns, lane, 1)
            u = conserved_of(cells)
            for f in range(NF):
                total = pltpu.roll(flux[f], NZ - 1, 0) - flux[f] + part[f] + (ext_flux[f, j + 1] - ext_flux[f, j])
                u[f] = u[f] - (0.5 * time_step) * total
            mid = primitive_of(u)
            mid[2] = mid[2] - plane_kick
            for f in range(NF):
                w[f, at + j] = mid[f]

    def side_at(k):
        return (k + jnp.where(rad == 0, 1, 0)) % 2

    def side_faces(w, side):
        x_faces(w, fx, 7 * side, 7 * side + 2)

    def row_total(x):
        return [-0.5 * (acc[f, x] + (fx[f, x + 1] - fx[f, x])) for f in range(NF)]

    def middle(x, carry):
        total = row_total(x)
        u = conserved_row(x)
        w = primitive_of([u[f] + time_step * total[f] for f in range(NF)])
        for f in range(NF):
            tend[f, x] = total[f]
            w2[f, x + 2] = w[f]
        return carry

    out_rows = out_ref.reshape(NF * NZ * NX, NY)

    def last(x, carry):
        total = row_total(x)
        for f in range(NF):
            out_rows[pl.ds(f * NZ * NX + x, NZ, NX), :] = 0.5 * (tend[f, x] + total[f])
        return carry

    def bulk(w):
        z_part(w)
        y_part()
        x_faces(w, fx, 2, 7)

    start_y(0)
    scatter()
    bulk(w1)
    finish_y(0)
    lax.fori_loop(2, 6, middle, 0)
    start_x(0, w1, 0)
    start_x(0, w1, 1)
    load_shift.wait()
    serve()

    def first_side(k, carry):
        side = side_at(k)
        receive_side(0, w1, side)
        side_faces(w1, side)
        lax.fori_loop(6 * side, 6 * side + 2, middle, 0)
        start_x(1, w2, side)
        return carry

    lax.fori_loop(0, 2, first_side, 0)
    turn_y(1, w2)
    start_y(1)
    bulk(w2)

    def second_side(k, carry):
        side = side_at(k)
        sheared = edge & (k == 1)

        @pl.when(sheared)
        def _():
            sheared_rows(w2)

        @pl.when(jnp.logical_not(sheared))
        def _():
            receive_side(1, w2, side)

        side_faces(w2, side)
        return carry

    lax.fori_loop(0, 2, second_side, 0)
    finish_y(1)
    lax.fori_loop(0, NX, last, 0)

    for sec, w in ((0, w1), (1, w2)):
        y_copy(sec, True).wait_send()
        y_copy(sec, False).wait_send()

        @pl.when(rad < RAD - 1)
        def _():
            x_copy(sec, w, True).wait_send()

        @pl.when(rad > 0)
        def _():
            x_copy(sec, w, False).wait_send()

    @pl.when(edge)
    def _():
        for t in range(2):
            most = stage.at[t, pl.ds(0, AZ - 1)]
            pltpu.make_async_copy(most, most, a_send.at[t]).wait()

            @pl.when(jnp.logical_not(relay))
            def _():
                pltpu.make_async_copy(stage.at[t, 0], stage.at[t, 0], a_send.at[t]).wait()

    @pl.when(relay)
    def _():
        pltpu.make_async_copy(near_out, near_out, b_send).wait()
        sent = far_out.at[:, pl.ds(0, 17)]
        pltpu.make_async_copy(sent, sent, far_send).wait()
        most = plane_out.at[pl.ds(0, AZ - 1)]
        pltpu.make_async_copy(most, most, plane_send).wait()

        @pl.when(jnp.logical_not(edge))
        def _():
            pltpu.make_async_copy(plane_out.at[0], plane_out.at[0], plane_send).wait()


def shards(conserved, shear_shift):
    f32 = jnp.float32
    return pl.pallas_call(
        kernel,
        out_shape=jax.ShapeDtypeStruct((NF, NZ, NX, NY), f32),
        in_specs=[pl.BlockSpec(memory_space=pltpu.HBM), pl.BlockSpec(memory_space=pltpu.HBM)],
        out_specs=pl.BlockSpec(memory_space=pltpu.VMEM),
        scratch_shapes=[
            pltpu.VMEM((NF, NZ, NX, NY), f32),
            pltpu.VMEM((NF, NX + 4, NZ, NY), f32),
            pltpu.VMEM((NF, NX + 4, NZ, NY), f32),
            pltpu.VMEM((NF, NX, NZ, NY), f32),
            pltpu.VMEM((NF, NX + 1, NZ, NY), f32),
            pltpu.VMEM((NF, NX, NZ, NY), f32),
            pltpu.VMEM((NF, NY + 24, NX * NZ), f32),
            pltpu.VMEM((NF, NY + 8, NX * NZ), f32),
            pltpu.VMEM((2, 2, 2 * NF, NX * NZ), f32),
            pltpu.VMEM((2, 2, 2 * NF, NX * NZ), f32),
            pltpu.VMEM((2, 2, NF, 2, NZ, NY), f32),
            pltpu.VMEM((2, AZ, 8, NY), f32),
            pltpu.VMEM((2, AZ, 8, NY), f32),
            pltpu.VMEM((2, AZ, 8, NY), f32),
            pltpu.VMEM((AZ, 8, NY), f32),
            pltpu.VMEM((AZ, 24, NY), f32),
            pltpu.VMEM((AZ, 8, NY), f32),
            pltpu.VMEM((AZ, 24, NY), f32),
            pltpu.VMEM((NF, 2, NZ, NY), f32),
            pltpu.VMEM((NF, 6, NZ, NY), f32),
            pltpu.VMEM((NF, 3, NZ, NY), f32),
            pltpu.SMEM((2,), jnp.int32),
            pltpu.SemaphoreType.DMA,
            pltpu.SemaphoreType.DMA,
            pltpu.SemaphoreType.DMA((2, 2)),
            pltpu.SemaphoreType.DMA((2, 2)),
            pltpu.SemaphoreType.DMA((2, 2)),
            pltpu.SemaphoreType.DMA((2, 2)),
            pltpu.SemaphoreType.DMA((2,)),
            pltpu.SemaphoreType.DMA((2,)),
            pltpu.SemaphoreType.DMA,
            pltpu.SemaphoreType.DMA,
            pltpu.SemaphoreType.DMA,
            pltpu.SemaphoreType.DMA,
            pltpu.SemaphoreType.DMA,
        ],
        name="mhd_step",
        compiler_params=pltpu.CompilerParams(
            collective_id=0, has_side_effects=True, vmem_limit_bytes=53 * 1024 * 1024),
    )(pltpu.with_memory_space_constraint(shear_shift, pltpu.HBM),
      pltpu.with_memory_space_constraint(conserved, pltpu.HBM))


def solution(mesh):
    return jax.shard_map(
        shards,
        mesh=mesh,
        in_specs=(P(None, None, "rad", "az"), P()),
        out_specs=P(None, None, "rad", "az"),
        check_vma=False,
    )
```

```python
import functools

import jax
import jax.numpy as jnp
from jax import lax
from jax.experimental import pallas as pl
from jax.experimental.pallas import tpu as pltpu
from jax.sharding import PartitionSpec as P

MESH = pl.DeviceIdType.MESH
time_step = 0.02
shear_jump = 0.5
AZ, RAD = 32, 8
NF, NX, NZ, NY = 8, 8, 16, 128
COLS = AZ * NY


def primitive_of(u):
    inv = 1.0 / u[0]
    v = [u[i] * inv for i in (1, 2, 3)]
    vv = v[0] * v[0] + v[1] * v[1] + v[2] * v[2]
    bb = u[5] * u[5] + u[6] * u[6] + u[7] * u[7]
    p = (2.0 / 3.0) * (u[4] - 0.5 * u[0] * vv - 0.5 * bb)
    return [u[0], v[0], v[1], v[2], p, u[5], u[6], u[7]]


def conserved_of(w):
    rho, v, p, b = w[0], w[1:4], w[4], w[5:8]
    vv = v[0] * v[0] + v[1] * v[1] + v[2] * v[2]
    bb = b[0] * b[0] + b[1] * b[1] + b[2] * b[2]
    return [rho] + [rho * c for c in v] + [1.5 * p + 0.5 * rho * vv + 0.5 * bb] + list(b)


def half_slope(a, b):
    return 0.5 * jnp.maximum(jnp.minimum(a, b), jnp.minimum(jnp.maximum(a, b), 0.0))


def state_of(w, n):
    rho, v, p, b = w[0], w[1:4], w[4], w[5:8]
    vn, bn = v[n], b[n]
    bb = b[0] * b[0] + b[1] * b[1] + b[2] * b[2]
    hb = 0.5 * bb
    vv = v[0] * v[0] + v[1] * v[1] + v[2] * v[2]
    vb = v[0] * b[0] + v[1] * b[1] + v[2] * b[2]
    pt = p + hb
    mom = [rho * c for c in v]
    en = 1.5 * p + 0.5 * rho * vv + hb
    fm = [mom[i] * vn - b[i] * bn for i in range(3)]
    fm[n] = fm[n] + pt
    fe = (en + pt) * vn - bn * vb
    fb = [None if i == n else b[i] * vn - v[i] * bn for i in range(3)]
    a = (5.0 / 3.0) * p + bb
    speed = jnp.abs(vn) + (a * lax.rsqrt(a)) * lax.rsqrt(rho)
    return [rho] + mom + [en] + list(b), [mom[n]] + fm + [fe] + fb, speed


def twice_flux(left, right, n):
    ul, fl, cl = state_of(left, n)
    ur, fr, cr = state_of(right, n)
    c = jnp.maximum(cl, cr)
    out = []
    for i in range(NF):
        diff = c * (ur[i] - ul[i])
        out.append(-diff if fl[i] is None else fl[i] + fr[i] - diff)
    return out


def rolled_faces(w, axis, n):
    size = w[0].shape[axis]
    left, right = [], []
    for f in range(NF):
        d = w[f] - pltpu.roll(w[f], 1, axis)
        h = half_slope(d, pltpu.roll(d, size - 1, axis))
        left.append(pltpu.roll(w[f] + h, 1, axis))
        right.append(w[f] - h)
    return twice_flux(left, right, n)


def ghosted_divergence(w, g, lane, n):
    size = w[0].shape[1]
    first, final = lane == 0, lane == size - 1
    left, right, left_g, right_g = [], [], [], []
    for f in range(NF):
        w_up, g_up = pltpu.roll(w[f], 1, 1), pltpu.roll(g[f], 1, 1)
        d = w[f] - jnp.where(first, g_up, w_up)
        d_g = g[f] - jnp.where(first, w_up, g_up)
        d_down, d_g_down = pltpu.roll(d, size - 1, 1), pltpu.roll(d_g, size - 1, 1)
        h = half_slope(d, jnp.where(final, d_g_down, d_down))
        h_g = half_slope(d_g, jnp.where(final, d_down, d_g_down))
        l_up = pltpu.roll(w[f] + h, 1, 1)
        left.append(jnp.where(first, pltpu.roll(g[f] + h_g, 1, 1), l_up))
        right.append(w[f] - h)
        left_g.append(l_up)
        right_g.append(g[f] - h_g)
    flux = twice_flux(left, right, n)
    flux_g = twice_flux(left_g, right_g, n)
    return [jnp.where(final, pltpu.roll(flux_g[f], size - 1, 1), pltpu.roll(flux[f], size - 1, 1)) - flux[f]
            for f in range(NF)]


def plane_of(z, x, core):
    s = z + x + core
    return 3 - (s - 3 * ((s * 11) >> 5))


def kernel(shift_hbm, u_hbm, out_ref, raw, w1, w2, acc, fx, tend, wt, ft, y_out, y_in, ghost, stage, relay_in,
           relay_roll, near_out, far_out, plane_out, far_in, plane_in, ext_rows, ext_flux, ext_part, shift_ref, in_sem, shift_sem,
           x_send, x_recv, y_send, y_recv, a_send, a_recv, b_send, far_send, far_recv, plane_send, plane_recv):
    az = lax.axis_index("az")
    rad = lax.axis_index("rad")
    right, left = (az + 1) % AZ, (az + AZ - 1) % AZ
    edge = (rad == 0) | (rad == RAD - 1)
    my_z, my_x, my_core = az >> 3, (az >> 1) & 3, az & 1
    my_plane = plane_of(my_z, my_x, my_core)
    relay_lo = rad == 4 + my_plane
    relay_hi = rad == 3 - my_plane
    relay = relay_lo | relay_hi
    both = edge & relay

    barrier = pltpu.get_barrier_semaphore()

    def signal(*device):
        pl.semaphore_signal(barrier, 1, device_id=device, device_id_type=MESH)

    load = pltpu.make_async_copy(u_hbm, raw, in_sem)
    load.start()
    load_shift = pltpu.make_async_copy(shift_hbm, shift_ref, shift_sem)
    load_shift.start()

    z_list = [3 - my_z, (my_z + 2) & 3, my_z + 1 - 2 * (my_z & 1), my_z]
    x_list = [(my_x + 2) & 3, (my_x + 1) & 3, (my_x + 3) & 3, my_x]
    core_list = [1 - my_core, my_core]

    def peers(across):
        out = []
        for z in range(4) if across else z_list:
            for x in x_list:
                for core in core_list:
                    out.append((z * 8 + x * 2 + core, plane_of(z, x, core)))
        return out

    def others(body):
        everyone = peers(False)
        for p, plane in everyone[:-1]:
            body(p, plane)

        @pl.when(jnp.logical_not(both))
        def _():
            body(*everyone[-1])

    @pl.when(relay)
    def _():
        source = jnp.where(relay_lo, RAD - 1, 0)
        others(lambda p, plane: signal(p, source))

    signal(right, rad)
    signal(left, rad)

    @pl.when(rad > 0)
    def _():
        signal(az, rad - 1)

    @pl.when(rad < RAD - 1)
    def _():
        signal(az, rad + 1)

    @pl.when(edge)
    def _():
        signal(az, RAD - 1 - rad)

    lane = lax.broadcasted_iota(jnp.int32, (NZ, NY), 1)
    load.wait()
    u_rows = raw.reshape(NF * NZ * NX, NY)

    def conserved_row(x):
        return [u_rows[pl.ds(f * NZ * NX + x, NZ, NX), :] for f in range(NF)]

    def first_rows(x, carry):
        w = primitive_of(conserved_row(x))
        for f in range(NF):
            w1[f, x + 2] = w[f]
        return carry

    lax.fori_loop(0, NX, first_rows, 0)

    def turn_y(sec, w):
        for f in range(NF):
            wt[f, 8:8 + NY] = w[f, 2:2 + NX].reshape(NX * NZ, NY).T
        for f in range(NF):
            y_out[sec, 0, 2 * f:2 * f + 2] = wt[f, 8 + NY - 2:8 + NY]
            y_out[sec, 1, 2 * f:2 * f + 2] = wt[f, 8:10]

    @pl.when(edge)
    def _():
        near, far = jnp.where(rad == 0, 2, 8), jnp.where(rad == 0, 4, 6)
        for f in range(NF):
            for j in range(2):
                for t, base in ((0, near), (1, far)):
                    row = w1[f, base + j]
                    for half in range(2):
                        stage[t, f * 4 + j * 2 + half] = row[half * 8:half * 8 + 8]

    turn_y(0, w1)
    pl.semaphore_wait(barrier, jnp.where(edge, AZ + 4, 4) - jnp.where(both, 1, 0))

    def x_copy(sec, w, up):
        rows = w.at[:, pl.ds(8 if up else 2, 2)]
        side = 0 if up else 1
        return pltpu.make_async_remote_copy(
            rows, ghost.at[sec, side], x_send.at[sec, side], x_recv.at[sec, side],
            device_id=(az, rad + 1 if up else rad - 1), device_id_type=MESH)

    def y_copy(sec, up):
        side = 0 if up else 1
        return pltpu.make_async_remote_copy(
            y_out.at[sec, side], y_in.at[sec, side], y_send.at[sec, side], y_recv.at[sec, side],
            device_id=(right if up else left, rad), device_id_type=MESH)

    def scatter():
        @pl.when(edge)
        def _():
            base, sign = jnp.where(rad == 0, 3, 4), jnp.where(rad == 0, -1, 1)
            for t in range(2):
                def send(p, plane):
                    pltpu.make_async_remote_copy(
                        stage.at[t, p], relay_in.at[t, az], a_send.at[t], a_recv.at[t],
                        device_id=(p, base + sign * plane), device_id_type=MESH).start()

                others(send)

                @pl.when(both)
                def _():
                    pltpu.make_async_copy(stage.at[t, az], relay_in.at[t, az], a_recv.at[t]).start()

    def start_x(sec, w, side):
        @pl.when((side == 1) & (rad < RAD - 1))
        def _():
            x_copy(sec, w, True).start()

        @pl.when((side == 0) & (rad > 0))
        def _():
            x_copy(sec, w, False).start()

    def start_y(sec):
        y_copy(sec, True).start()
        y_copy(sec, False).start()

    def serve():
        @pl.when(relay)
        def _():
            def signed(s):
                return jnp.where(relay_lo, s, COLS - s) % COLS

            shift_0, shift_1 = signed(shift_ref[0]), signed(shift_ref[1])
            f, j, half = az >> 2, (az >> 1) & 1, az & 1
            rows = pl.ds(pl.multiple_of(half * 8, 8), 8)
            side = jnp.where(relay_lo, 0, 1)
            across = jnp.where(relay_lo, 0, RAD - 1)
            small = lax.broadcasted_iota(jnp.int32, (8, NY), 1)

            def arrived(t):
                pltpu.make_async_copy(relay_in.at[t], relay_in.at[t], a_recv.at[t]).wait()

            def turn(slots, tiles, amount):
                part = amount % NY

                for k in range(AZ):
                    for c, t in zip(slots, tiles):
                        relay_roll[c, k] = pltpu.roll(relay_in[t, k], (NY - part) % NY, 1)

            def pick(c, d, amount):
                whole, part = amount >> 7, amount & (NY - 1)
                return jnp.where(
                    small < NY - part, relay_roll[c, (d + whole) & (AZ - 1)], relay_roll[c, (d + whole + 1) & (AZ - 1)])

            arrived(0)
            turn((0,), (0,), shift_0)
            for d in range(AZ):
                near_out[d] = pick(0, d, shift_0)
            for d, _ in peers(True):
                pltpu.make_async_remote_copy(
                    near_out.at[d], ghost.at[0, side, f, j, rows], b_send, x_recv.at[0, side],
                    device_id=(d, across), device_id_type=MESH).start()

            turn((0,), (0,), shift_1)
            for d in range(AZ):
                far_out[d, 0:8] = pick(0, d, shift_1)
            sub = lax.broadcasted_iota(jnp.int32, (8, NY), 0)
            for d in range(AZ):
                ends = jnp.where(small < NY // 2, far_out[(d + 1) % AZ, 0:8], far_out[(d + AZ - 1) % AZ, 0:8])
                ends = jnp.where(small < 4, pltpu.roll(ends, 2, 1), 0.0)
                for width in (4, 8, 16):
                    ends = ends + pltpu.roll(ends, width, 1)
                ends = jnp.where(small >> 2 == 7 - sub, ends, 0.0)
                far_out[d, 8:9] = jnp.sum(ends, axis=0, keepdims=True)

            def answer(begin, rows, t):
                for d, _ in peers(True):
                    pltpu.make_async_remote_copy(
                        far_out.at[d, pl.ds(begin, rows)], far_in.at[az, pl.ds(begin, rows)],
                        far_send.at[t], far_recv.at[t], device_id=(d, across), device_id_type=MESH).start()

            answer(0, 9, 0)
            arrived(1)
            turn((1,), (1,), shift_1)
            for d in range(AZ):
                far_out[d, 16:24] = pick(1, d, shift_1)
            answer(16, 8, 1)
            shift_2 = (shift_0 - shift_1 + COLS) % COLS
            turn((0,), (0,), shift_2)

            for d in range(AZ):
                plane_out[d] = pick(0, d, shift_2)

            def send(d, plane):
                pltpu.make_async_remote_copy(
                    plane_out.at[d], plane_in.at[f, j, rows], plane_send, plane_recv,
                    device_id=(d, RAD - 1 - across), device_id_type=MESH).start()

            others(send)

            @pl.when(both)
            def _():
                pltpu.make_async_copy(plane_out.at[az], plane_in.at[f, j, rows], plane_recv).start()

    def z_part(w):
        def row(x, carry):
            flux = rolled_faces([w[f, x + 2] for f in range(NF)], 0, 2)
            for f in range(NF):
                acc[f, x] = pltpu.roll(flux[f], NZ - 1, 0) - flux[f]
            return carry

        lax.fori_loop(0, NX, row, 0)

    def y_faces(k):
        lefts, rights = [], []
        for f in range(NF):
            c = [wt[f, pl.ds(8 * k + 6 + o, 8)] for o in range(4)]
            d = [c[o + 1] - c[o] for o in range(3)]
            lefts.append(c[1] + half_slope(d[0], d[1]))
            rights.append(c[2] - half_slope(d[1], d[2]))
        flux = twice_flux(lefts, rights, 1)
        for f in range(NF):
            ft[f, pl.ds(pl.multiple_of(8 * k, 8), 8)] = flux[f]

    def y_part():
        def pair(k, carry):
            y_faces(2 * k + 1)
            y_faces(2 * k + 2)
            return carry

        lax.fori_loop(0, 7, pair, 0)

    def x_faces(w, flux_ref, begin, end):
        def face(i, carry):
            lefts, rights = [], []
            for f in range(NF):
                c = [w[f, i + k] for k in range(4)]
                d = [c[k + 1] - c[k] for k in range(3)]
                lefts.append(c[1] + half_slope(d[0], d[1]))
                rights.append(c[2] - half_slope(d[1], d[2]))
            flux = twice_flux(lefts, rights, 0)
            for f in range(NF):
                flux_ref[f, i] = flux[f]
            return carry

        lax.fori_loop(begin, end, face, 0)

    def finish_y(sec):
        y_copy(sec, True).wait_recv()
        y_copy(sec, False).wait_recv()
        for f in range(NF):
            wt[f, 6:8] = y_in[sec, 0, 2 * f:2 * f + 2]
            wt[f, 8 + NY:10 + NY] = y_in[sec, 1, 2 * f:2 * f + 2]
        for k in (0, 15, 16):
            y_faces(k)
        for f in range(NF):
            part = (ft[f, 1:NY + 1] - ft[f, 0:NY]).T
            acc[f] += part.reshape(NX, NZ, NY)

    def receive_side(sec, w, side):
        pltpu.make_async_copy(ghost.at[sec, side], ghost.at[sec, side], x_recv.at[sec, side]).wait()
        kick = jnp.where((rad == 0) & (side == 0), shear_jump, 0.0) - jnp.where(
            (rad == RAD - 1) & (side == 1), shear_jump, 0.0)
        for f in range(NF):
            for j in range(2):
                value = ghost[sec, side, f, j]
                w[f, 10 * side + j] = value + kick if f == 2 else value

    def sheared_near():
        near = far_in.at[:, pl.ds(0, 9)]
        pltpu.make_async_copy(near, near, far_recv.at[0]).wait()
        for j in range(2):
            cells, columns = [], []
            for f in range(NF):
                at = f * 4 + j * 2
                cells.append(far_in[at:at + 2, 0:8].reshape(NZ, NY))
                pair = [pltpu.roll(jnp.broadcast_to(far_in[at + half, 8:9], (8, NY)), NY - 30, 1,
                                   stride=4, stride_axis=0) for half in range(2)]
                columns.append(jnp.concatenate(pair, axis=0))
                ext_rows[f, 2 + j] = cells[f]
            flux = rolled_faces(cells, 0, 2)
            part = ghosted_divergence(cells, columns, lane, 1)
            for f in range(NF):
                ext_part[f, j] = pltpu.roll(flux[f], NZ - 1, 0) - flux[f] + part[f]

    def sheared_rows(w):
        pltpu.make_async_copy(plane_in, plane_in, plane_recv).wait()
        far = far_in.at[:, pl.ds(16, 8)]
        pltpu.make_async_copy(far, far, far_recv.at[1]).wait()
        far_at = jnp.where(rad == 0, 0, 4)
        plane_kick = jnp.where(rad == 0, -shear_jump, shear_jump)
        for f in range(NF):
            for j in range(2):
                at = f * 4 + j * 2
                ext_rows[f, far_at + j] = far_in[at:at + 2, 16:24].reshape(NZ, NY)
                value = plane_in[f, j]
                if f == 2:
                    value = value + plane_kick
                ext_rows[f, 4 - far_at + j] = value
        x_faces(ext_rows, ext_flux, 0, 3)
        at = jnp.where(rad == 0, 0, 10)
        for j in range(2):
            u = conserved_of([ext_rows[f, 2 + j] for f in range(NF)])
            for f in range(NF):
                total = ext_part[f, j] + (ext_flux[f, j + 1] - ext_flux[f, j])
                u[f] = u[f] - (0.5 * time_step) * total
            mid = primitive_of(u)
            mid[2] = mid[2] - plane_kick
            for f in range(NF):
                w[f, at + j] = mid[f]

    def side_at(k):
        return (k + jnp.where(rad == 0, 1, 0)) % 2

    def side_faces(w, side):
        x_faces(w, fx, 7 * side, 7 * side + 2)

    def row_total(x):
        return [-0.5 * (acc[f, x] + (fx[f, x + 1] - fx[f, x])) for f in range(NF)]

    def middle(x, carry):
        total = row_total(x)
        u = conserved_row(x)
        w = primitive_of([u[f] + time_step * total[f] for f in range(NF)])
        for f in range(NF):
            tend[f, x] = total[f]
            w2[f, x + 2] = w[f]
        return carry

    out_rows = out_ref.reshape(NF * NZ * NX, NY)

    def last(x, carry):
        total = row_total(x)
        for f in range(NF):
            out_rows[pl.ds(f * NZ * NX + x, NZ, NX), :] = 0.5 * (tend[f, x] + total[f])
        return carry

    def bulk(w):
        z_part(w)
        y_part()
        x_faces(w, fx, 2, 7)

    start_y(0)
    scatter()
    bulk(w1)
    finish_y(0)
    lax.fori_loop(2, 6, middle, 0)
    start_x(0, w1, 0)
    start_x(0, w1, 1)
    load_shift.wait()
    serve()

    def first_side(k, carry):
        side = side_at(k)
        receive_side(0, w1, side)
        side_faces(w1, side)
        lax.fori_loop(6 * side, 6 * side + 2, middle, 0)
        start_x(1, w2, side)
        return carry

    lax.fori_loop(0, 2, first_side, 0)
    turn_y(1, w2)
    start_y(1)
    bulk(w2)

    def second_side(k, carry):
        side = side_at(k)
        sheared = edge & (k == 1)

        @pl.when(sheared)
        def _():
            sheared_near()
            sheared_rows(w2)

        @pl.when(jnp.logical_not(sheared))
        def _():
            receive_side(1, w2, side)

        side_faces(w2, side)
        return carry

    lax.fori_loop(0, 2, second_side, 0)
    finish_y(1)
    lax.fori_loop(0, NX, last, 0)

    for sec, w in ((0, w1), (1, w2)):
        y_copy(sec, True).wait_send()
        y_copy(sec, False).wait_send()

        @pl.when(rad < RAD - 1)
        def _():
            x_copy(sec, w, True).wait_send()

        @pl.when(rad > 0)
        def _():
            x_copy(sec, w, False).wait_send()

    @pl.when(edge)
    def _():
        for t in range(2):
            most = stage.at[t, pl.ds(0, AZ - 1)]
            pltpu.make_async_copy(most, most, a_send.at[t]).wait()

            @pl.when(jnp.logical_not(relay))
            def _():
                pltpu.make_async_copy(stage.at[t, 0], stage.at[t, 0], a_send.at[t]).wait()

    @pl.when(relay)
    def _():
        pltpu.make_async_copy(near_out, near_out, b_send).wait()
        for t, begin, rows in ((0, 0, 9), (1, 16, 8)):
            sent = far_out.at[:, pl.ds(begin, rows)]
            pltpu.make_async_copy(sent, sent, far_send.at[t]).wait()
        most = plane_out.at[pl.ds(0, AZ - 1)]
        pltpu.make_async_copy(most, most, plane_send).wait()

        @pl.when(jnp.logical_not(edge))
        def _():
            pltpu.make_async_copy(plane_out.at[0], plane_out.at[0], plane_send).wait()


def shards(conserved, shear_shift):
    f32 = jnp.float32
    return pl.pallas_call(
        kernel,
        out_shape=jax.ShapeDtypeStruct((NF, NZ, NX, NY), f32),
        in_specs=[pl.BlockSpec(memory_space=pltpu.HBM), pl.BlockSpec(memory_space=pltpu.HBM)],
        out_specs=pl.BlockSpec(memory_space=pltpu.VMEM),
        scratch_shapes=[
            pltpu.VMEM((NF, NZ, NX, NY), f32),
            pltpu.VMEM((NF, NX + 4, NZ, NY), f32),
            pltpu.VMEM((NF, NX + 4, NZ, NY), f32),
            pltpu.VMEM((NF, NX, NZ, NY), f32),
            pltpu.VMEM((NF, NX + 1, NZ, NY), f32),
            pltpu.VMEM((NF, NX, NZ, NY), f32),
            pltpu.VMEM((NF, NY + 24, NX * NZ), f32),
            pltpu.VMEM((NF, NY + 8, NX * NZ), f32),
            pltpu.VMEM((2, 2, 2 * NF, NX * NZ), f32),
            pltpu.VMEM((2, 2, 2 * NF, NX * NZ), f32),
            pltpu.VMEM((2, 2, NF, 2, NZ, NY), f32),
            pltpu.VMEM((2, AZ, 8, NY), f32),
            pltpu.VMEM((2, AZ, 8, NY), f32),
            pltpu.VMEM((2, AZ, 8, NY), f32),
            pltpu.VMEM((AZ, 8, NY), f32),
            pltpu.VMEM((AZ, 24, NY), f32),
            pltpu.VMEM((AZ, 8, NY), f32),
            pltpu.VMEM((AZ, 24, NY), f32),
            pltpu.VMEM((NF, 2, NZ, NY), f32),
            pltpu.VMEM((NF, 6, NZ, NY), f32),
            pltpu.VMEM((NF, 3, NZ, NY), f32),
            pltpu.VMEM((NF, 2, NZ, NY), f32),
            pltpu.SMEM((2,), jnp.int32),
            pltpu.SemaphoreType.DMA,
            pltpu.SemaphoreType.DMA,
            pltpu.SemaphoreType.DMA((2, 2)),
            pltpu.SemaphoreType.DMA((2, 2)),
            pltpu.SemaphoreType.DMA((2, 2)),
            pltpu.SemaphoreType.DMA((2, 2)),
            pltpu.SemaphoreType.DMA((2,)),
            pltpu.SemaphoreType.DMA((2,)),
            pltpu.SemaphoreType.DMA,
            pltpu.SemaphoreType.DMA((2,)),
            pltpu.SemaphoreType.DMA((2,)),
            pltpu.SemaphoreType.DMA,
            pltpu.SemaphoreType.DMA,
        ],
        name="mhd_step",
        compiler_params=pltpu.CompilerParams(
            collective_id=0, has_side_effects=True, vmem_limit_bytes=53 * 1024 * 1024),
    )(pltpu.with_memory_space_constraint(shear_shift, pltpu.HBM),
      pltpu.with_memory_space_constraint(conserved, pltpu.HBM))


def solution(mesh):
    return jax.shard_map(
        shards,
        mesh=mesh,
        in_specs=(P(None, None, "rad", "az"), P()),
        out_specs=P(None, None, "rad", "az"),
        check_vma=False,
    )
```

```python
import functools

import jax
import jax.numpy as jnp
from jax import lax
from jax.experimental import pallas as pl
from jax.experimental.pallas import tpu as pltpu
from jax.sharding import PartitionSpec as P

MESH = pl.DeviceIdType.MESH
time_step = 0.02
shear_jump = 0.5
AZ, RAD = 32, 8
NF, NX, NZ, NY = 8, 8, 16, 128
COLS = AZ * NY


def primitive_of(u):
    inv = 1.0 / u[0]
    v = [u[i] * inv for i in (1, 2, 3)]
    vv = v[0] * v[0] + v[1] * v[1] + v[2] * v[2]
    bb = u[5] * u[5] + u[6] * u[6] + u[7] * u[7]
    p = (2.0 / 3.0) * (u[4] - 0.5 * u[0] * vv - 0.5 * bb)
    return [u[0], v[0], v[1], v[2], p, u[5], u[6], u[7]]


def conserved_of(w):
    rho, v, p, b = w[0], w[1:4], w[4], w[5:8]
    vv = v[0] * v[0] + v[1] * v[1] + v[2] * v[2]
    bb = b[0] * b[0] + b[1] * b[1] + b[2] * b[2]
    return [rho] + [rho * c for c in v] + [1.5 * p + 0.5 * rho * vv + 0.5 * bb] + list(b)


def half_slope(a, b):
    return 0.5 * jnp.maximum(jnp.minimum(a, b), jnp.minimum(jnp.maximum(a, b), 0.0))


def state_of(w, n):
    rho, v, p, b = w[0], w[1:4], w[4], w[5:8]
    vn, bn = v[n], b[n]
    bb = b[0] * b[0] + b[1] * b[1] + b[2] * b[2]
    hb = 0.5 * bb
    vv = v[0] * v[0] + v[1] * v[1] + v[2] * v[2]
    vb = v[0] * b[0] + v[1] * b[1] + v[2] * b[2]
    pt = p + hb
    mom = [rho * c for c in v]
    en = 1.5 * p + 0.5 * rho * vv + hb
    fm = [mom[i] * vn - b[i] * bn for i in range(3)]
    fm[n] = fm[n] + pt
    fe = (en + pt) * vn - bn * vb
    fb = [None if i == n else b[i] * vn - v[i] * bn for i in range(3)]
    a = (5.0 / 3.0) * p + bb
    speed = jnp.abs(vn) + (a * lax.rsqrt(a)) * lax.rsqrt(rho)
    return [rho] + mom + [en] + list(b), [mom[n]] + fm + [fe] + fb, speed


def twice_flux(left, right, n):
    ul, fl, cl = state_of(left, n)
    ur, fr, cr = state_of(right, n)
    c = jnp.maximum(cl, cr)
    out = []
    for i in range(NF):
        diff = c * (ur[i] - ul[i])
        out.append(-diff if fl[i] is None else fl[i] + fr[i] - diff)
    return out


def rolled_faces(w, axis, n):
    size = w[0].shape[axis]
    left, right = [], []
    for f in range(NF):
        d = w[f] - pltpu.roll(w[f], 1, axis)
        h = half_slope(d, pltpu.roll(d, size - 1, axis))
        left.append(pltpu.roll(w[f] + h, 1, axis))
        right.append(w[f] - h)
    return twice_flux(left, right, n)


def ghosted_divergence(w, g, lane, n):
    size = w[0].shape[1]
    first, final = lane == 0, lane == size - 1
    left, right, left_g, right_g = [], [], [], []
    for f in range(NF):
        w_up, g_up = pltpu.roll(w[f], 1, 1), pltpu.roll(g[f], 1, 1)
        d = w[f] - jnp.where(first, g_up, w_up)
        d_g = g[f] - jnp.where(first, w_up, g_up)
        d_down, d_g_down = pltpu.roll(d, size - 1, 1), pltpu.roll(d_g, size - 1, 1)
        h = half_slope(d, jnp.where(final, d_g_down, d_down))
        h_g = half_slope(d_g, jnp.where(final, d_down, d_g_down))
        l_up = pltpu.roll(w[f] + h, 1, 1)
        left.append(jnp.where(first, pltpu.roll(g[f] + h_g, 1, 1), l_up))
        right.append(w[f] - h)
        left_g.append(l_up)
        right_g.append(g[f] - h_g)
    flux = twice_flux(left, right, n)
    flux_g = twice_flux(left_g, right_g, n)
    return [jnp.where(final, pltpu.roll(flux_g[f], size - 1, 1), pltpu.roll(flux[f], size - 1, 1)) - flux[f]
            for f in range(NF)]


def plane_of(z, x, core):
    s = z + x + core
    return 3 - (s - 3 * ((s * 11) >> 5))


def kernel(shift_hbm, u_hbm, out_ref, raw, w1, w2, acc, fx, tend, wt, ft, y_out, y_in, ghost, stage, relay_in,
           relay_roll, near_out, far_out, plane_out, far_in, plane_in, ext_rows, ext_flux, ext_part, shift_ref, in_sem, shift_sem,
           x_send, x_recv, y_send, y_recv, a_send, a_recv, b_send, far_send, far_recv, plane_send, plane_recv):
    az = lax.axis_index("az")
    rad = lax.axis_index("rad")
    right, left = (az + 1) % AZ, (az + AZ - 1) % AZ
    edge = (rad == 0) | (rad == RAD - 1)
    my_z, my_x, my_core = az >> 3, (az >> 1) & 3, az & 1
    my_plane = plane_of(my_z, my_x, my_core)
    relay_lo = rad == 4 + my_plane
    relay_hi = rad == 3 - my_plane
    relay = relay_lo | relay_hi
    both = edge & relay

    barrier = pltpu.get_barrier_semaphore()

    def signal(*device):
        pl.semaphore_signal(barrier, 1, device_id=device, device_id_type=MESH)

    load = pltpu.make_async_copy(u_hbm, raw, in_sem)
    load.start()
    load_shift = pltpu.make_async_copy(shift_hbm, shift_ref, shift_sem)
    load_shift.start()

    z_list = [3 - my_z, (my_z + 2) & 3, my_z + 1 - 2 * (my_z & 1), my_z]
    x_list = [(my_x + 2) & 3, (my_x + 1) & 3, (my_x + 3) & 3, my_x]
    core_list = [1 - my_core, my_core]

    def peers(across):
        out = []
        for z in range(4) if across else z_list:
            for x in x_list:
                for core in core_list:
                    out.append((z * 8 + x * 2 + core, plane_of(z, x, core)))
        return out

    def others(body):
        everyone = peers(False)
        for p, plane in everyone[:-1]:
            body(p, plane)

        @pl.when(jnp.logical_not(both))
        def _():
            body(*everyone[-1])

    @pl.when(relay)
    def _():
        source = jnp.where(relay_lo, RAD - 1, 0)
        others(lambda p, plane: signal(p, source))

    signal(right, rad)
    signal(left, rad)

    @pl.when(rad > 0)
    def _():
        signal(az, rad - 1)

    @pl.when(rad < RAD - 1)
    def _():
        signal(az, rad + 1)

    @pl.when(edge)
    def _():
        signal(az, RAD - 1 - rad)

    lane = lax.broadcasted_iota(jnp.int32, (NZ, NY), 1)
    load.wait()
    u_rows = raw.reshape(NF * NZ * NX, NY)

    def conserved_row(x):
        return [u_rows[pl.ds(f * NZ * NX + x, NZ, NX), :] for f in range(NF)]

    def first_rows(x, carry):
        w = primitive_of(conserved_row(x))
        for f in range(NF):
            w1[f, x + 2] = w[f]
        return carry

    lax.fori_loop(0, NX, first_rows, 0)

    def turn_y(sec, w):
        for f in range(NF):
            wt[f, 8:8 + NY] = w[f, 2:2 + NX].reshape(NX * NZ, NY).T
        for f in range(NF):
            y_out[sec, 0, 2 * f:2 * f + 2] = wt[f, 8 + NY - 2:8 + NY]
            y_out[sec, 1, 2 * f:2 * f + 2] = wt[f, 8:10]

    @pl.when(edge)
    def _():
        near, far = jnp.where(rad == 0, 2, 8), jnp.where(rad == 0, 4, 6)
        for f in range(NF):
            for j in range(2):
                for t, base in ((0, near), (1, far)):
                    row = w1[f, base + j]
                    for half in range(2):
                        stage[t, f * 4 + j * 2 + half] = row[half * 8:half * 8 + 8]

    turn_y(0, w1)
    pl.semaphore_wait(barrier, jnp.where(edge, AZ + 4, 4) - jnp.where(both, 1, 0))

    def x_copy(sec, w, up):
        rows = w.at[:, pl.ds(8 if up else 2, 2)]
        side = 0 if up else 1
        return pltpu.make_async_remote_copy(
            rows, ghost.at[sec, side], x_send.at[sec, side], x_recv.at[sec, side],
            device_id=(az, rad + 1 if up else rad - 1), device_id_type=MESH)

    def y_copy(sec, up):
        side = 0 if up else 1
        return pltpu.make_async_remote_copy(
            y_out.at[sec, side], y_in.at[sec, side], y_send.at[sec, side], y_recv.at[sec, side],
            device_id=(right if up else left, rad), device_id_type=MESH)

    def scatter():
        @pl.when(edge)
        def _():
            base, sign = jnp.where(rad == 0, 3, 4), jnp.where(rad == 0, -1, 1)
            for t in range(2):
                def send(p, plane):
                    pltpu.make_async_remote_copy(
                        stage.at[t, p], relay_in.at[t, az], a_send.at[t], a_recv.at[t],
                        device_id=(p, base + sign * plane), device_id_type=MESH).start()

                others(send)

                @pl.when(both)
                def _():
                    pltpu.make_async_copy(stage.at[t, az], relay_in.at[t, az], a_recv.at[t]).start()

    def start_x(sec, w, side):
        @pl.when((side == 1) & (rad < RAD - 1))
        def _():
            x_copy(sec, w, True).start()

        @pl.when((side == 0) & (rad > 0))
        def _():
            x_copy(sec, w, False).start()

    def start_y(sec):
        y_copy(sec, True).start()
        y_copy(sec, False).start()

    def serve():
        @pl.when(relay)
        def _():
            def signed(s):
                return jnp.where(relay_lo, s, COLS - s) % COLS

            shift_0, shift_1 = signed(shift_ref[0]), signed(shift_ref[1])
            f, j, half = az >> 2, (az >> 1) & 1, az & 1
            rows = pl.ds(pl.multiple_of(half * 8, 8), 8)
            side = jnp.where(relay_lo, 0, 1)
            across = jnp.where(relay_lo, 0, RAD - 1)
            small = lax.broadcasted_iota(jnp.int32, (8, NY), 1)

            def arrived(t):
                pltpu.make_async_copy(relay_in.at[t], relay_in.at[t], a_recv.at[t]).wait()

            def turn(slots, tiles, amount):
                part = amount % NY

                for k in range(AZ):
                    for c, t in zip(slots, tiles):
                        relay_roll[c, k] = pltpu.roll(relay_in[t, k], (NY - part) % NY, 1)

            def pick(c, d, amount):
                whole, part = amount >> 7, amount & (NY - 1)
                return jnp.where(
                    small < NY - part, relay_roll[c, (d + whole) & (AZ - 1)], relay_roll[c, (d + whole + 1) & (AZ - 1)])

            arrived(0)
            turn((0,), (0,), shift_0)
            for d in range(AZ):
                near_out[d] = pick(0, d, shift_0)
            for d, _ in peers(True):
                pltpu.make_async_remote_copy(
                    near_out.at[d], ghost.at[0, side, f, j, rows], b_send, x_recv.at[0, side],
                    device_id=(d, across), device_id_type=MESH).start()

            turn((0,), (0,), shift_1)
            for d in range(AZ):
                far_out[d, 0:8] = pick(0, d, shift_1)
            sub = lax.broadcasted_iota(jnp.int32, (8, NY), 0)
            for d in range(AZ):
                ends = jnp.where(small < NY // 2, far_out[(d + 1) % AZ, 0:8], far_out[(d + AZ - 1) % AZ, 0:8])
                ends = jnp.where(small < 4, pltpu.roll(ends, 2, 1), 0.0)
                for width in (4, 8, 16):
                    ends = ends + pltpu.roll(ends, width, 1)
                ends = jnp.where(small >> 2 == 7 - sub, ends, 0.0)
                far_out[d, 8:9] = jnp.sum(ends, axis=0, keepdims=True)

            def answer(begin, rows, t):
                for d, _ in peers(True):
                    pltpu.make_async_remote_copy(
                        far_out.at[d, pl.ds(begin, rows)], far_in.at[az, pl.ds(begin, rows)],
                        far_send.at[t], far_recv.at[t], device_id=(d, across), device_id_type=MESH).start()

            answer(0, 9, 0)
            arrived(1)
            turn((1,), (1,), shift_1)
            for d in range(AZ):
                far_out[d, 16:24] = pick(1, d, shift_1)
            answer(16, 8, 1)
            shift_2 = (shift_0 - shift_1 + COLS) % COLS
            turn((0,), (0,), shift_2)

            for d in range(AZ):
                plane_out[d] = pick(0, d, shift_2)

            def send(d, plane):
                pltpu.make_async_remote_copy(
                    plane_out.at[d], plane_in.at[f, j, rows], plane_send, plane_recv,
                    device_id=(d, RAD - 1 - across), device_id_type=MESH).start()

            others(send)

            @pl.when(both)
            def _():
                pltpu.make_async_copy(plane_out.at[az], plane_in.at[f, j, rows], plane_recv).start()

    def z_row(w, x):
        flux = rolled_faces([w[f, x + 2] for f in range(NF)], 0, 2)
        for f in range(NF):
            acc[f, x] = pltpu.roll(flux[f], NZ - 1, 0) - flux[f]

    def z_first(x, carry):
        z_row(w1, x)
        return carry

    def y_faces(k):
        lefts, rights = [], []
        for f in range(NF):
            c = [wt[f, pl.ds(8 * k + 6 + o, 8)] for o in range(4)]
            d = [c[o + 1] - c[o] for o in range(3)]
            lefts.append(c[1] + half_slope(d[0], d[1]))
            rights.append(c[2] - half_slope(d[1], d[2]))
        flux = twice_flux(lefts, rights, 1)
        for f in range(NF):
            ft[f, pl.ds(pl.multiple_of(8 * k, 8), 8)] = flux[f]

    def y_part():
        def pair(k, carry):
            y_faces(2 * k + 1)
            y_faces(2 * k + 2)
            return carry

        lax.fori_loop(0, 7, pair, 0)

    def x_faces(w, flux_ref, begin, end):
        def face(i, carry):
            lefts, rights = [], []
            for f in range(NF):
                c = [w[f, i + k] for k in range(4)]
                d = [c[k + 1] - c[k] for k in range(3)]
                lefts.append(c[1] + half_slope(d[0], d[1]))
                rights.append(c[2] - half_slope(d[1], d[2]))
            flux = twice_flux(lefts, rights, 0)
            for f in range(NF):
                flux_ref[f, i] = flux[f]
            return carry

        lax.fori_loop(begin, end, face, 0)

    def finish_y(sec):
        y_copy(sec, True).wait_recv()
        y_copy(sec, False).wait_recv()
        for f in range(NF):
            wt[f, 6:8] = y_in[sec, 0, 2 * f:2 * f + 2]
            wt[f, 8 + NY:10 + NY] = y_in[sec, 1, 2 * f:2 * f + 2]
        for k in (0, 15, 16):
            y_faces(k)
        for f in range(NF):
            part = (ft[f, 1:NY + 1] - ft[f, 0:NY]).T
            acc[f] += part.reshape(NX, NZ, NY)

    def receive_side(sec, w, side):
        pltpu.make_async_copy(ghost.at[sec, side], ghost.at[sec, side], x_recv.at[sec, side]).wait()
        kick = jnp.where((rad == 0) & (side == 0), shear_jump, 0.0) - jnp.where(
            (rad == RAD - 1) & (side == 1), shear_jump, 0.0)
        for f in range(NF):
            for j in range(2):
                value = ghost[sec, side, f, j]
                w[f, 10 * side + j] = value + kick if f == 2 else value

    def sheared_near():
        near = far_in.at[:, pl.ds(0, 9)]
        pltpu.make_async_copy(near, near, far_recv.at[0]).wait()
        for j in range(2):
            cells, columns = [], []
            for f in range(NF):
                at = f * 4 + j * 2
                cells.append(far_in[at:at + 2, 0:8].reshape(NZ, NY))
                pair = [pltpu.roll(jnp.broadcast_to(far_in[at + half, 8:9], (8, NY)), NY - 30, 1,
                                   stride=4, stride_axis=0) for half in range(2)]
                columns.append(jnp.concatenate(pair, axis=0))
                ext_rows[f, 2 + j] = cells[f]
            flux = rolled_faces(cells, 0, 2)
            part = ghosted_divergence(cells, columns, lane, 1)
            for f in range(NF):
                ext_part[f, j] = pltpu.roll(flux[f], NZ - 1, 0) - flux[f] + part[f]

    def sheared_rows(w):
        pltpu.make_async_copy(plane_in, plane_in, plane_recv).wait()
        far = far_in.at[:, pl.ds(16, 8)]
        pltpu.make_async_copy(far, far, far_recv.at[1]).wait()
        far_at = jnp.where(rad == 0, 0, 4)
        plane_kick = jnp.where(rad == 0, -shear_jump, shear_jump)
        for f in range(NF):
            for j in range(2):
                at = f * 4 + j * 2
                ext_rows[f, far_at + j] = far_in[at:at + 2, 16:24].reshape(NZ, NY)
                value = plane_in[f, j]
                if f == 2:
                    value = value + plane_kick
                ext_rows[f, 4 - far_at + j] = value
        x_faces(ext_rows, ext_flux, 0, 3)
        at = jnp.where(rad == 0, 0, 10)
        for j in range(2):
            u = conserved_of([ext_rows[f, 2 + j] for f in range(NF)])
            for f in range(NF):
                total = ext_part[f, j] + (ext_flux[f, j + 1] - ext_flux[f, j])
                u[f] = u[f] - (0.5 * time_step) * total
            mid = primitive_of(u)
            mid[2] = mid[2] - plane_kick
            for f in range(NF):
                w[f, at + j] = mid[f]

    def side_at(k):
        return (k + jnp.where(rad == 0, 1, 0)) % 2

    def side_faces(w, side):
        x_faces(w, fx, 7 * side, 7 * side + 2)

    def row_total(x):
        return [-0.5 * (acc[f, x] + (fx[f, x + 1] - fx[f, x])) for f in range(NF)]

    def middle(x, carry):
        total = row_total(x)
        u = conserved_row(x)
        w = primitive_of([u[f] + time_step * total[f] for f in range(NF)])
        for f in range(NF):
            tend[f, x] = total[f]
            w2[f, x + 2] = w[f]
        z_row(w2, x)
        return carry

    out_rows = out_ref.reshape(NF * NZ * NX, NY)

    def last(x, carry):
        total = row_total(x)
        for f in range(NF):
            out_rows[pl.ds(f * NZ * NX + x, NZ, NX), :] = 0.5 * (tend[f, x] + total[f])
        return carry

    start_y(0)
    scatter()
    lax.fori_loop(0, NX, z_first, 0)
    y_part()
    x_faces(w1, fx, 2, 7)
    finish_y(0)
    lax.fori_loop(2, 6, middle, 0)
    start_x(0, w1, 0)
    start_x(0, w1, 1)
    load_shift.wait()
    serve()

    def first_side(k, carry):
        side = side_at(k)
        receive_side(0, w1, side)
        side_faces(w1, side)
        lax.fori_loop(6 * side, 6 * side + 2, middle, 0)
        start_x(1, w2, side)

        @pl.when(k == 0)
        def _():
            soon = jnp.where(rad == 0, 4, 2)
            x_faces(w2, fx, soon, soon + 3)

        return carry

    lax.fori_loop(0, 2, first_side, 0)
    turn_y(1, w2)
    start_y(1)
    y_part()
    late = jnp.where(rad == 0, 2, 5)
    x_faces(w2, fx, late, late + 2)

    def second_side(k, carry):
        side = side_at(k)
        sheared = edge & (k == 1)

        @pl.when(sheared)
        def _():
            sheared_near()
            sheared_rows(w2)

        @pl.when(jnp.logical_not(sheared))
        def _():
            receive_side(1, w2, side)

        side_faces(w2, side)
        return carry

    lax.fori_loop(0, 2, second_side, 0)
    finish_y(1)
    lax.fori_loop(0, NX, last, 0)

    for sec, w in ((0, w1), (1, w2)):
        y_copy(sec, True).wait_send()
        y_copy(sec, False).wait_send()

        @pl.when(rad < RAD - 1)
        def _():
            x_copy(sec, w, True).wait_send()

        @pl.when(rad > 0)
        def _():
            x_copy(sec, w, False).wait_send()

    @pl.when(edge)
    def _():
        for t in range(2):
            most = stage.at[t, pl.ds(0, AZ - 1)]
            pltpu.make_async_copy(most, most, a_send.at[t]).wait()

            @pl.when(jnp.logical_not(relay))
            def _():
                pltpu.make_async_copy(stage.at[t, 0], stage.at[t, 0], a_send.at[t]).wait()

    @pl.when(relay)
    def _():
        pltpu.make_async_copy(near_out, near_out, b_send).wait()
        for t, begin, rows in ((0, 0, 9), (1, 16, 8)):
            sent = far_out.at[:, pl.ds(begin, rows)]
            pltpu.make_async_copy(sent, sent, far_send.at[t]).wait()
        most = plane_out.at[pl.ds(0, AZ - 1)]
        pltpu.make_async_copy(most, most, plane_send).wait()

        @pl.when(jnp.logical_not(edge))
        def _():
            pltpu.make_async_copy(plane_out.at[0], plane_out.at[0], plane_send).wait()


def shards(conserved, shear_shift):
    f32 = jnp.float32
    return pl.pallas_call(
        kernel,
        out_shape=jax.ShapeDtypeStruct((NF, NZ, NX, NY), f32),
        in_specs=[pl.BlockSpec(memory_space=pltpu.HBM), pl.BlockSpec(memory_space=pltpu.HBM)],
        out_specs=pl.BlockSpec(memory_space=pltpu.VMEM),
        scratch_shapes=[
            pltpu.VMEM((NF, NZ, NX, NY), f32),
            pltpu.VMEM((NF, NX + 4, NZ, NY), f32),
            pltpu.VMEM((NF, NX + 4, NZ, NY), f32),
            pltpu.VMEM((NF, NX, NZ, NY), f32),
            pltpu.VMEM((NF, NX + 1, NZ, NY), f32),
            pltpu.VMEM((NF, NX, NZ, NY), f32),
            pltpu.VMEM((NF, NY + 24, NX * NZ), f32),
            pltpu.VMEM((NF, NY + 8, NX * NZ), f32),
            pltpu.VMEM((2, 2, 2 * NF, NX * NZ), f32),
            pltpu.VMEM((2, 2, 2 * NF, NX * NZ), f32),
            pltpu.VMEM((2, 2, NF, 2, NZ, NY), f32),
            pltpu.VMEM((2, AZ, 8, NY), f32),
            pltpu.VMEM((2, AZ, 8, NY), f32),
            pltpu.VMEM((2, AZ, 8, NY), f32),
            pltpu.VMEM((AZ, 8, NY), f32),
            pltpu.VMEM((AZ, 24, NY), f32),
            pltpu.VMEM((AZ, 8, NY), f32),
            pltpu.VMEM((AZ, 24, NY), f32),
            pltpu.VMEM((NF, 2, NZ, NY), f32),
            pltpu.VMEM((NF, 6, NZ, NY), f32),
            pltpu.VMEM((NF, 3, NZ, NY), f32),
            pltpu.VMEM((NF, 2, NZ, NY), f32),
            pltpu.SMEM((2,), jnp.int32),
            pltpu.SemaphoreType.DMA,
            pltpu.SemaphoreType.DMA,
            pltpu.SemaphoreType.DMA((2, 2)),
            pltpu.SemaphoreType.DMA((2, 2)),
            pltpu.SemaphoreType.DMA((2, 2)),
            pltpu.SemaphoreType.DMA((2, 2)),
            pltpu.SemaphoreType.DMA((2,)),
            pltpu.SemaphoreType.DMA((2,)),
            pltpu.SemaphoreType.DMA,
            pltpu.SemaphoreType.DMA((2,)),
            pltpu.SemaphoreType.DMA((2,)),
            pltpu.SemaphoreType.DMA,
            pltpu.SemaphoreType.DMA,
        ],
        name="mhd_step",
        compiler_params=pltpu.CompilerParams(
            collective_id=0, has_side_effects=True, vmem_limit_bytes=53 * 1024 * 1024),
    )(pltpu.with_memory_space_constraint(shear_shift, pltpu.HBM),
      pltpu.with_memory_space_constraint(conserved, pltpu.HBM))


def solution(mesh):
    return jax.shard_map(
        shards,
        mesh=mesh,
        in_specs=(P(None, None, "rad", "az"), P()),
        out_specs=P(None, None, "rad", "az"),
        check_vma=False,
    )
```

```python
import functools

import jax
import jax.numpy as jnp
from jax import lax
from jax.experimental import pallas as pl
from jax.experimental.pallas import tpu as pltpu
from jax.sharding import PartitionSpec as P

MESH = pl.DeviceIdType.MESH
time_step = 0.02
shear_jump = 0.5
AZ, RAD = 32, 8
NF, NX, NZ, NY = 8, 8, 16, 128
COLS = AZ * NY


def primitive_of(u):
    inv = 1.0 / u[0]
    v = [u[i] * inv for i in (1, 2, 3)]
    vv = v[0] * v[0] + v[1] * v[1] + v[2] * v[2]
    bb = u[5] * u[5] + u[6] * u[6] + u[7] * u[7]
    p = (2.0 / 3.0) * (u[4] - 0.5 * u[0] * vv - 0.5 * bb)
    return [u[0], v[0], v[1], v[2], p, u[5], u[6], u[7]]


def conserved_of(w):
    rho, v, p, b = w[0], w[1:4], w[4], w[5:8]
    vv = v[0] * v[0] + v[1] * v[1] + v[2] * v[2]
    bb = b[0] * b[0] + b[1] * b[1] + b[2] * b[2]
    return [rho] + [rho * c for c in v] + [1.5 * p + 0.5 * rho * vv + 0.5 * bb] + list(b)


def half_slope(a, b):
    return 0.5 * jnp.maximum(jnp.minimum(a, b), jnp.minimum(jnp.maximum(a, b), 0.0))


def state_of(w, n):
    rho, v, p, b = w[0], w[1:4], w[4], w[5:8]
    vn, bn = v[n], b[n]
    bb = b[0] * b[0] + b[1] * b[1] + b[2] * b[2]
    hb = 0.5 * bb
    vv = v[0] * v[0] + v[1] * v[1] + v[2] * v[2]
    vb = v[0] * b[0] + v[1] * b[1] + v[2] * b[2]
    pt = p + hb
    mom = [rho * c for c in v]
    en = 1.5 * p + 0.5 * rho * vv + hb
    fm = [mom[i] * vn - b[i] * bn for i in range(3)]
    fm[n] = fm[n] + pt
    fe = (en + pt) * vn - bn * vb
    fb = [None if i == n else b[i] * vn - v[i] * bn for i in range(3)]
    a = (5.0 / 3.0) * p + bb
    speed = jnp.abs(vn) + (a * lax.rsqrt(a)) * lax.rsqrt(rho)
    return [rho] + mom + [en] + list(b), [mom[n]] + fm + [fe] + fb, speed


def twice_flux(left, right, n):
    ul, fl, cl = state_of(left, n)
    ur, fr, cr = state_of(right, n)
    c = jnp.maximum(cl, cr)
    out = []
    for i in range(NF):
        diff = c * (ur[i] - ul[i])
        out.append(-diff if fl[i] is None else fl[i] + fr[i] - diff)
    return out


def rolled_faces(w, axis, n):
    size = w[0].shape[axis]
    left, right = [], []
    for f in range(NF):
        d = w[f] - pltpu.roll(w[f], 1, axis)
        h = half_slope(d, pltpu.roll(d, size - 1, axis))
        left.append(pltpu.roll(w[f] + h, 1, axis))
        right.append(w[f] - h)
    return twice_flux(left, right, n)


def ghosted_divergence(w, g, lane, n):
    size = w[0].shape[1]
    first, final = lane == 0, lane == size - 1
    left, right, left_g, right_g = [], [], [], []
    for f in range(NF):
        w_up, g_up = pltpu.roll(w[f], 1, 1), pltpu.roll(g[f], 1, 1)
        d = w[f] - jnp.where(first, g_up, w_up)
        d_g = g[f] - jnp.where(first, w_up, g_up)
        d_down, d_g_down = pltpu.roll(d, size - 1, 1), pltpu.roll(d_g, size - 1, 1)
        h = half_slope(d, jnp.where(final, d_g_down, d_down))
        h_g = half_slope(d_g, jnp.where(final, d_down, d_g_down))
        l_up = pltpu.roll(w[f] + h, 1, 1)
        left.append(jnp.where(first, pltpu.roll(g[f] + h_g, 1, 1), l_up))
        right.append(w[f] - h)
        left_g.append(l_up)
        right_g.append(g[f] - h_g)
    flux = twice_flux(left, right, n)
    flux_g = twice_flux(left_g, right_g, n)
    return [jnp.where(final, pltpu.roll(flux_g[f], size - 1, 1), pltpu.roll(flux[f], size - 1, 1)) - flux[f]
            for f in range(NF)]


def plane_of(z, x, core):
    s = z + x + core
    return 3 - (s - 3 * ((s * 11) >> 5))


def kernel(shift_hbm, u_hbm, out_ref, raw, w1, w2, acc, fx, tend, wt, ft, y_out, y_in, ghost, stage, relay_in,
           relay_roll, near_out, far_out, plane_out, far_in, plane_in, ext_rows, ext_flux, ext_part, shift_ref, in_sem, shift_sem,
           x_send, x_recv, y_send, y_recv, a_send, a_recv, b_send, far_send, far_recv, plane_send, plane_recv):
    az = lax.axis_index("az")
    rad = lax.axis_index("rad")
    right, left = (az + 1) % AZ, (az + AZ - 1) % AZ
    edge = (rad == 0) | (rad == RAD - 1)
    my_z, my_x, my_core = az >> 3, (az >> 1) & 3, az & 1
    my_plane = plane_of(my_z, my_x, my_core)
    relay_lo = rad == 4 + my_plane
    relay_hi = rad == 3 - my_plane
    relay = relay_lo | relay_hi
    both = edge & relay

    barrier = pltpu.get_barrier_semaphore()

    def signal(*device):
        pl.semaphore_signal(barrier, 1, device_id=device, device_id_type=MESH)

    load = pltpu.make_async_copy(u_hbm, raw, in_sem)
    load.start()
    load_shift = pltpu.make_async_copy(shift_hbm, shift_ref, shift_sem)
    load_shift.start()

    z_list = [3 - my_z, (my_z + 2) & 3, my_z + 1 - 2 * (my_z & 1), my_z]
    x_list = [(my_x + 2) & 3, (my_x + 1) & 3, (my_x + 3) & 3, my_x]
    core_list = [1 - my_core, my_core]

    def peers(across):
        out = []
        for z in range(4) if across else z_list:
            for x in x_list:
                for core in core_list:
                    out.append((z * 8 + x * 2 + core, plane_of(z, x, core)))
        return out

    def others(body):
        everyone = peers(False)
        for p, plane in everyone[:-1]:
            body(p, plane)

        @pl.when(jnp.logical_not(both))
        def _():
            body(*everyone[-1])

    @pl.when(relay)
    def _():
        source = jnp.where(relay_lo, RAD - 1, 0)
        others(lambda p, plane: signal(p, source))

    signal(right, rad)
    signal(left, rad)

    @pl.when(rad > 0)
    def _():
        signal(az, rad - 1)

    @pl.when(rad < RAD - 1)
    def _():
        signal(az, rad + 1)

    @pl.when(edge)
    def _():
        signal(az, RAD - 1 - rad)

    lane = lax.broadcasted_iota(jnp.int32, (NZ, NY), 1)
    load.wait()
    u_rows = raw.reshape(NF * NZ * NX, NY)

    def conserved_row(x):
        return [u_rows[pl.ds(f * NZ * NX + x, NZ, NX), :] for f in range(NF)]

    def first_rows(x, carry):
        w = primitive_of(conserved_row(x))
        for f in range(NF):
            w1[f, x + 2] = w[f]
        return carry

    lax.fori_loop(0, NX, first_rows, 0)

    def turn_y(sec, w):
        for f in range(NF):
            wt[f, 8:8 + NY] = w[f, 2:2 + NX].reshape(NX * NZ, NY).T
        for f in range(NF):
            y_out[sec, 0, 2 * f:2 * f + 2] = wt[f, 8 + NY - 2:8 + NY]
            y_out[sec, 1, 2 * f:2 * f + 2] = wt[f, 8:10]

    @pl.when(edge)
    def _():
        near, far = jnp.where(rad == 0, 2, 8), jnp.where(rad == 0, 4, 6)
        for f in range(NF):
            for j in range(2):
                for t, base in ((0, near), (1, far)):
                    row = w1[f, base + j]
                    for half in range(2):
                        stage[t, f * 4 + j * 2 + half] = row[half * 8:half * 8 + 8]

    turn_y(0, w1)
    pl.semaphore_wait(barrier, jnp.where(edge, AZ + 4, 4) - jnp.where(both, 1, 0))

    def x_copy(sec, w, up):
        rows = w.at[:, pl.ds(8 if up else 2, 2)]
        side = 0 if up else 1
        return pltpu.make_async_remote_copy(
            rows, ghost.at[sec, side], x_send.at[sec, side], x_recv.at[sec, side],
            device_id=(az, rad + 1 if up else rad - 1), device_id_type=MESH)

    def y_copy(sec, up):
        side = 0 if up else 1
        return pltpu.make_async_remote_copy(
            y_out.at[sec, side], y_in.at[sec, side], y_send.at[sec, side], y_recv.at[sec, side],
            device_id=(right if up else left, rad), device_id_type=MESH)

    def scatter(t):
        @pl.when(edge)
        def _():
            base, sign = jnp.where(rad == 0, 3, 4), jnp.where(rad == 0, -1, 1)
            def send(p, plane):
                pltpu.make_async_remote_copy(
                    stage.at[t, p], relay_in.at[t, az], a_send.at[t], a_recv.at[t],
                    device_id=(p, base + sign * plane), device_id_type=MESH).start()

            others(send)

            @pl.when(both)
            def _():
                pltpu.make_async_copy(stage.at[t, az], relay_in.at[t, az], a_recv.at[t]).start()

    def start_x(sec, w, side):
        @pl.when((side == 1) & (rad < RAD - 1))
        def _():
            x_copy(sec, w, True).start()

        @pl.when((side == 0) & (rad > 0))
        def _():
            x_copy(sec, w, False).start()

    def start_y(sec):
        y_copy(sec, True).start()
        y_copy(sec, False).start()

    def serve():
        @pl.when(relay)
        def _():
            def signed(s):
                return jnp.where(relay_lo, s, COLS - s) % COLS

            shift_0, shift_1 = signed(shift_ref[0]), signed(shift_ref[1])
            f, j, half = az >> 2, (az >> 1) & 1, az & 1
            rows = pl.ds(pl.multiple_of(half * 8, 8), 8)
            side = jnp.where(relay_lo, 0, 1)
            across = jnp.where(relay_lo, 0, RAD - 1)
            small = lax.broadcasted_iota(jnp.int32, (8, NY), 1)

            def arrived(t):
                pltpu.make_async_copy(relay_in.at[t], relay_in.at[t], a_recv.at[t]).wait()

            def turn(slots, tiles, amount):
                part = amount % NY

                for k in range(AZ):
                    for c, t in zip(slots, tiles):
                        relay_roll[c, k] = pltpu.roll(relay_in[t, k], (NY - part) % NY, 1)

            def pick(c, d, amount):
                whole, part = amount >> 7, amount & (NY - 1)
                return jnp.where(
                    small < NY - part, relay_roll[c, (d + whole) & (AZ - 1)], relay_roll[c, (d + whole + 1) & (AZ - 1)])

            arrived(0)
            turn((0,), (0,), shift_0)
            for d, _ in peers(True):
                near_out[d] = pick(0, d, shift_0)
                pltpu.make_async_remote_copy(
                    near_out.at[d], ghost.at[0, side, f, j, rows], b_send, x_recv.at[0, side],
                    device_id=(d, across), device_id_type=MESH).start()

            turn((0,), (0,), shift_1)
            for d in range(AZ):
                far_out[d, 0:8] = pick(0, d, shift_1)
            sub = lax.broadcasted_iota(jnp.int32, (8, NY), 0)
            for d in range(AZ):
                ends = jnp.where(small < NY // 2, far_out[(d + 1) % AZ, 0:8], far_out[(d + AZ - 1) % AZ, 0:8])
                ends = jnp.where(small < 4, pltpu.roll(ends, 2, 1), 0.0)
                for width in (4, 8, 16):
                    ends = ends + pltpu.roll(ends, width, 1)
                ends = jnp.where(small >> 2 == 7 - sub, ends, 0.0)
                far_out[d, 8:9] = jnp.sum(ends, axis=0, keepdims=True)

            def answer(begin, rows, t):
                for d, _ in peers(True):
                    pltpu.make_async_remote_copy(
                        far_out.at[d, pl.ds(begin, rows)], far_in.at[az, pl.ds(begin, rows)],
                        far_send.at[t], far_recv.at[t], device_id=(d, across), device_id_type=MESH).start()

            answer(0, 9, 0)
            arrived(1)
            turn((1,), (1,), shift_1)
            for d in range(AZ):
                far_out[d, 16:24] = pick(1, d, shift_1)
            answer(16, 8, 1)
            shift_2 = (shift_0 - shift_1 + COLS) % COLS
            turn((0,), (0,), shift_2)

            for d in range(AZ):
                plane_out[d] = pick(0, d, shift_2)

            def send(d, plane):
                pltpu.make_async_remote_copy(
                    plane_out.at[d], plane_in.at[f, j, rows], plane_send, plane_recv,
                    device_id=(d, RAD - 1 - across), device_id_type=MESH).start()

            others(send)

            @pl.when(both)
            def _():
                pltpu.make_async_copy(plane_out.at[az], plane_in.at[f, j, rows], plane_recv).start()

    def z_row(w, x):
        flux = rolled_faces([w[f, x + 2] for f in range(NF)], 0, 2)
        for f in range(NF):
            acc[f, x] = pltpu.roll(flux[f], NZ - 1, 0) - flux[f]

    def z_first(x, carry):
        z_row(w1, x)
        return carry

    def y_faces(k):
        lefts, rights = [], []
        for f in range(NF):
            c = [wt[f, pl.ds(8 * k + 6 + o, 8)] for o in range(4)]
            d = [c[o + 1] - c[o] for o in range(3)]
            lefts.append(c[1] + half_slope(d[0], d[1]))
            rights.append(c[2] - half_slope(d[1], d[2]))
        flux = twice_flux(lefts, rights, 1)
        for f in range(NF):
            ft[f, pl.ds(pl.multiple_of(8 * k, 8), 8)] = flux[f]

    def y_part():
        def pair(k, carry):
            y_faces(2 * k + 1)
            y_faces(2 * k + 2)
            return carry

        lax.fori_loop(0, 7, pair, 0)

    def x_faces(w, flux_ref, begin, end, unrolled=0):
        def face(i, carry):
            lefts, rights = [], []
            for f in range(NF):
                c = [w[f, i + k] for k in range(4)]
                d = [c[k + 1] - c[k] for k in range(3)]
                lefts.append(c[1] + half_slope(d[0], d[1]))
                rights.append(c[2] - half_slope(d[1], d[2]))
            flux = twice_flux(lefts, rights, 0)
            for f in range(NF):
                flux_ref[f, i] = flux[f]
            return carry

        if unrolled:
            for k in range(unrolled):
                face(begin + k, 0)
        else:
            lax.fori_loop(begin, end, face, 0)

    def finish_y(sec):
        y_copy(sec, True).wait_recv()
        y_copy(sec, False).wait_recv()
        for f in range(NF):
            wt[f, 6:8] = y_in[sec, 0, 2 * f:2 * f + 2]
            wt[f, 8 + NY:10 + NY] = y_in[sec, 1, 2 * f:2 * f + 2]
        for k in (0, 15, 16):
            y_faces(k)
        for f in range(NF):
            part = (ft[f, 1:NY + 1] - ft[f, 0:NY]).T
            acc[f] += part.reshape(NX, NZ, NY)

    def receive_side(sec, w, side):
        pltpu.make_async_copy(ghost.at[sec, side], ghost.at[sec, side], x_recv.at[sec, side]).wait()
        kick = jnp.where((rad == 0) & (side == 0), shear_jump, 0.0) - jnp.where(
            (rad == RAD - 1) & (side == 1), shear_jump, 0.0)
        for f in range(NF):
            for j in range(2):
                value = ghost[sec, side, f, j]
                w[f, 10 * side + j] = value + kick if f == 2 else value

    def sheared_near():
        near = far_in.at[:, pl.ds(0, 9)]
        pltpu.make_async_copy(near, near, far_recv.at[0]).wait()
        for j in range(2):
            cells, columns = [], []
            for f in range(NF):
                at = f * 4 + j * 2
                cells.append(far_in[at:at + 2, 0:8].reshape(NZ, NY))
                pair = [pltpu.roll(jnp.broadcast_to(far_in[at + half, 8:9], (8, NY)), NY - 30, 1,
                                   stride=4, stride_axis=0) for half in range(2)]
                columns.append(jnp.concatenate(pair, axis=0))
                ext_rows[f, 2 + j] = cells[f]
            flux = rolled_faces(cells, 0, 2)
            part = ghosted_divergence(cells, columns, lane, 1)
            for f in range(NF):
                ext_part[f, j] = pltpu.roll(flux[f], NZ - 1, 0) - flux[f] + part[f]

    def sheared_rows(w):
        pltpu.make_async_copy(plane_in, plane_in, plane_recv).wait()
        far = far_in.at[:, pl.ds(16, 8)]
        pltpu.make_async_copy(far, far, far_recv.at[1]).wait()
        far_at = jnp.where(rad == 0, 0, 4)
        plane_kick = jnp.where(rad == 0, -shear_jump, shear_jump)
        for f in range(NF):
            for j in range(2):
                at = f * 4 + j * 2
                ext_rows[f, far_at + j] = far_in[at:at + 2, 16:24].reshape(NZ, NY)
                value = plane_in[f, j]
                if f == 2:
                    value = value + plane_kick
                ext_rows[f, 4 - far_at + j] = value
        x_faces(ext_rows, ext_flux, 0, 3, 3)
        at = jnp.where(rad == 0, 0, 10)
        for j in range(2):
            u = conserved_of([ext_rows[f, 2 + j] for f in range(NF)])
            for f in range(NF):
                total = ext_part[f, j] + (ext_flux[f, j + 1] - ext_flux[f, j])
                u[f] = u[f] - (0.5 * time_step) * total
            mid = primitive_of(u)
            mid[2] = mid[2] - plane_kick
            for f in range(NF):
                w[f, at + j] = mid[f]

    def side_at(k):
        return (k + jnp.where(rad == 0, 1, 0)) % 2

    def side_faces(w, side):
        x_faces(w, fx, 7 * side, 7 * side + 2, 2)

    def row_total(x):
        return [-0.5 * (acc[f, x] + (fx[f, x + 1] - fx[f, x])) for f in range(NF)]

    def middle(x, carry):
        total = row_total(x)
        u = conserved_row(x)
        w = primitive_of([u[f] + time_step * total[f] for f in range(NF)])
        for f in range(NF):
            tend[f, x] = total[f]
            w2[f, x + 2] = w[f]
        return carry

    def z_second(x, carry):
        z_row(w2, x)
        return carry

    out_rows = out_ref.reshape(NF * NZ * NX, NY)

    def last(x, carry):
        total = row_total(x)
        for f in range(NF):
            out_rows[pl.ds(f * NZ * NX + x, NZ, NX), :] = 0.5 * (tend[f, x] + total[f])
        return carry

    start_y(0)
    scatter(0)
    lax.fori_loop(0, NX, z_first, 0)
    y_part()
    x_faces(w1, fx, 2, 7)
    scatter(1)
    finish_y(0)
    lax.fori_loop(2, 6, middle, 0)
    lax.fori_loop(2, 6, z_second, 0)
    start_x(0, w1, 0)
    start_x(0, w1, 1)
    load_shift.wait()
    serve()

    def first_side(k, carry):
        side = side_at(k)
        receive_side(0, w1, side)
        side_faces(w1, side)
        lax.fori_loop(6 * side, 6 * side + 2, middle, 0)
        start_x(1, w2, side)

        @pl.when(k == 0)
        def _():
            lax.fori_loop(6 * side, 6 * side + 2, z_second, 0)
            soon = jnp.where(rad == 0, 4, 2)
            x_faces(w2, fx, soon, soon + 3)

        return carry

    lax.fori_loop(0, 2, first_side, 0)
    turn_y(1, w2)
    start_y(1)
    after = 6 * side_at(1)
    lax.fori_loop(after, after + 2, z_second, 0)
    y_part()
    late = jnp.where(rad == 0, 2, 5)
    x_faces(w2, fx, late, late + 2)

    def second_side(k, carry):
        side = side_at(k)
        sheared = edge & (k == 1)

        @pl.when(sheared)
        def _():
            sheared_rows(w2)

        @pl.when(jnp.logical_not(sheared))
        def _():
            receive_side(1, w2, side)

        side_faces(w2, side)

        @pl.when(k == 0)
        def _():
            @pl.when(edge)
            def _():
                sheared_near()

            finish_y(1)

        return carry

    lax.fori_loop(0, 2, second_side, 0)
    lax.fori_loop(0, NX, last, 0)

    for sec, w in ((0, w1), (1, w2)):
        y_copy(sec, True).wait_send()
        y_copy(sec, False).wait_send()

        @pl.when(rad < RAD - 1)
        def _():
            x_copy(sec, w, True).wait_send()

        @pl.when(rad > 0)
        def _():
            x_copy(sec, w, False).wait_send()

    @pl.when(edge)
    def _():
        for t in range(2):
            most = stage.at[t, pl.ds(0, AZ - 1)]
            pltpu.make_async_copy(most, most, a_send.at[t]).wait()

            @pl.when(jnp.logical_not(relay))
            def _():
                pltpu.make_async_copy(stage.at[t, 0], stage.at[t, 0], a_send.at[t]).wait()

    @pl.when(relay)
    def _():
        pltpu.make_async_copy(near_out, near_out, b_send).wait()
        for t, begin, rows in ((0, 0, 9), (1, 16, 8)):
            sent = far_out.at[:, pl.ds(begin, rows)]
            pltpu.make_async_copy(sent, sent, far_send.at[t]).wait()
        most = plane_out.at[pl.ds(0, AZ - 1)]
        pltpu.make_async_copy(most, most, plane_send).wait()

        @pl.when(jnp.logical_not(edge))
        def _():
            pltpu.make_async_copy(plane_out.at[0], plane_out.at[0], plane_send).wait()


def shards(conserved, shear_shift):
    f32 = jnp.float32
    return pl.pallas_call(
        kernel,
        out_shape=jax.ShapeDtypeStruct((NF, NZ, NX, NY), f32),
        in_specs=[pl.BlockSpec(memory_space=pltpu.HBM), pl.BlockSpec(memory_space=pltpu.HBM)],
        out_specs=pl.BlockSpec(memory_space=pltpu.VMEM),
        scratch_shapes=[
            pltpu.VMEM((NF, NZ, NX, NY), f32),
            pltpu.VMEM((NF, NX + 4, NZ, NY), f32),
            pltpu.VMEM((NF, NX + 4, NZ, NY), f32),
            pltpu.VMEM((NF, NX, NZ, NY), f32),
            pltpu.VMEM((NF, NX + 1, NZ, NY), f32),
            pltpu.VMEM((NF, NX, NZ, NY), f32),
            pltpu.VMEM((NF, NY + 24, NX * NZ), f32),
            pltpu.VMEM((NF, NY + 8, NX * NZ), f32),
            pltpu.VMEM((2, 2, 2 * NF, NX * NZ), f32),
            pltpu.VMEM((2, 2, 2 * NF, NX * NZ), f32),
            pltpu.VMEM((2, 2, NF, 2, NZ, NY), f32),
            pltpu.VMEM((2, AZ, 8, NY), f32),
            pltpu.VMEM((2, AZ, 8, NY), f32),
            pltpu.VMEM((2, AZ, 8, NY), f32),
            pltpu.VMEM((AZ, 8, NY), f32),
            pltpu.VMEM((AZ, 24, NY), f32),
            pltpu.VMEM((AZ, 8, NY), f32),
            pltpu.VMEM((AZ, 24, NY), f32),
            pltpu.VMEM((NF, 2, NZ, NY), f32),
            pltpu.VMEM((NF, 6, NZ, NY), f32),
            pltpu.VMEM((NF, 3, NZ, NY), f32),
            pltpu.VMEM((NF, 2, NZ, NY), f32),
            pltpu.SMEM((2,), jnp.int32),
            pltpu.SemaphoreType.DMA,
            pltpu.SemaphoreType.DMA,
            pltpu.SemaphoreType.DMA((2, 2)),
            pltpu.SemaphoreType.DMA((2, 2)),
            pltpu.SemaphoreType.DMA((2, 2)),
            pltpu.SemaphoreType.DMA((2, 2)),
            pltpu.SemaphoreType.DMA((2,)),
            pltpu.SemaphoreType.DMA((2,)),
            pltpu.SemaphoreType.DMA,
            pltpu.SemaphoreType.DMA((2,)),
            pltpu.SemaphoreType.DMA((2,)),
            pltpu.SemaphoreType.DMA,
            pltpu.SemaphoreType.DMA,
        ],
        name="mhd_step",
        compiler_params=pltpu.CompilerParams(
            collective_id=0, has_side_effects=True, vmem_limit_bytes=53 * 1024 * 1024),
    )(pltpu.with_memory_space_constraint(shear_shift, pltpu.HBM),
      pltpu.with_memory_space_constraint(conserved, pltpu.HBM))


def solution(mesh):
    return jax.shard_map(
        shards,
        mesh=mesh,
        in_specs=(P(None, None, "rad", "az"), P()),
        out_specs=P(None, None, "rad", "az"),
        check_vma=False,
    )
```

```python
import functools

import jax
import jax.numpy as jnp
from jax import lax
from jax.experimental import pallas as pl
from jax.experimental.pallas import tpu as pltpu
from jax.sharding import PartitionSpec as P

MESH = pl.DeviceIdType.MESH
time_step = 0.02
shear_jump = 0.5
AZ, RAD = 32, 8
NF, NX, NZ, NY = 8, 8, 16, 128
COLS = AZ * NY


def primitive_of(u):
    inv = 1.0 / u[0]
    v = [u[i] * inv for i in (1, 2, 3)]
    vv = v[0] * v[0] + v[1] * v[1] + v[2] * v[2]
    bb = u[5] * u[5] + u[6] * u[6] + u[7] * u[7]
    p = (2.0 / 3.0) * (u[4] - 0.5 * u[0] * vv - 0.5 * bb)
    return [u[0], v[0], v[1], v[2], p, u[5], u[6], u[7]]


def conserved_of(w):
    rho, v, p, b = w[0], w[1:4], w[4], w[5:8]
    vv = v[0] * v[0] + v[1] * v[1] + v[2] * v[2]
    bb = b[0] * b[0] + b[1] * b[1] + b[2] * b[2]
    return [rho] + [rho * c for c in v] + [1.5 * p + 0.5 * rho * vv + 0.5 * bb] + list(b)


def half_slope(a, b):
    return 0.5 * jnp.maximum(jnp.minimum(a, b), jnp.minimum(jnp.maximum(a, b), 0.0))


def state_of(w, n):
    rho, v, p, b = w[0], w[1:4], w[4], w[5:8]
    vn, bn = v[n], b[n]
    bb = b[0] * b[0] + b[1] * b[1] + b[2] * b[2]
    hb = 0.5 * bb
    vv = v[0] * v[0] + v[1] * v[1] + v[2] * v[2]
    vb = v[0] * b[0] + v[1] * b[1] + v[2] * b[2]
    pt = p + hb
    mom = [rho * c for c in v]
    en = 1.5 * p + 0.5 * rho * vv + hb
    fm = [mom[i] * vn - b[i] * bn for i in range(3)]
    fm[n] = fm[n] + pt
    fe = (en + pt) * vn - bn * vb
    fb = [None if i == n else b[i] * vn - v[i] * bn for i in range(3)]
    a = (5.0 / 3.0) * p + bb
    speed = jnp.abs(vn) + (a * lax.rsqrt(a)) * lax.rsqrt(rho)
    return [rho] + mom + [en] + list(b), [mom[n]] + fm + [fe] + fb, speed


def twice_flux(left, right, n):
    ul, fl, cl = state_of(left, n)
    ur, fr, cr = state_of(right, n)
    c = jnp.maximum(cl, cr)
    out = []
    for i in range(NF):
        diff = c * (ur[i] - ul[i])
        out.append(-diff if fl[i] is None else fl[i] + fr[i] - diff)
    return out


def rolled_faces(w, axis, n):
    size = w[0].shape[axis]
    left, right = [], []
    for f in range(NF):
        d = w[f] - pltpu.roll(w[f], 1, axis)
        h = half_slope(d, pltpu.roll(d, size - 1, axis))
        left.append(pltpu.roll(w[f] + h, 1, axis))
        right.append(w[f] - h)
    return twice_flux(left, right, n)


def ghosted_divergence(w, g, lane, n):
    size = w[0].shape[1]
    first, final = lane == 0, lane == size - 1
    left, right, left_g, right_g = [], [], [], []
    for f in range(NF):
        w_up, g_up = pltpu.roll(w[f], 1, 1), pltpu.roll(g[f], 1, 1)
        d = w[f] - jnp.where(first, g_up, w_up)
        d_g = g[f] - jnp.where(first, w_up, g_up)
        d_down, d_g_down = pltpu.roll(d, size - 1, 1), pltpu.roll(d_g, size - 1, 1)
        h = half_slope(d, jnp.where(final, d_g_down, d_down))
        h_g = half_slope(d_g, jnp.where(final, d_down, d_g_down))
        l_up = pltpu.roll(w[f] + h, 1, 1)
        left.append(jnp.where(first, pltpu.roll(g[f] + h_g, 1, 1), l_up))
        right.append(w[f] - h)
        left_g.append(l_up)
        right_g.append(g[f] - h_g)
    flux = twice_flux(left, right, n)
    flux_g = twice_flux(left_g, right_g, n)
    return [jnp.where(final, pltpu.roll(flux_g[f], size - 1, 1), pltpu.roll(flux[f], size - 1, 1)) - flux[f]
            for f in range(NF)]


def plane_of(z, x, core):
    s = z + x + core
    return 3 - (s - 3 * ((s * 11) >> 5))


def kernel(shift_hbm, u_hbm, out_ref, raw, w1, w2, acc, fx, tend, wt, ft, y_out, y_in, ghost, stage, relay_in,
           relay_roll, near_out, far_out, plane_out, far_in, plane_in, ext_rows, ext_flux, ext_part, shift_ref, in_sem, shift_sem,
           x_send, x_recv, y_send, y_recv, a_send, a_recv, b_send, far_send, far_recv, plane_send, plane_recv):
    az = lax.axis_index("az")
    rad = lax.axis_index("rad")
    right, left = (az + 1) % AZ, (az + AZ - 1) % AZ
    edge = (rad == 0) | (rad == RAD - 1)
    my_z, my_x, my_core = az >> 3, (az >> 1) & 3, az & 1
    my_plane = plane_of(my_z, my_x, my_core)
    relay_lo = rad == 4 + my_plane
    relay_hi = rad == 3 - my_plane
    relay = relay_lo | relay_hi
    both = edge & relay

    barrier = pltpu.get_barrier_semaphore()

    def signal(*device):
        pl.semaphore_signal(barrier, 1, device_id=device, device_id_type=MESH)

    load = pltpu.make_async_copy(u_hbm, raw, in_sem)
    load.start()
    load_shift = pltpu.make_async_copy(shift_hbm, shift_ref, shift_sem)
    load_shift.start()

    z_list = [3 - my_z, (my_z + 2) & 3, my_z + 1 - 2 * (my_z & 1), my_z]
    x_list = [(my_x + 2) & 3, (my_x + 1) & 3, (my_x + 3) & 3, my_x]
    core_list = [1 - my_core, my_core]

    def peers(across):
        out = []
        for z in range(4) if across else z_list:
            for x in x_list:
                for core in core_list:
                    out.append((z * 8 + x * 2 + core, plane_of(z, x, core)))
        return out

    def others(body):
        everyone = peers(False)
        for p, plane in everyone[:-1]:
            body(p, plane)

        @pl.when(jnp.logical_not(both))
        def _():
            body(*everyone[-1])

    @pl.when(relay)
    def _():
        source = jnp.where(relay_lo, RAD - 1, 0)
        others(lambda p, plane: signal(p, source))

    signal(right, rad)
    signal(left, rad)

    @pl.when(rad > 0)
    def _():
        signal(az, rad - 1)

    @pl.when(rad < RAD - 1)
    def _():
        signal(az, rad + 1)

    @pl.when(edge)
    def _():
        signal(az, RAD - 1 - rad)

    lane = lax.broadcasted_iota(jnp.int32, (NZ, NY), 1)
    load.wait()
    u_rows = raw.reshape(NF * NZ * NX, NY)

    def conserved_row(x):
        return [u_rows[pl.ds(f * NZ * NX + x, NZ, NX), :] for f in range(NF)]

    def first_rows(x, carry):
        w = primitive_of(conserved_row(x))
        for f in range(NF):
            w1[f, x + 2] = w[f]
        return carry

    lax.fori_loop(0, NX, first_rows, 0)

    def turn_y(sec, w):
        for f in range(NF):
            wt[f, 8:8 + NY] = w[f, 2:2 + NX].reshape(NX * NZ, NY).T
        for f in range(NF):
            y_out[sec, 0, 2 * f:2 * f + 2] = wt[f, 8 + NY - 2:8 + NY]
            y_out[sec, 1, 2 * f:2 * f + 2] = wt[f, 8:10]

    @pl.when(edge)
    def _():
        near, far = jnp.where(rad == 0, 2, 8), jnp.where(rad == 0, 4, 6)
        for f in range(NF):
            for j in range(2):
                for t, base in ((0, near), (1, far)):
                    row = w1[f, base + j]
                    for half in range(2):
                        stage[t, f * 4 + j * 2 + half] = row[half * 8:half * 8 + 8]

    turn_y(0, w1)
    pl.semaphore_wait(barrier, jnp.where(edge, AZ + 4, 4) - jnp.where(both, 1, 0))

    def x_copy(sec, w, up):
        rows = w.at[:, pl.ds(8 if up else 2, 2)]
        side = 0 if up else 1
        return pltpu.make_async_remote_copy(
            rows, ghost.at[sec, side], x_send.at[sec, side], x_recv.at[sec, side],
            device_id=(az, rad + 1 if up else rad - 1), device_id_type=MESH)

    def y_copy(sec, up):
        side = 0 if up else 1
        return pltpu.make_async_remote_copy(
            y_out.at[sec, side], y_in.at[sec, side], y_send.at[sec, side], y_recv.at[sec, side],
            device_id=(right if up else left, rad), device_id_type=MESH)

    def scatter(t):
        @pl.when(edge)
        def _():
            base, sign = jnp.where(rad == 0, 3, 4), jnp.where(rad == 0, -1, 1)
            def send(p, plane):
                pltpu.make_async_remote_copy(
                    stage.at[t, p], relay_in.at[t, az], a_send.at[t], a_recv.at[t],
                    device_id=(p, base + sign * plane), device_id_type=MESH).start()

            others(send)

            @pl.when(both)
            def _():
                pltpu.make_async_copy(stage.at[t, az], relay_in.at[t, az], a_recv.at[t]).start()

    def start_x(sec, w, side):
        @pl.when((side == 1) & (rad < RAD - 1))
        def _():
            x_copy(sec, w, True).start()

        @pl.when((side == 0) & (rad > 0))
        def _():
            x_copy(sec, w, False).start()

    def start_y(sec):
        y_copy(sec, True).start()
        y_copy(sec, False).start()

    def serve():
        @pl.when(relay)
        def _():
            def signed(s):
                return jnp.where(relay_lo, s, COLS - s) % COLS

            shift_0, shift_1 = signed(shift_ref[0]), signed(shift_ref[1])
            f, j, half = az >> 2, (az >> 1) & 1, az & 1
            rows = pl.ds(pl.multiple_of(half * 8, 8), 8)
            side = jnp.where(relay_lo, 0, 1)
            across = jnp.where(relay_lo, 0, RAD - 1)
            small = lax.broadcasted_iota(jnp.int32, (8, NY), 1)

            def arrived(t):
                pltpu.make_async_copy(relay_in.at[t], relay_in.at[t], a_recv.at[t]).wait()

            def turn(slots, tiles, amount):
                part = amount % NY

                for k in range(AZ):
                    for c, t in zip(slots, tiles):
                        relay_roll[c, k] = pltpu.roll(relay_in[t, k], (NY - part) % NY, 1)

            def pick(c, d, amount):
                whole, part = amount >> 7, amount & (NY - 1)
                return jnp.where(
                    small < NY - part, relay_roll[c, (d + whole) & (AZ - 1)], relay_roll[c, (d + whole + 1) & (AZ - 1)])

            arrived(0)
            turn((0,), (0,), shift_0)
            for d in range(AZ):
                near_out[d] = pick(0, d, shift_0)
            for d, _ in peers(True):
                pltpu.make_async_remote_copy(
                    near_out.at[d], ghost.at[0, side, f, j, rows], b_send, x_recv.at[0, side],
                    device_id=(d, across), device_id_type=MESH).start()

            turn((0,), (0,), shift_1)
            for d in range(AZ):
                far_out[d, 0:8] = pick(0, d, shift_1)
            sub = lax.broadcasted_iota(jnp.int32, (8, NY), 0)
            for d in range(AZ):
                ends = jnp.where(small < NY // 2, far_out[(d + 1) % AZ, 0:8], far_out[(d + AZ - 1) % AZ, 0:8])
                ends = jnp.where(small < 4, pltpu.roll(ends, 2, 1), 0.0)
                for width in (4, 8, 16):
                    ends = ends + pltpu.roll(ends, width, 1)
                ends = jnp.where(small >> 2 == 7 - sub, ends, 0.0)
                far_out[d, 8:9] = jnp.sum(ends, axis=0, keepdims=True)

            def answer(begin, rows, t):
                for d, _ in peers(True):
                    pltpu.make_async_remote_copy(
                        far_out.at[d, pl.ds(begin, rows)], far_in.at[az, pl.ds(begin, rows)],
                        far_send.at[t], far_recv.at[t], device_id=(d, across), device_id_type=MESH).start()

            answer(0, 9, 0)
            arrived(1)
            turn((1,), (1,), shift_1)
            for d in range(AZ):
                far_out[d, 16:24] = pick(1, d, shift_1)
            answer(16, 8, 1)
            shift_2 = (shift_0 - shift_1 + COLS) % COLS
            turn((0,), (0,), shift_2)

            for d in range(AZ):
                plane_out[d] = pick(0, d, shift_2)

            def send(d, plane):
                pltpu.make_async_remote_copy(
                    plane_out.at[d], plane_in.at[f, j, rows], plane_send, plane_recv,
                    device_id=(d, RAD - 1 - across), device_id_type=MESH).start()

            others(send)

            @pl.when(both)
            def _():
                pltpu.make_async_copy(plane_out.at[az], plane_in.at[f, j, rows], plane_recv).start()

    def z_row(w, x):
        flux = rolled_faces([w[f, x + 2] for f in range(NF)], 0, 2)
        for f in range(NF):
            acc[f, x] = pltpu.roll(flux[f], NZ - 1, 0) - flux[f]

    def z_first(x, carry):
        z_row(w1, x)
        return carry

    def y_faces(k):
        lefts, rights = [], []
        for f in range(NF):
            c = [wt[f, pl.ds(8 * k + 6 + o, 8)] for o in range(4)]
            d = [c[o + 1] - c[o] for o in range(3)]
            lefts.append(c[1] + half_slope(d[0], d[1]))
            rights.append(c[2] - half_slope(d[1], d[2]))
        flux = twice_flux(lefts, rights, 1)
        for f in range(NF):
            ft[f, pl.ds(pl.multiple_of(8 * k, 8), 8)] = flux[f]

    def y_part():
        def pair(k, carry):
            y_faces(2 * k + 1)
            y_faces(2 * k + 2)
            return carry

        lax.fori_loop(0, 7, pair, 0)

    def x_faces(w, flux_ref, begin, end):
        def face(i, carry):
            lefts, rights = [], []
            for f in range(NF):
                c = [w[f, i + k] for k in range(4)]
                d = [c[k + 1] - c[k] for k in range(3)]
                lefts.append(c[1] + half_slope(d[0], d[1]))
                rights.append(c[2] - half_slope(d[1], d[2]))
            flux = twice_flux(lefts, rights, 0)
            for f in range(NF):
                flux_ref[f, i] = flux[f]
            return carry

        lax.fori_loop(begin, end, face, 0)

    def finish_y(sec):
        y_copy(sec, True).wait_recv()
        y_copy(sec, False).wait_recv()
        for f in range(NF):
            wt[f, 6:8] = y_in[sec, 0, 2 * f:2 * f + 2]
            wt[f, 8 + NY:10 + NY] = y_in[sec, 1, 2 * f:2 * f + 2]
        for k in (0, 15, 16):
            y_faces(k)
        for f in range(NF):
            part = (ft[f, 1:NY + 1] - ft[f, 0:NY]).T
            acc[f] += part.reshape(NX, NZ, NY)

    def receive_side(sec, w, side):
        pltpu.make_async_copy(ghost.at[sec, side], ghost.at[sec, side], x_recv.at[sec, side]).wait()
        kick = jnp.where((rad == 0) & (side == 0), shear_jump, 0.0) - jnp.where(
            (rad == RAD - 1) & (side == 1), shear_jump, 0.0)
        for f in range(NF):
            for j in range(2):
                value = ghost[sec, side, f, j]
                w[f, 10 * side + j] = value + kick if f == 2 else value

    def sheared_near():
        near = far_in.at[:, pl.ds(0, 9)]
        pltpu.make_async_copy(near, near, far_recv.at[0]).wait()
        for j in range(2):
            cells, columns = [], []
            for f in range(NF):
                at = f * 4 + j * 2
                cells.append(far_in[at:at + 2, 0:8].reshape(NZ, NY))
                pair = [pltpu.roll(jnp.broadcast_to(far_in[at + half, 8:9], (8, NY)), NY - 30, 1,
                                   stride=4, stride_axis=0) for half in range(2)]
                columns.append(jnp.concatenate(pair, axis=0))
                ext_rows[f, 2 + j] = cells[f]
            flux = rolled_faces(cells, 0, 2)
            part = ghosted_divergence(cells, columns, lane, 1)
            for f in range(NF):
                ext_part[f, j] = pltpu.roll(flux[f], NZ - 1, 0) - flux[f] + part[f]

    def sheared_rows(w):
        pltpu.make_async_copy(plane_in, plane_in, plane_recv).wait()
        far = far_in.at[:, pl.ds(16, 8)]
        pltpu.make_async_copy(far, far, far_recv.at[1]).wait()
        far_at = jnp.where(rad == 0, 0, 4)
        plane_kick = jnp.where(rad == 0, -shear_jump, shear_jump)
        for f in range(NF):
            for j in range(2):
                at = f * 4 + j * 2
                ext_rows[f, far_at + j] = far_in[at:at + 2, 16:24].reshape(NZ, NY)
                value = plane_in[f, j]
                if f == 2:
                    value = value + plane_kick
                ext_rows[f, 4 - far_at + j] = value
        x_faces(ext_rows, ext_flux, 0, 3)
        at = jnp.where(rad == 0, 0, 10)
        for j in range(2):
            u = conserved_of([ext_rows[f, 2 + j] for f in range(NF)])
            for f in range(NF):
                total = ext_part[f, j] + (ext_flux[f, j + 1] - ext_flux[f, j])
                u[f] = u[f] - (0.5 * time_step) * total
            mid = primitive_of(u)
            mid[2] = mid[2] - plane_kick
            for f in range(NF):
                w[f, at + j] = mid[f]

    def side_at(k):
        return (k + jnp.where(rad == 0, 1, 0)) % 2

    def side_faces(w, side):
        x_faces(w, fx, 7 * side, 7 * side + 2)

    def row_total(x):
        return [-0.5 * (acc[f, x] + (fx[f, x + 1] - fx[f, x])) for f in range(NF)]

    def middle(x, carry):
        total = row_total(x)
        u = conserved_row(x)
        w = primitive_of([u[f] + time_step * total[f] for f in range(NF)])
        for f in range(NF):
            tend[f, x] = total[f]
            w2[f, x + 2] = w[f]
        z_row(w2, x)
        return carry

    out_rows = out_ref.reshape(NF * NZ * NX, NY)

    def last(x, carry):
        total = row_total(x)
        for f in range(NF):
            out_rows[pl.ds(f * NZ * NX + x, NZ, NX), :] = 0.5 * (tend[f, x] + total[f])
        return carry

    start_y(0)
    scatter(0)
    lax.fori_loop(0, NX, z_first, 0)
    y_part()
    x_faces(w1, fx, 2, 7)
    scatter(1)
    finish_y(0)
    lax.fori_loop(2, 6, middle, 0)
    start_x(0, w1, 0)
    start_x(0, w1, 1)
    load_shift.wait()
    serve()

    def first_side(k, carry):
        side = side_at(k)
        receive_side(0, w1, side)
        side_faces(w1, side)
        lax.fori_loop(6 * side, 6 * side + 2, middle, 0)
        start_x(1, w2, side)

        @pl.when(k == 0)
        def _():
            soon = jnp.where(rad == 0, 4, 2)
            x_faces(w2, fx, soon, soon + 3)

        return carry

    lax.fori_loop(0, 2, first_side, 0)
    turn_y(1, w2)
    start_y(1)
    y_part()
    late = jnp.where(rad == 0, 2, 5)
    x_faces(w2, fx, late, late + 2)

    def second_side(k, carry):
        side = side_at(k)
        sheared = edge & (k == 1)

        @pl.when(sheared)
        def _():
            sheared_near()
            sheared_rows(w2)

        @pl.when(jnp.logical_not(sheared))
        def _():
            receive_side(1, w2, side)

        side_faces(w2, side)
        return carry

    lax.fori_loop(0, 2, second_side, 0)
    finish_y(1)
    lax.fori_loop(0, NX, last, 0)

    for sec, w in ((0, w1), (1, w2)):
        y_copy(sec, True).wait_send()
        y_copy(sec, False).wait_send()

        @pl.when(rad < RAD - 1)
        def _():
            x_copy(sec, w, True).wait_send()

        @pl.when(rad > 0)
        def _():
            x_copy(sec, w, False).wait_send()

    @pl.when(edge)
    def _():
        for t in range(2):
            most = stage.at[t, pl.ds(0, AZ - 1)]
            pltpu.make_async_copy(most, most, a_send.at[t]).wait()

            @pl.when(jnp.logical_not(relay))
            def _():
                pltpu.make_async_copy(stage.at[t, 0], stage.at[t, 0], a_send.at[t]).wait()

    @pl.when(relay)
    def _():
        pltpu.make_async_copy(near_out, near_out, b_send).wait()
        for t, begin, rows in ((0, 0, 9), (1, 16, 8)):
            sent = far_out.at[:, pl.ds(begin, rows)]
            pltpu.make_async_copy(sent, sent, far_send.at[t]).wait()
        most = plane_out.at[pl.ds(0, AZ - 1)]
        pltpu.make_async_copy(most, most, plane_send).wait()

        @pl.when(jnp.logical_not(edge))
        def _():
            pltpu.make_async_copy(plane_out.at[0], plane_out.at[0], plane_send).wait()


def shards(conserved, shear_shift):
    f32 = jnp.float32
    return pl.pallas_call(
        kernel,
        out_shape=jax.ShapeDtypeStruct((NF, NZ, NX, NY), f32),
        in_specs=[pl.BlockSpec(memory_space=pltpu.HBM), pl.BlockSpec(memory_space=pltpu.HBM)],
        out_specs=pl.BlockSpec(memory_space=pltpu.VMEM),
        scratch_shapes=[
            pltpu.VMEM((NF, NZ, NX, NY), f32),
            pltpu.VMEM((NF, NX + 4, NZ, NY), f32),
            pltpu.VMEM((NF, NX + 4, NZ, NY), f32),
            pltpu.VMEM((NF, NX, NZ, NY), f32),
            pltpu.VMEM((NF, NX + 1, NZ, NY), f32),
            pltpu.VMEM((NF, NX, NZ, NY), f32),
            pltpu.VMEM((NF, NY + 24, NX * NZ), f32),
            pltpu.VMEM((NF, NY + 8, NX * NZ), f32),
            pltpu.VMEM((2, 2, 2 * NF, NX * NZ), f32),
            pltpu.VMEM((2, 2, 2 * NF, NX * NZ), f32),
            pltpu.VMEM((2, 2, NF, 2, NZ, NY), f32),
            pltpu.VMEM((2, AZ, 8, NY), f32),
            pltpu.VMEM((2, AZ, 8, NY), f32),
            pltpu.VMEM((2, AZ, 8, NY), f32),
            pltpu.VMEM((AZ, 8, NY), f32),
            pltpu.VMEM((AZ, 24, NY), f32),
            pltpu.VMEM((AZ, 8, NY), f32),
            pltpu.VMEM((AZ, 24, NY), f32),
            pltpu.VMEM((NF, 2, NZ, NY), f32),
            pltpu.VMEM((NF, 6, NZ, NY), f32),
            pltpu.VMEM((NF, 3, NZ, NY), f32),
            pltpu.VMEM((NF, 2, NZ, NY), f32),
            pltpu.SMEM((2,), jnp.int32),
            pltpu.SemaphoreType.DMA,
            pltpu.SemaphoreType.DMA,
            pltpu.SemaphoreType.DMA((2, 2)),
            pltpu.SemaphoreType.DMA((2, 2)),
            pltpu.SemaphoreType.DMA((2, 2)),
            pltpu.SemaphoreType.DMA((2, 2)),
            pltpu.SemaphoreType.DMA((2,)),
            pltpu.SemaphoreType.DMA((2,)),
            pltpu.SemaphoreType.DMA,
            pltpu.SemaphoreType.DMA((2,)),
            pltpu.SemaphoreType.DMA((2,)),
            pltpu.SemaphoreType.DMA,
            pltpu.SemaphoreType.DMA,
        ],
        name="mhd_step",
        compiler_params=pltpu.CompilerParams(
            collective_id=0, has_side_effects=True, vmem_limit_bytes=53 * 1024 * 1024),
    )(pltpu.with_memory_space_constraint(shear_shift, pltpu.HBM),
      pltpu.with_memory_space_constraint(conserved, pltpu.HBM))


def solution(mesh):
    return jax.shard_map(
        shards,
        mesh=mesh,
        in_specs=(P(None, None, "rad", "az"), P()),
        out_specs=P(None, None, "rad", "az"),
        check_vma=False,
    )
```
